256 devices in a mesh: ctx: 32 (over x, z), tp: 4 (over y_hi, core), grp: 2 (over y_lo).
Axes of the slice: x: 4, y: 4 (y_hi: 2, y_lo: 2; y = y_hi * 2 + y_lo), z: 8, core: 2. Of those that a mesh axis runs over, the one named last changes fastest.
Arguments:
- prefill_query: bfloat16 [4096, 24576], P('ctx', ('tp', 'grp')), may hold values from -80 to 80
- prompt_cache: bfloat16 [4096, 576], P('ctx'), may hold values from -6 to 6
- key_up: bfloat16 [512, 16384], P(None, ('tp', 'grp')), may hold values from -0.5 to 0.5
- value_up: bfloat16 [512, 16384], P(None, ('tp', 'grp')), may hold values from -0.25 to 0.25
- block_place: int32 [64], replicated, may hold values from 0 to 63, each once
- decode_query: bfloat16 [256, 24576], P('ctx', ('tp', 'grp')), may hold values from -80 to 80
- decode_cache: bfloat16 [256, 576], P('ctx'), may hold values from -6 to 6
- row_length: int32 [256], replicated, may hold values from 1 to 4096, as said below
- row_slot: int32 [256], replicated, may hold values from 0 to 255, each once
Outputs:
- prefill_out: bfloat16 [4096, 16384], P(('ctx', 'tp', 'grp'))
- decode_out: bfloat16 [256, 16384], P('ctx', ('tp', 'grp'))
The draws below stay inside these ranges and needn't reach their ends.
Inputs may be any that keep to these rules, and one draw needn't show every extreme that they name: `row_length`: some row reads the whole prompt. `block_place`: a permutation. `row_slot`: a permutation; slot s belongs to index s // 8 of ctx.
All inputs are finite; a program needn't handle non-finite values.
Results may differ from the reference program's by a relative error of at most 0.027.
Values may be sent and summed in bfloat16 or wider, within the bound.
A program may use at most 128 MiB of HBM per device.

```python
import jax
import jax.numpy as jnp
from jax import lax

HEADS = 128
DL = 512
DR = 64
DN = 128
DV = 128
TOKENS = 4096
SPAN = 64
SPANS = 64
ROWS = 256


def draw_prefill_query(key, part):
    key = jax.random.fold_in(key, 11)
    values = jax.random.normal(key, (TOKENS, HEADS * (DN + DR)), jnp.float32)
    return jnp.clip(values, -80.0, 80.0).astype(jnp.bfloat16)


def draw_decode_query(key, part):
    key = jax.random.fold_in(key, 13)
    values = jax.random.normal(key, (ROWS, HEADS * (DN + DR)), jnp.float32)
    return jnp.clip(values, -80.0, 80.0).astype(jnp.bfloat16)


def draw_row_length(key, part):
    key = jax.random.fold_in(key, 23)
    lengths = jax.random.randint(key, (ROWS,), 1, TOKENS + 1)
    chosen = jax.random.randint(jax.random.fold_in(key, 5), (), 0, ROWS)
    return jnp.where(jnp.arange(ROWS) == chosen, TOKENS, lengths).astype(jnp.int32)


def level_of(key, extent, cuts, least, largest):
    loudness = 1.0
    for position, shards_of in cuts:
        draws = jax.random.uniform(jax.random.fold_in(jax.random.fold_in(key, 6), position), (shards_of,), jnp.float32, least / len(cuts), largest / len(cuts))
        loudness = loudness * jnp.repeat(jnp.exp(draws), extent[position] // shards_of).reshape((-1,) + (1,) * (len(extent) - 1 - position))
    return loudness


def scatter_about(stream_key, extent, width, limit, split=(), held_as=jnp.bfloat16):
    array = width * jax.random.normal(stream_key, extent, jnp.float32)
    if split:
        array = array * level_of(stream_key, extent, split, -0.22, 0.18)
    return jnp.clip(array, -limit, limit).astype(held_as)


def setup_inputs(seed: int = 0) -> dict:
    streams_of = jax.random.split(jax.random.key(seed), 10)
    return {
        "prefill_query": draw_prefill_query(jax.random.fold_in(streams_of[9], 71), 0),
        "prompt_cache": scatter_about(streams_of[1], (TOKENS, DL + DR), 1.0, 6.0, ((0, 32),)),
        "key_up": scatter_about(streams_of[2], (DL, HEADS * DN), DN ** -0.5, 0.5, ((1, 8),)),
        "value_up": scatter_about(streams_of[3], (DL, HEADS * DV), DL ** -0.5, 0.25, ((1, 8),)),
        "block_place": jax.random.permutation(streams_of[4], SPANS).astype(jnp.int32),
        "decode_query": draw_decode_query(jax.random.fold_in(streams_of[9], 71), 0),
        "decode_cache": scatter_about(streams_of[6], (ROWS, DL + DR), 1.0, 6.0, ((0, 32),)),
        "row_length": draw_row_length(jax.random.fold_in(streams_of[9], 71), 0),
        "row_slot": jax.random.permutation(streams_of[8], ROWS).astype(jnp.int32),
    }


masked_score = -1.0e30


def reference(prefill_query, prompt_cache, key_up, value_up, block_place, decode_query, decode_cache, row_length, row_slot):
    head_dim = DN + DR
    scale = head_dim ** -0.5
    stored = jnp.arange(TOKENS, dtype=jnp.int32)
    positions = (jnp.take(block_place, stored // SPAN) * SPAN + stored % SPAN).astype(jnp.int32)
    latent = prompt_cache[:, :DL]
    rope_key = prompt_cache[:, DL:]
    query = prefill_query.reshape(TOKENS, HEADS, head_dim)
    key_heads = key_up.reshape(DL, HEADS, DN)
    value_heads = value_up.reshape(DL, HEADS, DV)
    allowed = positions[None, :] <= positions[:, None]

    def prefill_head(head):
        qhead = query[:, head]
        q_abs = jnp.dot(qhead[:, :DN], key_heads[:, head].T, preferred_element_type=jnp.float32).astype(jnp.bfloat16)
        score = (jnp.dot(q_abs, latent.T, preferred_element_type=jnp.float32) + jnp.dot(qhead[:, DN:], rope_key.T, preferred_element_type=jnp.float32)) * scale
        score = jnp.where(allowed, score, masked_score)
        top = jnp.max(score, axis=1)
        expo = jnp.where(allowed, jnp.exp(score - top[:, None]), jnp.float32(0.0))
        total = jnp.sum(expo, axis=1)
        lat_out = (jnp.dot(expo.astype(jnp.bfloat16), latent, preferred_element_type=jnp.float32) / total[:, None]).astype(jnp.bfloat16)
        return jnp.dot(lat_out, value_heads[:, head], preferred_element_type=jnp.float32)

    prefill_heads = lax.map(prefill_head, jnp.arange(HEADS, dtype=jnp.int32))
    prefill_out = jnp.transpose(prefill_heads, (1, 0, 2)).reshape(TOKENS, HEADS * DV).astype(jnp.bfloat16)

    inverse = jnp.zeros((ROWS,), jnp.int32).at[row_slot].set(jnp.arange(ROWS, dtype=jnp.int32))
    slot_query = jnp.take(decode_query, inverse, axis=0).reshape(ROWS, HEADS, head_dim)
    slot_cache = jnp.take(decode_cache, inverse, axis=0)
    slot_length = jnp.take(row_length, inverse)
    valid = positions[None, :] < slot_length[:, None]
    own_latent = slot_cache[:, :DL].astype(jnp.float32)
    own_rope = slot_cache[:, DL:].astype(jnp.float32)

    def decode_head(head):
        qhead = slot_query[:, head]
        q_abs = jnp.dot(qhead[:, :DN], key_heads[:, head].T, preferred_element_type=jnp.float32).astype(jnp.bfloat16)
        score = (jnp.dot(q_abs, latent.T, preferred_element_type=jnp.float32) + jnp.dot(qhead[:, DN:], rope_key.T, preferred_element_type=jnp.float32)) * scale
        own = (jnp.sum(q_abs.astype(jnp.float32) * own_latent, axis=1) + jnp.sum(qhead[:, DN:].astype(jnp.float32) * own_rope, axis=1)) * scale
        score = jnp.where(valid, score, masked_score)
        top = jnp.maximum(jnp.max(score, axis=1), own)
        expo = jnp.where(valid, jnp.exp(score - top[:, None]), jnp.float32(0.0))
        own_weight = jnp.exp(own - top)
        total = jnp.sum(expo, axis=1) + own_weight
        numer = jnp.dot(expo.astype(jnp.bfloat16), latent, preferred_element_type=jnp.float32) + own_weight[:, None] * own_latent
        dlat = numer / total[:, None]
        return jnp.dot(dlat, value_heads[:, head].astype(jnp.float32), precision=lax.Precision.HIGHEST)

    decode_heads = lax.map(decode_head, jnp.arange(HEADS, dtype=jnp.int32))
    decode_out = jnp.transpose(decode_heads, (1, 0, 2)).reshape(ROWS, HEADS * DV).astype(jnp.bfloat16)
    return prefill_out, decode_out
```

```python
import functools
import math

import jax
import jax.numpy as jnp
from jax import lax
from jax.experimental import pallas as pl
from jax.experimental.pallas import tpu as pltpu
from jax.sharding import PartitionSpec as P

DL = 512
DR = 64
DN = 128
DV = 128
HD = DN + DR
WIDE = DL + 2 * DR
SPAN = 64
FACTOR = HD**-0.5 * math.log2(math.e)
MASKED = -1e30
F32 = jnp.float32
BF16 = jnp.bfloat16


def dot(a, b, ca, cb):
    return lax.dot_general(a, b, (((ca,), (cb,)), ((), ())), preferred_element_type=F32)


def kernel(
    place, length, q_hbm, k_hbm, kup_hbm, vup_hbm, dq_ref, dc_ref, out_ref, dec_ref,
    q_ref, keys, kup, vup, queries, score, top, bias, sems,
):
    toks = q_ref.shape[0]
    rows = dq_ref.shape[0]
    heads = q_ref.shape[1] // HD
    count = keys.shape[0]
    pre = heads * toks
    dec = heads * rows
    chunk = bias.shape[1]
    me = lax.axis_index("ctx")

    loads = [
        pltpu.make_async_copy(src, dst, sems.at[i])
        for i, (src, dst) in enumerate(
            [(q_hbm, q_ref), (kup_hbm, kup), (k_hbm, keys), (vup_hbm, vup)]
        )
    ]
    for load in loads:
        load.start()
    loads[0].wait()
    loads[1].wait()

    @pl.loop(0, heads // 2)
    def _(pair):
        at = pl.ds(pl.multiple_of(pair * 2 * HD, 2 * HD), 2 * HD)
        both = q_ref[:, at].astype(F32)
        dboth = dq_ref[:, at].astype(F32)
        kept = []
        for sub in range(2):
            h = pair * 2 + sub
            left = jnp.concatenate([both, dboth, dboth], axis=0)[:, sub * HD : (sub + 1) * HD]
            up = kup[:, pl.ds(pl.multiple_of(h * DN, DN), DN)]
            absorbed = (dot(left[:, :DN].astype(BF16), up, 1, 1) * FACTOR).astype(BF16)
            rope = left[:, DN:] * FACTOR
            high = rope.astype(BF16).astype(F32)
            rope = jnp.concatenate([high, rope - high], axis=1).astype(BF16)
            here = pl.ds(pl.multiple_of(h * toks, toks), toks)
            queries[here, :DL] = absorbed[:toks]
            queries[here, DL:] = rope[:toks]
            kept.append((absorbed[toks:].astype(F32)[:rows], rope[toks:].astype(F32)[:rows]))
        here = pl.ds(pl.multiple_of(pre + pair * 2 * rows, 2 * rows), 2 * rows)
        queries[here, :DL] = jnp.concatenate([kept[0][0], kept[1][0]], axis=0).astype(BF16)
        queries[here, DL:] = jnp.concatenate([kept[0][1], kept[1][1]], axis=0).astype(BF16)

    top[...] = jnp.full_like(top, MASKED)
    loads[2].wait()

    lane = lax.broadcasted_iota(jnp.int32, (1, 128), 1)
    tok = lax.broadcasted_iota(jnp.int32, (toks, 1), 0)
    my_pos = jnp.where(tok < SPAN, place[2 * me], place[2 * me + 1]) * SPAN + tok % SPAN
    row = lax.broadcasted_iota(jnp.int32, (rows, 1), 0)
    limit = jnp.zeros((rows, 1), jnp.int32)
    for r in range(rows):
        limit = jnp.where(row == r, length[me * rows + r], limit)

    @pl.loop(0, count // chunk)
    def _(c):
        for j in range(chunk // 128):
            block = c * (chunk // SPAN) + 2 * j
            pos = jnp.where(lane < SPAN, place[block], place[block + 1]) * SPAN + lane % SPAN
            cols = slice(j * 128, (j + 1) * 128)
            bias[:toks, cols] = jnp.where(pos <= my_pos, 0.0, MASKED)
            part = jnp.where(pos < limit, 0.0, MASKED)
            bias[toks:, cols] = jnp.concatenate([part] * (dec // rows), axis=0)
        cols = pl.ds(pl.multiple_of(c * chunk, chunk), chunk)

        def tile(first, size, add):
            here = pl.ds(pl.multiple_of(first, 128), size)
            s = dot(queries[here, :], keys[cols, :], 1, 1) + add
            score[here, cols] = s
            best = top[here, :]
            for j in range(chunk // 128):
                best = jnp.maximum(best, s[:, j * 128 : (j + 1) * 128])
            top[here, :] = best

        @pl.loop(0, pre // 1024)
        def _(i):
            tile(i * 1024, 1024, jnp.concatenate([bias[:toks, :]] * (1024 // toks), axis=0))

        tile(pre, dec, bias[toks:, :])

    loads[3].wait()
    step = 512

    def weigh(here, size, best):
        den = jnp.zeros((size, 128), F32)
        num = None
        for c in range(count // step):
            e = jnp.exp2(score[here, c * step : (c + 1) * step] - best)
            for j in range(step // 128):
                den = den + e[:, j * 128 : (j + 1) * 128]
            part = dot(e.astype(BF16), keys[c * step : (c + 1) * step, :DL], 1, 0)
            num = part if num is None else num + part
        return num, jnp.sum(den, axis=1, keepdims=True)

    here = pl.ds(pre, dec)
    cache = dc_ref[...].astype(F32)
    own = jnp.concatenate([cache, cache[:, DL:]], axis=1)
    own = jnp.concatenate([own] * heads, axis=0)
    own_score = jnp.sum(queries[here, :].astype(F32) * own, axis=1, keepdims=True)
    best = jnp.maximum(jnp.max(top[here, :], axis=1, keepdims=True), own_score)
    num, den = weigh(here, dec, best)
    own_weight = jnp.exp2(own_score - best)
    lat = (num + own_weight * own[:, :DL]) / (den + own_weight)
    high = lat.astype(BF16).astype(F32)
    low = lat - high
    for h in range(heads):
        part = slice(h * rows, (h + 1) * rows)
        left = jnp.concatenate([high[part], low[part]], axis=0).astype(BF16)
        both = dot(left, vup[:, h * DV : (h + 1) * DV], 1, 0)
        dec_ref[:, h * DV : (h + 1) * DV] = (both[:rows] + both[rows:]).astype(BF16)

    @pl.loop(0, heads // 2)
    def _(pair):
        here = pl.ds(pl.multiple_of(pair * 2 * toks, 2 * toks), 2 * toks)
        best = jnp.max(top[here, :], axis=1, keepdims=True)
        num, den = weigh(here, 2 * toks, best)
        lat = (num / den).astype(BF16)
        for sub in range(2):
            cols = pl.ds(pl.multiple_of((pair * 2 + sub) * DV, DV), DV)
            out_ref[:, cols] = dot(lat[sub * toks : (sub + 1) * toks], vup[:, cols], 1, 0).astype(BF16)


def per_device(
    prefill_query, prompt_cache, key_up, value_up, block_place, decode_query, decode_cache,
    row_length, row_slot,
):
    toks, width = prefill_query.shape
    heads = width // HD
    rows = decode_query.shape[0]
    wide = jnp.concatenate([prompt_cache, prompt_cache[:, DL:]], axis=1)
    every = lax.all_gather(wide, "ctx", axis=0, tiled=True)
    count = every.shape[0]
    chunk = 512
    smem = pl.BlockSpec(memory_space=pltpu.SMEM)
    vmem = pl.BlockSpec(memory_space=pltpu.VMEM)
    hbm = pl.BlockSpec(memory_space=pl.ANY)
    total = heads * (toks + rows)
    out, dec = pl.pallas_call(
        kernel,
        out_shape=(
            jax.ShapeDtypeStruct((toks, heads * DV), BF16),
            jax.ShapeDtypeStruct((rows, heads * DV), BF16),
        ),
        in_specs=[smem, smem, hbm, hbm, hbm, hbm, vmem, vmem],
        out_specs=(vmem, vmem),
        scratch_shapes=[
            pltpu.VMEM((toks, width), BF16),
            pltpu.VMEM((count, WIDE), BF16),
            pltpu.VMEM(key_up.shape, BF16),
            pltpu.VMEM(value_up.shape, BF16),
            pltpu.VMEM((total, WIDE), BF16),
            pltpu.VMEM((total, count), F32),
            pltpu.VMEM((total, 128), F32),
            pltpu.VMEM((toks + heads * rows, chunk), F32),
            pltpu.SemaphoreType.DMA((4,)),
        ],
        compiler_params=pltpu.CompilerParams(vmem_limit_bytes=60 << 20),
    )(block_place, row_length, prefill_query, every, key_up, value_up, decode_query, decode_cache)
    all_dec = lax.all_gather(dec, "ctx", axis=0, tiled=True)
    mine = lax.axis_index("ctx") * rows + jnp.arange(rows, dtype=jnp.int32)
    pick = (row_slot[None, :] == mine[:, None]).astype(BF16)
    decode_out = jnp.dot(pick, all_dec, preferred_element_type=F32).astype(BF16)
    prefill_out = lax.all_to_all(out, ("tp", "grp"), split_axis=0, concat_axis=1, tiled=True)
    return prefill_out, decode_out


def solution(mesh):
    return jax.shard_map(
        per_device,
        mesh=mesh,
        in_specs=(
            P("ctx", ("tp", "grp")),
            P("ctx", None),
            P(None, ("tp", "grp")),
            P(None, ("tp", "grp")),
            P(),
            P("ctx", ("tp", "grp")),
            P("ctx", None),
            P(),
            P(),
        ),
        out_specs=(P(("ctx", "tp", "grp"), None), P("ctx", ("tp", "grp"))),
        check_vma=False,
    )
```

```python
import functools
import math

import jax
import jax.numpy as jnp
from jax import lax
from jax.experimental import pallas as pl
from jax.experimental.pallas import tpu as pltpu
from jax.sharding import PartitionSpec as P

DL = 512
DR = 64
DN = 128
DV = 128
HD = DN + DR
WIDE = DL + 2 * DR
SPAN = 64
FACTOR = HD**-0.5 * math.log2(math.e)
MASKED = -1e30
NX, NZ = 4, 8
HALF = NX * NZ * SPAN
MESH = pl.DeviceIdType.MESH
F32 = jnp.float32
BF16 = jnp.bfloat16


def dot(a, b, ca, cb):
    return lax.dot_general(a, b, (((ca,), (cb,)), ((), ())), preferred_element_type=F32)


def kernel(
    place, length, slots, cache_ref, dq_ref, dc_ref, q_hbm, kup_hbm, vup_hbm, out_ref, dec_ref,
    q_ref, keys, kup, vup, queries, score, top, bias, staged, xrows, zsend, zrecv,
    load_sem, send, recv, out_send, out_recv, dec_send, dec_recv,
):
    toks = q_ref.shape[0]
    rows = dq_ref.shape[0]
    heads = q_ref.shape[1] // HD
    count = keys.shape[0]
    pre = heads * toks
    dec = heads * rows
    ctx = lax.axis_index("ctx")
    tp = lax.axis_index("tp")
    grp = lax.axis_index("grp")
    x, z = ctx // NZ, lax.rem(ctx, NZ)
    core = lax.rem(tp, 2)
    member = tp * 2 + grp

    def at_x(d):
        return lax.rem(x + d + NX, NX)

    def at_z(d):
        return lax.rem(z + d + NZ, NZ)

    def x_peer(d):
        return (at_x(d) * NZ + z, tp, grp)

    def z_peer(d):
        return (x * NZ + at_z(d), tp, grp)

    def group_peer(d):
        other = lax.rem(member + d, 8)
        return (ctx, other // 2, lax.rem(other, 2))

    sibling = (ctx, tp + 1 - 2 * core, grp)

    loads = [
        pltpu.make_async_copy(src, dst, load_sem.at[i])
        for i, (src, dst) in enumerate([(q_hbm, q_ref), (kup_hbm, kup), (vup_hbm, vup)])
    ]
    for load in loads:
        load.start()

    barrier = pltpu.get_barrier_semaphore()
    peers = [x_peer(d) for d in range(1, NX)] + [z_peer(d) for d in range(1, NZ)]
    peers += [group_peer(d) for d in range(1, 8)]
    for peer in peers:
        pl.semaphore_signal(barrier, inc=1, device_id=peer, device_id_type=MESH)

    own_row = jnp.where(core == 0, ctx * SPAN, HALF + (z * NX + x) * SPAN)
    mine = cache_ref[pl.ds(pl.multiple_of(core * SPAN, SPAN), SPAN), :]
    here = pl.ds(pl.multiple_of(own_row, SPAN), SPAN)
    keys[here, : DL + DR] = mine
    keys[here, DL + DR :] = mine[:, DL:]
    pl.semaphore_wait(barrier, len(peers))

    def copy(first, size, sem, peer):
        part = keys.at[pl.ds(pl.multiple_of(first, SPAN), size), :]
        return pltpu.make_async_remote_copy(
            src_ref=part, dst_ref=part, send_sem=send.at[sem], recv_sem=recv.at[sem],
            device_id=peer, device_id_type=MESH,
        )

    def even(dx, dz):
        return (at_x(dx) * NZ + at_z(dz)) * SPAN

    def odd(dx, dz):
        return HALF + (at_z(dz) * NX + at_x(dx)) * SPAN

    def odd_group(dz):
        return HALF + at_z(dz) * (NX * SPAN)

    order = [0, -1, 1, -2, 2, -3, 3, 4]

    def up(t, come=0):
        return copy(even(0, -t - come), SPAN, t, z_peer(1))

    def down(t, come=0):
        return copy(even(0, t + come), SPAN, 4 + t, z_peer(-1))

    def right(k, come=0):
        return copy(even(-come, order[k]), SPAN, 8 + k, x_peer(1))

    def left(k, come=0):
        return copy(even(come, order[k]), SPAN, 16 + k, x_peer(-1))

    def further(k, come=0):
        if k % 2 == 0:
            return copy(even(-1 - come, order[k]), SPAN, 24 + k, x_peer(1))
        return copy(even(1 + come, order[k]), SPAN, 24 + k, x_peer(-1))

    def even_twin(dx):
        return copy(at_x(dx) * (NZ * SPAN), NZ * SPAN, 32 + dx % NX, sibling)

    def across(d, come=0):
        return copy(odd(-d * come, 0), SPAN, 35 + d, x_peer(d))

    def odd_up(t, come=0):
        size = NX * SPAN if t < 3 else NX * SPAN // 2
        return copy(odd_group(-t - come), size, 40 + t, z_peer(1))

    def odd_down(t, come=0):
        if t < 3:
            return copy(odd_group(t + come), NX * SPAN, 44 + t, z_peer(-1))
        return copy(odd_group(t + come) + NX * SPAN // 2, NX * SPAN // 2, 44 + t, z_peer(-1))

    def odd_twin(dz):
        return copy(odd_group(dz), NX * SPAN, 48 + dz % NZ, sibling)

    def on(which):
        return pl.when(core == which)

    @on(0)
    def _():
        up(0).start()
        down(0).start()
        right(0).start()
        left(0).start()

    @on(1)
    def _():
        for d in (1, 3, 2):
            across(d).start()

    loads[0].wait()
    loads[1].wait()

    def absorb(pair):
        at = pl.ds(pl.multiple_of(pair * 2 * HD, 2 * HD), 2 * HD)
        both = q_ref[:, at].astype(F32)
        dboth = dq_ref[:, at].astype(F32)
        kept = []
        for sub in range(2):
            h = pair * 2 + sub
            every = jnp.concatenate([both, dboth, dboth], axis=0)[:, sub * HD : (sub + 1) * HD]
            block = kup[:, pl.ds(pl.multiple_of(h * DN, DN), DN)]
            absorbed = (dot(every[:, :DN].astype(BF16), block, 1, 1) * FACTOR).astype(BF16)
            rope = every[:, DN:] * FACTOR
            high = rope.astype(BF16).astype(F32)
            rope = jnp.concatenate([high, rope - high], axis=1).astype(BF16)
            here = pl.ds(pl.multiple_of(h * toks, toks), toks)
            queries[here, :DL] = absorbed[:toks]
            queries[here, DL:] = rope[:toks]
            kept.append((absorbed[toks:].astype(F32)[:rows], rope[toks:].astype(F32)[:rows]))
        here = pl.ds(pl.multiple_of(pre + pair * 2 * rows, 2 * rows), 2 * rows)
        queries[here, :DL] = jnp.concatenate([kept[0][0], kept[1][0]], axis=0).astype(BF16)
        queries[here, DL:] = jnp.concatenate([kept[0][1], kept[1][1]], axis=0).astype(BF16)

    lane = lax.broadcasted_iota(jnp.int32, (1, 128), 1)
    tok = lax.broadcasted_iota(jnp.int32, (toks, 1), 0)
    my_pos = jnp.where(tok < SPAN, place[2 * ctx], place[2 * ctx + 1]) * SPAN + (tok & (SPAN - 1))
    row = lax.broadcasted_iota(jnp.int32, (rows, 1), 0)
    limit = jnp.zeros((rows, 1), jnp.int32)
    for r in range(rows):
        limit = jnp.where(row == r, length[ctx * rows + r], limit)

    def scores(first, size, blocks):
        for j in range(size // 128):
            a, b = place[blocks[2 * j]], place[blocks[2 * j + 1]]
            pos = jnp.where(lane < SPAN, a, b) * SPAN + (lane & (SPAN - 1))
            cols = slice(j * 128, (j + 1) * 128)
            bias[:toks, cols] = jnp.where(pos <= my_pos, 0.0, MASKED)
            part = jnp.where(pos < limit, 0.0, MASKED)
            bias[toks:, cols] = jnp.concatenate([part] * (dec // rows), axis=0)
        cols = pl.ds(pl.multiple_of(first, 256), size)
        half = pre // 2
        for begin, tall, extra in ((0, half, 0), (half, half, dec)):
            here = pl.ds(begin, tall + extra)
            add = [bias[:toks, :size]] * (tall // toks)
            if extra:
                add = add + [bias[toks:, :size]]
            s = dot(queries[here, :], keys[cols, :], 1, 1) + jnp.concatenate(add, axis=0)
            score[here, cols] = s
            best = top[here, :]
            for j in range(size // 128):
                best = jnp.maximum(best, s[:, j * 128 : (j + 1) * 128])
            top[here, :] = best

    def even_scores(dx):
        first = at_x(dx) * NZ
        scores(first * SPAN, NZ * SPAN, [2 * (first + j) for j in range(NZ)])

    def odd_scores(dz):
        blocks = [2 * (j * NZ + at_z(dz)) + 1 for j in range(NX)]
        scores(odd_group(dz), NX * SPAN, blocks)

    pl.loop(0, 2)(absorb)

    @on(0)
    def _():
        up(0, 1).wait_recv()
        up(1).start()
        down(0, 1).wait_recv()
        down(1).start()
        for k in (1, 2):
            right(k).start()
            left(k).start()

    @on(1)
    def _():
        for d in (1, 3, 2):
            across(d, 1).wait_recv()
        odd_up(0).start()
        odd_down(0).start()
        odd_twin(0).start()

    pl.loop(2, 5)(absorb)

    @on(0)
    def _():
        up(1, 1).wait_recv()
        up(2).start()
        down(1, 1).wait_recv()
        down(2).start()
        for k in (3, 4):
            right(k).start()
            left(k).start()

    pl.loop(5, heads // 2)(absorb)
    top[...] = jnp.full_like(top, MASKED)

    @on(0)
    def _():
        up(2, 1).wait_recv()
        up(3).start()
        down(2, 1).wait_recv()
        for k in (5, 6):
            right(k).start()
            left(k).start()
        odd_twin(0).wait_recv()

    odd_scores(0)

    @on(0)
    def _():
        up(3, 1).wait_recv()
        right(7).start()
        left(7).start()
        even_twin(0).start()
        for k in (0, 1, 2):
            (right if k % 2 == 0 else left)(k, 1).wait_recv()
            further(k).start()

    @on(1)
    def _():
        odd_up(0, 1).wait_recv()
        odd_up(1).start()
        odd_down(0, 1).wait_recv()
        odd_down(1).start()
        odd_twin(-1).start()
        odd_twin(1).start()
        even_twin(0).wait_recv()

    even_scores(0)

    @on(0)
    def _():
        for k in (3, 4, 5):
            (right if k % 2 == 0 else left)(k, 1).wait_recv()
            further(k).start()
        odd_twin(-1).wait_recv()
        odd_twin(1).wait_recv()

    @pl.loop(0, 2)
    def _(i):
        odd_scores(2 * i - 1)

    @on(0)
    def _():
        for k in (6, 7):
            (right if k % 2 == 0 else left)(k, 1).wait_recv()
            further(k).start()
        for k in range(NZ):
            (left if k % 2 == 0 else right)(k, 1).wait_recv()
        even_twin(1).start()
        even_twin(-1).start()

    @on(1)
    def _():
        odd_up(1, 1).wait_recv()
        odd_up(2).start()
        odd_down(1, 1).wait_recv()
        odd_down(2).start()
        odd_twin(-2).start()
        odd_twin(2).start()
        even_twin(1).wait_recv()
        even_twin(-1).wait_recv()

    @pl.loop(0, 2)
    def _(i):
        even_scores(2 * i - 1)

    @on(0)
    def _():
        for k in range(NZ):
            further(k, 1).wait_recv()
        even_twin(2).start()
        odd_twin(-2).wait_recv()
        odd_twin(2).wait_recv()

    @on(1)
    def _():
        odd_up(2, 1).wait_recv()
        odd_up(3).start()
        odd_down(2, 1).wait_recv()
        odd_down(3).start()
        odd_twin(-3).start()
        odd_twin(3).start()

    @pl.loop(0, 2)
    def _(i):
        odd_scores(4 * i - 2)

    @on(0)
    def _():
        odd_twin(-3).wait_recv()
        odd_twin(3).wait_recv()

    @on(1)
    def _():
        odd_up(3, 1).wait_recv()
        odd_down(3, 1).wait_recv()
        odd_twin(4).start()
        even_twin(2).wait_recv()

    @pl.loop(0, 2)
    def _(i):
        odd_scores(6 * i - 3)

    even_scores(2)

    @on(0)
    def _():
        odd_twin(4).wait_recv()

    odd_scores(4)
    loads[2].wait()
    step = 512

    def weigh(here, size, best):
        den = jnp.zeros((size, 128), F32)
        num = None
        for c in range(count // step):
            e = jnp.exp2(score[here, c * step : (c + 1) * step] - best)
            for j in range(step // 128):
                den = den + e[:, j * 128 : (j + 1) * 128]
            part = dot(e.astype(BF16), keys[c * step : (c + 1) * step, :DL], 1, 0)
            num = part if num is None else num + part
        return num, jnp.sum(den, axis=1, keepdims=True)

    here = pl.ds(pre, dec)
    cache = dc_ref[...].astype(F32)
    own = jnp.concatenate([cache, cache[:, DL:]], axis=1)
    own = jnp.concatenate([own] * heads, axis=0)
    own_score = jnp.sum(queries[here, :].astype(F32) * own, axis=1, keepdims=True)
    best = jnp.maximum(jnp.max(top[here, :], axis=1, keepdims=True), own_score)
    num, den = weigh(here, dec, best)
    own_weight = jnp.exp2(own_score - best)
    lat = (num + own_weight * own[:, :DL]) / (den + own_weight)
    high = lat.astype(BF16).astype(F32)
    low = lat - high
    outs = []
    for h in range(heads):
        part = slice(h * rows, (h + 1) * rows)
        pieces = jnp.concatenate([high[part], low[part]], axis=0).astype(BF16)
        both = dot(pieces, vup[:, h * DV : (h + 1) * DV], 1, 0)
        outs.append(both[:rows] + both[rows:])
    wide = heads // 2 * DV
    halves = [jnp.concatenate(outs[: heads // 2], axis=1), jnp.concatenate(outs[heads // 2 :], axis=1)]
    xrows[x] = jnp.concatenate(halves, axis=0).astype(BF16)

    def x_rows(d, come=0):
        slot = xrows.at[at_x(-d * come)]
        return pltpu.make_async_remote_copy(
            src_ref=slot, dst_ref=slot, send_sem=dec_send.at[d - 1], recv_sem=dec_recv.at[d - 1],
            device_id=x_peer(d), device_id_type=MESH,
        )

    def z_rows(d):
        return pltpu.make_async_remote_copy(
            src_ref=zsend.at[at_z(d)], dst_ref=zrecv.at[d - 1], send_sem=dec_send.at[2 + d],
            recv_sem=dec_recv.at[2 + d], device_id=z_peer(d), device_id_type=MESH,
        )

    for d in range(1, NX):
        x_rows(d).start()

    groups = out_send.shape[0]
    span = heads * DV // groups
    share = out_ref.shape[0]

    def deliver(g, d):
        other = lax.rem(member + d, 8)
        return pltpu.make_async_remote_copy(
            src_ref=staged.at[
                pl.ds(pl.multiple_of(other * share, share), share),
                pl.ds(pl.multiple_of(g * span, span), span),
            ],
            dst_ref=out_ref.at[:, pl.ds(pl.multiple_of(member * heads * DV + g * span, span), span)],
            send_sem=out_send.at[g, d - 1], recv_sem=out_recv.at[g, d - 1],
            device_id=group_peer(d), device_id_type=MESH,
        )

    def arrival(g, d):
        other = lax.rem(member + 8 - d, 8)
        part = out_ref.at[:, pl.ds(pl.multiple_of(other * heads * DV + g * span, span), span)]
        return pltpu.make_async_remote_copy(
            src_ref=part, dst_ref=part, send_sem=out_send.at[g, d - 1], recv_sem=out_recv.at[g, d - 1],
            device_id=group_peer(d), device_id_type=MESH,
        )

    per_group = heads // 2 // groups

    def group(g):
        @pl.loop(0, per_group)
        def _(i):
            pair = g * per_group + i
            here = pl.ds(pl.multiple_of(pair * 2 * toks, 2 * toks), 2 * toks)
            best = jnp.max(top[here, :], axis=1, keepdims=True)
            num, den = weigh(here, 2 * toks, best)
            lat = (num / den).astype(BF16)
            for sub in range(2):
                cols = pl.ds(pl.multiple_of((pair * 2 + sub) * DV, DV), DV)
                part = dot(lat[sub * toks : (sub + 1) * toks], vup[:, cols], 1, 0)
                staged[:, cols] = part.astype(BF16)

        for d in range(1, 8):
            deliver(g, d).start()
        cols = pl.ds(pl.multiple_of(g * span, span), span)
        ours = pl.ds(pl.multiple_of(member * heads * DV + g * span, span), span)
        out_ref[:, ours] = staged[pl.ds(pl.multiple_of(member * share, share), share), cols]

    pl.loop(0, 1)(group)

    for d in range(1, NX):
        x_rows(d, 1).wait_recv()
    tall = 2 * rows
    to = lax.broadcasted_iota(jnp.int32, (NZ * tall, NX * tall), 0)
    fro = lax.broadcasted_iota(jnp.int32, (NZ * tall, NX * tall), 1)
    target = (x * NZ + to // tall) * rows + (to & (rows - 1))
    slot = jnp.full((NZ * tall, NX * tall), -1, jnp.int32)
    for j in range(NX):
        for i in range(rows):
            hit = (fro // tall == j) & ((fro & (rows - 1)) == i)
            slot = jnp.where(hit, slots[(j * NZ + z) * rows + i], slot)
    pick = (slot == target) & ((to & rows) == (fro & rows))
    pick = jnp.where(pick, 1.0, 0.0).astype(BF16)
    moved = dot(pick, xrows[...].reshape(NX * tall, wide), 1, 0).astype(BF16)
    zsend[...] = moved.reshape(NZ, tall, wide)
    for d in range(1, NZ):
        z_rows(d).start()

    pl.loop(1, groups)(group)

    total = zsend[z].astype(F32)
    for d in range(1, NZ):
        z_rows(d).wait_recv()
        total = total + zrecv[d - 1].astype(F32)
    dec_ref[...] = jnp.concatenate([total[:rows], total[rows:]], axis=1).astype(BF16)

    @pl.loop(0, groups)
    def _(g):
        for d in range(1, 8):
            arrival(g, d).wait_recv()
            deliver(g, d).wait_send()

    for d in range(1, NX):
        x_rows(d).wait_send()
    for d in range(1, NZ):
        z_rows(d).wait_send()

    @on(0)
    def _():
        for t in range(4):
            up(t).wait_send()
        for t in range(3):
            down(t).wait_send()
        for k in range(NZ):
            right(k).wait_send()
            left(k).wait_send()
            further(k).wait_send()
        for d in range(NX):
            even_twin(d).wait_send()

    @on(1)
    def _():
        for d in range(1, NX):
            across(d).wait_send()
        for t in range(4):
            odd_up(t).wait_send()
            odd_down(t).wait_send()
        for d in range(NZ):
            odd_twin(d).wait_send()


def per_device(
    prefill_query, prompt_cache, key_up, value_up, block_place, decode_query, decode_cache,
    row_length, row_slot,
):
    toks, width = prefill_query.shape
    heads = width // HD
    rows = decode_query.shape[0]
    count = NX * NZ * toks
    smem = pl.BlockSpec(memory_space=pltpu.SMEM)
    vmem = pl.BlockSpec(memory_space=pltpu.VMEM)
    hbm = pl.BlockSpec(memory_space=pl.ANY)
    total = heads * (toks + rows)
    groups = 4
    wide = heads // 2 * DV
    return pl.pallas_call(
        kernel,
        out_shape=(
            jax.ShapeDtypeStruct((toks // 8, 8 * heads * DV), BF16),
            jax.ShapeDtypeStruct((rows, heads * DV), BF16),
        ),
        in_specs=[smem, smem, smem, vmem, vmem, vmem, hbm, hbm, hbm],
        out_specs=(vmem, vmem),
        scratch_shapes=[
            pltpu.VMEM((toks, width), BF16),
            pltpu.VMEM((count, WIDE), BF16),
            pltpu.VMEM(key_up.shape, BF16),
            pltpu.VMEM(value_up.shape, BF16),
            pltpu.VMEM((total, WIDE), BF16),
            pltpu.VMEM((total, count), F32),
            pltpu.VMEM((total, 128), F32),
            pltpu.VMEM((toks + heads * rows, NZ * SPAN), F32),
            pltpu.VMEM((toks, heads * DV), BF16),
            pltpu.VMEM((NX, 2 * rows, wide), BF16),
            pltpu.VMEM((NZ, 2 * rows, wide), BF16),
            pltpu.VMEM((NZ - 1, 2 * rows, wide), BF16),
            pltpu.SemaphoreType.DMA((3,)),
            pltpu.SemaphoreType.DMA((56,)),
            pltpu.SemaphoreType.DMA((56,)),
            pltpu.SemaphoreType.DMA((groups, 7)),
            pltpu.SemaphoreType.DMA((groups, 7)),
            pltpu.SemaphoreType.DMA((NX + NZ - 2,)),
            pltpu.SemaphoreType.DMA((NX + NZ - 2,)),
        ],
        compiler_params=pltpu.CompilerParams(
            vmem_limit_bytes=60 << 20, collective_id=0, has_side_effects=True
        ),
    )(
        block_place, row_length, row_slot, prompt_cache, decode_query, decode_cache,
        prefill_query, key_up, value_up,
    )


def solution(mesh):
    return jax.shard_map(
        per_device,
        mesh=mesh,
        in_specs=(
            P("ctx", ("tp", "grp")),
            P("ctx", None),
            P(None, ("tp", "grp")),
            P(None, ("tp", "grp")),
            P(),
            P("ctx", ("tp", "grp")),
            P("ctx", None),
            P(),
            P(),
        ),
        out_specs=(P(("ctx", "tp", "grp"), None), P("ctx", ("tp", "grp"))),
        check_vma=False,
    )
```

```python
import functools
import math

import jax
import jax.numpy as jnp
from jax import lax
from jax.experimental import pallas as pl
from jax.experimental.pallas import tpu as pltpu
from jax.sharding import PartitionSpec as P

DL = 512
DR = 64
DN = 128
DV = 128
HD = DN + DR
WIDE = DL + 2 * DR
SPAN = 64
FACTOR = HD**-0.5 * math.log2(math.e)
MASKED = -1e30
NX, NZ = 4, 8
LINE = NX * SPAN
MESH = pl.DeviceIdType.MESH
F32 = jnp.float32
BF16 = jnp.bfloat16


def dot(a, b, ca, cb):
    return lax.dot_general(a, b, (((ca,), (cb,)), ((), ())), preferred_element_type=F32)


def kernel(
    place, length, slots, cache_ref, dq_ref, dc_ref, q_hbm, kup_hbm, vup_hbm, out_ref, dec_ref,
    q_ref, keys, kup, vup, queries, score, top, bias, staged, xrows, zsend, zrecv,
    load_sem, send, recv, out_send, out_recv, dec_send, dec_recv,
):
    toks = q_ref.shape[0]
    rows = dq_ref.shape[0]
    heads = q_ref.shape[1] // HD
    count = keys.shape[0]
    pre = heads * toks
    dec = heads * rows
    ctx = lax.axis_index("ctx")
    tp = lax.axis_index("tp")
    grp = lax.axis_index("grp")
    x, z = ctx // NZ, lax.rem(ctx, NZ)
    core = lax.rem(tp, 2)
    member = tp * 2 + grp

    def at_x(d):
        return lax.rem(x + d + NX, NX)

    def at_z(d):
        return lax.rem(z + d + NZ, NZ)

    def x_peer(d):
        return (at_x(d) * NZ + z, tp, grp)

    def z_peer(d):
        return (x * NZ + at_z(d), tp, grp)

    def group_peer(d):
        other = lax.rem(member + d, 8)
        return (ctx, other // 2, lax.rem(other, 2))

    sibling = (ctx, tp + 1 - 2 * core, grp)

    loads = [
        pltpu.make_async_copy(src, dst, load_sem.at[i])
        for i, (src, dst) in enumerate([(q_hbm, q_ref), (kup_hbm, kup), (vup_hbm, vup)])
    ]
    for load in loads:
        load.start()

    barrier = pltpu.get_barrier_semaphore()
    peers = [x_peer(d) for d in range(1, NX)] + [z_peer(d) for d in range(1, NZ)]
    peers += [group_peer(d) for d in range(1, 8)]
    for peer in peers:
        pl.semaphore_signal(barrier, inc=1, device_id=peer, device_id_type=MESH)

    def place_of(half, xx, zz):
        return (zz * 2 + half) * LINE + xx * SPAN

    turned = cache_ref[...].astype(F32).T
    mine = jnp.where(core == 0, turned[:SPAN], turned[SPAN:]).astype(BF16)
    here = pl.ds(pl.multiple_of(place_of(core, x, z), SPAN), SPAN)
    keys[here, : DL + DR] = mine
    keys[here, DL + DR :] = mine[:, DL:]
    pl.semaphore_wait(barrier, len(peers))

    def copy(first, size, sem, peer):
        part = keys.at[pl.ds(pl.multiple_of(first, SPAN // 2), size), :]
        return pltpu.make_async_remote_copy(
            src_ref=part, dst_ref=part, send_sem=send.at[sem], recv_sem=recv.at[sem],
            device_id=peer, device_id_type=MESH,
        )

    def along_z(half, xx, way, t, sem, come):
        far = at_z(-way * (t + come))
        first = place_of(half, xx, far)
        if t < NZ // 2 - 1:
            return copy(first, SPAN, sem, z_peer(way))
        return copy(first + (0 if way == 1 else SPAN // 2), SPAN // 2, sem, z_peer(way))

    def even_z(way, t, come=0):
        return along_z(0, x, way, t, t + (0 if way == 1 else 4), come)

    def odd_z(way, t, q, come=0):
        xx = at_x(jnp.where(q < 2, q, 5 - q))
        return along_z(1, xx, way, t, 48 + (0 if way == 1 else 16) + t * 4 + q, come)

    def odd_x(d, come=0):
        return copy(place_of(1, at_x(-d * come), z), SPAN, 7 + d, x_peer(d))

    def even_x(dz, d, come=0):
        return copy(place_of(0, at_x(-d * come), at_z(dz)), SPAN, 23 + (dz % NZ) * 3 + d, x_peer(d))

    def twin(half, dz):
        zz = at_z(dz)
        return copy(place_of(half, 0, zz), LINE, 16 + lax.rem(dz + NZ, NZ), sibling)

    def on(which):
        return pl.when(core == which)

    ways = (1, -1)

    @on(0)
    def _():
        for way in ways:
            even_z(way, 0).start()
        for d in (1, 3, 2):
            even_x(0, d).start()

    @on(1)
    def _():
        for d in (3, 1, 2):
            odd_x(d).start()
        for way in ways:
            odd_z(way, 0, 0).start()

    loads[0].wait()
    loads[1].wait()

    def absorb(pair):
        at = pl.ds(pl.multiple_of(pair * 2 * HD, 2 * HD), 2 * HD)
        both = q_ref[:, at].astype(F32)
        dboth = dq_ref[:, at].astype(F32)
        kept = []
        for sub in range(2):
            h = pair * 2 + sub
            every = jnp.concatenate([both, dboth, dboth], axis=0)[:, sub * HD : (sub + 1) * HD]
            block = kup[:, pl.ds(pl.multiple_of(h * DN, DN), DN)]
            absorbed = (dot(every[:, :DN].astype(BF16), block, 1, 1) * FACTOR).astype(BF16)
            rope = every[:, DN:] * FACTOR
            high = rope.astype(BF16).astype(F32)
            rope = jnp.concatenate([high, rope - high], axis=1).astype(BF16)
            here = pl.ds(pl.multiple_of(h * toks, toks), toks)
            queries[here, :DL] = absorbed[:toks]
            queries[here, DL:] = rope[:toks]
            kept.append((absorbed[toks:].astype(F32)[:rows], rope[toks:].astype(F32)[:rows]))
        here = pl.ds(pl.multiple_of(pre + pair * 2 * rows, 2 * rows), 2 * rows)
        queries[here, :DL] = jnp.concatenate([kept[0][0], kept[1][0]], axis=0).astype(BF16)
        queries[here, DL:] = jnp.concatenate([kept[0][1], kept[1][1]], axis=0).astype(BF16)

    lane = lax.broadcasted_iota(jnp.int32, (1, 128), 1)
    tok = lax.broadcasted_iota(jnp.int32, (toks, 1), 0)
    my_pos = jnp.where(tok < SPAN, place[2 * ctx], place[2 * ctx + 1]) * SPAN + (tok & (SPAN - 1))
    row = lax.broadcasted_iota(jnp.int32, (rows, 1), 0)
    limit = jnp.zeros((rows, 1), jnp.int32)
    for r in range(rows):
        limit = jnp.where(row == r, length[ctx * rows + r], limit)

    def scores(first, size, blocks):
        for j in range(size // 128):
            a, b = place[blocks[2 * j]], place[blocks[2 * j + 1]]
            pos = jnp.where(lane < SPAN, a, b) * SPAN + (lane & (SPAN - 1))
            cols = slice(j * 128, (j + 1) * 128)
            bias[:toks, cols] = jnp.where(pos <= my_pos, 0.0, MASKED)
            part = jnp.where(pos < limit, 0.0, MASKED)
            bias[toks:, cols] = jnp.concatenate([part] * (dec // rows), axis=0)
        cols = pl.ds(pl.multiple_of(first, 256), size)
        half = pre // 2
        for begin, tall, extra in ((0, half, 0), (half, half, dec)):
            here = pl.ds(begin, tall + extra)
            add = [bias[:toks, :size]] * (tall // toks)
            if extra:
                add = add + [bias[toks:, :size]]
            s = dot(queries[here, :], keys[cols, :], 1, 1) + jnp.concatenate(add, axis=0)
            score[here, cols] = s
            best = top[here, :]
            for j in range(size // 128):
                best = jnp.maximum(best, s[:, j * 128 : (j + 1) * 128])
            top[here, :] = best

    def unit(dz, half):
        zz = at_z(dz)
        scores(place_of(half, 0, zz), LINE, [2 * (j * NZ + zz) + half for j in range(NX)])

    pl.loop(0, 5)(absorb)

    @on(0)
    def _():
        for way in ways:
            even_z(way, 0, 1).wait_recv()
            even_z(way, 1).start()
        for dz in (-1, 1):
            for d in (1, 3, 2):
                even_x(dz, d).start()
        for d in (1, 3, 2):
            even_x(0, d, 1).wait_recv()

    @on(1)
    def _():
        for q, d in ((1, 3), (2, 1), (3, 2)):
            odd_x(d, 1).wait_recv()
            for way in ways:
                odd_z(way, 0, q).start()

    twin(core, 0).start()
    pl.loop(5, heads // 2)(absorb)
    top[...] = jnp.full_like(top, MASKED)

    def pass_on(t, q):
        @on(1)
        def _():
            for way in ways:
                odd_z(way, t, q, 1).wait_recv()
                if t < NZ // 2 - 1:
                    odd_z(way, t + 1, q).start()

    def gather_line(t):
        places = (t + 1, -t - 1) if t < NZ // 2 - 1 else (t + 1,)

        @on(0)
        def _():
            for dz in places:
                for d in (1, 3, 2):
                    even_x(dz, d, 1).wait_recv()

        for dz in places:
            twin(core, dz).start()

    @pl.loop(0, 2)
    def _(i):
        pass_on(0, 2 * i)

        @pl.when(i == 1)
        def _():
            twin(1 - core, 0).wait_recv()

        unit(0, jnp.where(i == 0, core, 1 - core))
        pass_on(0, 2 * i + 1)

    gather_line(0)

    for t in range(1, NZ // 2):

        @on(0)
        def _(t=t):
            for way in ways:
                even_z(way, t, 1).wait_recv()
                if t < NZ // 2 - 1:
                    even_z(way, t + 1).start()
            for dz in (-t - 1, t + 1) if t < NZ // 2 - 1 else (t + 1,):
                for d in (1, 3, 2):
                    even_x(dz, d).start()

        @pl.loop(0, 4)
        def _(q, t=t):
            pass_on(t, q)

            @pl.when(q == 2)
            def _():
                twin(1 - core, t).wait_recv()
                twin(1 - core, -t).wait_recv()

            unit(jnp.where(lax.rem(q, 2) == 0, t, -t), jnp.where(q < 2, core, 1 - core))

        gather_line(t)

    @pl.loop(0, 2)
    def _(i):
        @pl.when(i == 1)
        def _():
            twin(1 - core, NZ // 2).wait_recv()

        unit(NZ // 2, jnp.where(i == 0, core, 1 - core))

    loads[2].wait()
    step = 512

    def weigh(here, size, best):
        den = jnp.zeros((size, 128), F32)
        num = None
        for c in range(count // step):
            e = jnp.exp2(score[here, c * step : (c + 1) * step] - best)
            for j in range(step // 128):
                den = den + e[:, j * 128 : (j + 1) * 128]
            part = dot(e.astype(BF16), keys[c * step : (c + 1) * step, :DL], 1, 0)
            num = part if num is None else num + part
        return num, jnp.sum(den, axis=1, keepdims=True)

    here = pl.ds(pre, dec)
    cache = dc_ref[...].astype(F32)
    own = jnp.concatenate([cache, cache[:, DL:]], axis=1)
    own = jnp.concatenate([own] * heads, axis=0)
    own_score = jnp.sum(queries[here, :].astype(F32) * own, axis=1, keepdims=True)
    best = jnp.maximum(jnp.max(top[here, :], axis=1, keepdims=True), own_score)
    num, den = weigh(here, dec, best)
    own_weight = jnp.exp2(own_score - best)
    lat = (num + own_weight * own[:, :DL]) / (den + own_weight)
    high = lat.astype(BF16).astype(F32)
    low = lat - high
    outs = []
    for h in range(heads):
        part = slice(h * rows, (h + 1) * rows)
        pieces = jnp.concatenate([high[part], low[part]], axis=0).astype(BF16)
        both = dot(pieces, vup[:, h * DV : (h + 1) * DV], 1, 0)
        outs.append(both[:rows] + both[rows:])
    wide = heads // 2 * DV
    halves = [jnp.concatenate(outs[: heads // 2], axis=1), jnp.concatenate(outs[heads // 2 :], axis=1)]
    xrows[x] = jnp.concatenate(halves, axis=0).astype(BF16)

    def x_rows(d, come=0):
        slot = xrows.at[at_x(-d * come)]
        return pltpu.make_async_remote_copy(
            src_ref=slot, dst_ref=slot, send_sem=dec_send.at[d - 1], recv_sem=dec_recv.at[d - 1],
            device_id=x_peer(d), device_id_type=MESH,
        )

    def z_rows(d):
        return pltpu.make_async_remote_copy(
            src_ref=zsend.at[at_z(d)], dst_ref=zrecv.at[d - 1], send_sem=dec_send.at[2 + d],
            recv_sem=dec_recv.at[2 + d], device_id=z_peer(d), device_id_type=MESH,
        )

    for d in range(1, NX):
        x_rows(d).start()

    groups = out_send.shape[0]
    span = heads * DV // groups
    share = out_ref.shape[0]

    def deliver(g, d):
        other = lax.rem(member + d, 8)
        return pltpu.make_async_remote_copy(
            src_ref=staged.at[
                pl.ds(pl.multiple_of(other * share, share), share),
                pl.ds(pl.multiple_of(g * span, span), span),
            ],
            dst_ref=out_ref.at[:, pl.ds(pl.multiple_of(member * heads * DV + g * span, span), span)],
            send_sem=out_send.at[g, d - 1], recv_sem=out_recv.at[g, d - 1],
            device_id=group_peer(d), device_id_type=MESH,
        )

    def arrival(g, d):
        other = lax.rem(member + 8 - d, 8)
        part = out_ref.at[:, pl.ds(pl.multiple_of(other * heads * DV + g * span, span), span)]
        return pltpu.make_async_remote_copy(
            src_ref=part, dst_ref=part, send_sem=out_send.at[g, d - 1], recv_sem=out_recv.at[g, d - 1],
            device_id=group_peer(d), device_id_type=MESH,
        )

    per_group = heads // 2 // groups

    def group(g):
        @pl.loop(0, per_group)
        def _(i):
            pair = g * per_group + i
            here = pl.ds(pl.multiple_of(pair * 2 * toks, 2 * toks), 2 * toks)
            best = jnp.max(top[here, :], axis=1, keepdims=True)
            num, den = weigh(here, 2 * toks, best)
            lat = (num / den).astype(BF16)
            for sub in range(2):
                cols = pl.ds(pl.multiple_of((pair * 2 + sub) * DV, DV), DV)
                part = dot(lat[sub * toks : (sub + 1) * toks], vup[:, cols], 1, 0)
                staged[:, cols] = part.astype(BF16)

        for d in range(1, 8):
            deliver(g, d).start()
        cols = pl.ds(pl.multiple_of(g * span, span), span)
        ours = pl.ds(pl.multiple_of(member * heads * DV + g * span, span), span)
        out_ref[:, ours] = staged[pl.ds(pl.multiple_of(member * share, share), share), cols]

    pl.loop(0, 1)(group)

    for d in range(1, NX):
        x_rows(d, 1).wait_recv()
    tall = 2 * rows
    to = lax.broadcasted_iota(jnp.int32, (NZ * tall, NX * tall), 0)
    fro = lax.broadcasted_iota(jnp.int32, (NZ * tall, NX * tall), 1)
    target = (x * NZ + to // tall) * rows + (to & (rows - 1))
    slot = jnp.full((NZ * tall, NX * tall), -1, jnp.int32)
    for j in range(NX):
        for i in range(rows):
            hit = (fro // tall == j) & ((fro & (rows - 1)) == i)
            slot = jnp.where(hit, slots[(j * NZ + z) * rows + i], slot)
    pick = (slot == target) & ((to & rows) == (fro & rows))
    pick = jnp.where(pick, 1.0, 0.0).astype(BF16)
    moved = dot(pick, xrows[...].reshape(NX * tall, wide), 1, 0).astype(BF16)
    zsend[...] = moved.reshape(NZ, tall, wide)
    for d in range(1, NZ):
        z_rows(d).start()

    pl.loop(1, groups)(group)

    total = zsend[z].astype(F32)
    for d in range(1, NZ):
        z_rows(d).wait_recv()
        total = total + zrecv[d - 1].astype(F32)
    dec_ref[...] = jnp.concatenate([total[:rows], total[rows:]], axis=1).astype(BF16)

    @pl.loop(0, groups)
    def _(g):
        for d in range(1, 8):
            arrival(g, d).wait_recv()
            deliver(g, d).wait_send()

    for d in range(1, NX):
        x_rows(d).wait_send()
    for d in range(1, NZ):
        z_rows(d).wait_send()

    @pl.loop(0, NZ)
    def _(dz):
        twin(core, dz).wait_send()

    @on(0)
    def _():
        for t in range(NZ // 2):
            for way in ways:
                even_z(way, t).wait_send()

        @pl.loop(0, NZ)
        def _(dz):
            for d in range(1, NX):
                even_x(dz, d).wait_send()

    @on(1)
    def _():
        for d in range(1, NX):
            odd_x(d).wait_send()
        for t in range(NZ // 2):

            @pl.loop(0, 4)
            def _(q, t=t):
                for way in ways:
                    odd_z(way, t, q).wait_send()


def per_device(
    prefill_query, prompt_cache, key_up, value_up, block_place, decode_query, decode_cache,
    row_length, row_slot,
):
    toks, width = prefill_query.shape
    heads = width // HD
    rows = decode_query.shape[0]
    count = NX * NZ * toks
    smem = pl.BlockSpec(memory_space=pltpu.SMEM)
    vmem = pl.BlockSpec(memory_space=pltpu.VMEM)
    hbm = pl.BlockSpec(memory_space=pl.ANY)
    total = heads * (toks + rows)
    groups = 8
    wide = heads // 2 * DV
    return pl.pallas_call(
        kernel,
        out_shape=(
            jax.ShapeDtypeStruct((toks // 8, 8 * heads * DV), BF16),
            jax.ShapeDtypeStruct((rows, heads * DV), BF16),
        ),
        in_specs=[smem, smem, smem, vmem, vmem, vmem, hbm, hbm, hbm],
        out_specs=(vmem, vmem),
        scratch_shapes=[
            pltpu.VMEM((toks, width), BF16),
            pltpu.VMEM((count, WIDE), BF16),
            pltpu.VMEM(key_up.shape, BF16),
            pltpu.VMEM(value_up.shape, BF16),
            pltpu.VMEM((total, WIDE), BF16),
            pltpu.VMEM((total, count), F32),
            pltpu.VMEM((total, 128), F32),
            pltpu.VMEM((toks + heads * rows, LINE), F32),
            pltpu.VMEM((toks, heads * DV), BF16),
            pltpu.VMEM((NX, 2 * rows, wide), BF16),
            pltpu.VMEM((NZ, 2 * rows, wide), BF16),
            pltpu.VMEM((NZ - 1, 2 * rows, wide), BF16),
            pltpu.SemaphoreType.DMA((3,)),
            pltpu.SemaphoreType.DMA((80,)),
            pltpu.SemaphoreType.DMA((80,)),
            pltpu.SemaphoreType.DMA((groups, 7)),
            pltpu.SemaphoreType.DMA((groups, 7)),
            pltpu.SemaphoreType.DMA((NX + NZ - 2,)),
            pltpu.SemaphoreType.DMA((NX + NZ - 2,)),
        ],
        compiler_params=pltpu.CompilerParams(
            vmem_limit_bytes=60 << 20, collective_id=0, has_side_effects=True
        ),
    )(
        block_place, row_length, row_slot, prompt_cache.T, decode_query, decode_cache,
        prefill_query, key_up, value_up,
    )


def solution(mesh):
    return jax.shard_map(
        per_device,
        mesh=mesh,
        in_specs=(
            P("ctx", ("tp", "grp")),
            P("ctx", None),
            P(None, ("tp", "grp")),
            P(None, ("tp", "grp")),
            P(),
            P("ctx", ("tp", "grp")),
            P("ctx", None),
            P(),
            P(),
        ),
        out_specs=(P(("ctx", "tp", "grp"), None), P("ctx", ("tp", "grp"))),
        check_vma=False,
    )
```

```python
import functools
import math

import jax
import jax.numpy as jnp
from jax import lax
from jax.experimental import pallas as pl
from jax.experimental.pallas import tpu as pltpu
from jax.sharding import PartitionSpec as P

DL = 512
DR = 64
DN = 128
DV = 128
HD = DN + DR
WIDE = DL + 2 * DR
SPAN = 64
FACTOR = HD**-0.5 * math.log2(math.e)
MASKED = -1e30
NX, NZ = 4, 8
LINE = NX * SPAN
MESH = pl.DeviceIdType.MESH
F32 = jnp.float32
BF16 = jnp.bfloat16


def dot(a, b, ca, cb):
    return lax.dot_general(a, b, (((ca,), (cb,)), ((), ())), preferred_element_type=F32)


def kernel(
    place, length, slots, cache_ref, dq_ref, dc_ref, q_hbm, kup_hbm, vup_hbm, out_ref, dec_ref,
    q_ref, keys, kup, vup, queries, score, top, acc, part_den, base, bias,
    staged, xrows, zsend, zrecv,
    load_sem, send, recv, out_send, out_recv, dec_send, dec_recv,
):
    toks = q_ref.shape[0]
    rows = dq_ref.shape[0]
    heads = q_ref.shape[1] // HD
    count = keys.shape[0]
    pre = heads * toks
    dec = heads * rows
    ctx = lax.axis_index("ctx")
    tp = lax.axis_index("tp")
    grp = lax.axis_index("grp")
    x, z = ctx // NZ, lax.rem(ctx, NZ)
    core = lax.rem(tp, 2)
    member = tp * 2 + grp

    def at_x(d):
        return lax.rem(x + d + NX, NX)

    def at_z(d):
        return lax.rem(z + d + NZ, NZ)

    def x_peer(d):
        return (at_x(d) * NZ + z, tp, grp)

    def z_peer(d):
        return (x * NZ + at_z(d), tp, grp)

    def group_peer(d):
        other = lax.rem(member + d, 8)
        return (ctx, other // 2, lax.rem(other, 2))

    sibling = (ctx, tp + 1 - 2 * core, grp)

    loads = [
        pltpu.make_async_copy(src, dst, load_sem.at[i])
        for i, (src, dst) in enumerate([(q_hbm, q_ref), (kup_hbm, kup), (vup_hbm, vup)])
    ]
    for load in loads:
        load.start()

    barrier = pltpu.get_barrier_semaphore()
    peers = [x_peer(d) for d in range(1, NX)] + [z_peer(d) for d in range(1, NZ)]
    peers += [group_peer(d) for d in range(1, 8)]
    for peer in peers:
        pl.semaphore_signal(barrier, inc=1, device_id=peer, device_id_type=MESH)

    def place_of(half, xx, zz):
        return (zz * 2 + half) * LINE + xx * SPAN

    turned = cache_ref[...].astype(F32).T
    mine = jnp.where(core == 0, turned[:SPAN], turned[SPAN:]).astype(BF16)
    here = pl.ds(pl.multiple_of(place_of(core, x, z), SPAN), SPAN)
    keys[here, : DL + DR] = mine
    keys[here, DL + DR :] = mine[:, DL:]
    pl.semaphore_wait(barrier, len(peers))

    def copy(first, size, sem, peer):
        part = keys.at[pl.ds(pl.multiple_of(first, SPAN // 2), size), :]
        return pltpu.make_async_remote_copy(
            src_ref=part, dst_ref=part, send_sem=send.at[0], recv_sem=recv.at[sem],
            device_id=peer, device_id_type=MESH,
        )

    def landed(sem, size):
        copy(0, size, sem, sibling).wait_recv()

    EVEN_Z, ODD_X, TWIN, EVEN_X, ODD_Z = 0, 4, 8, 13, 18
    ways = (1, -1)
    last = NZ // 2 - 1

    def along_z(half, xx, way, t, sem):
        first = place_of(half, xx, at_z(-way * t))
        if t < last:
            return copy(first, SPAN, sem, z_peer(way))
        return copy(first + (0 if way == 1 else SPAN // 2), SPAN // 2, sem, z_peer(way))

    def even_z(t):
        return [along_z(0, x, way, t, EVEN_Z + t) for way in ways]

    def odd_z(t, q):
        xx = at_x(jnp.where(q < 2, q, 5 - q))
        return [along_z(1, xx, way, t, ODD_Z + t * 4 + q) for way in ways]

    def both(t):
        return 2 * SPAN if t < last else SPAN

    def odd_x(d):
        return copy(place_of(1, x, z), SPAN, ODD_X + d, x_peer(d))

    def even_x(dz):
        first = place_of(0, x, at_z(dz))
        return [copy(first, SPAN, EVEN_X + abs(dz), x_peer(d)) for d in (1, 3, 2)]

    def twin(dz):
        return copy(place_of(core, 0, at_z(dz)), LINE, TWIN + abs(dz), sibling)

    def twins_landed(dz):
        landed(TWIN + dz, LINE if dz in (0, NZ // 2) else 2 * LINE)

    def start(copies):
        for one in copies:
            one.start()

    def on(which):
        return pl.when(core == which)

    @on(0)
    def _():
        start(even_z(0))
        start(even_x(0))

    @on(1)
    def _():
        for d in (3, 1, 2):
            odd_x(d).start()
        start(odd_z(0, 0))

    loads[0].wait()
    loads[1].wait()

    def absorb(pair):
        at = pl.ds(pl.multiple_of(pair * 2 * HD, 2 * HD), 2 * HD)
        both = q_ref[:, at].astype(F32)
        dboth = dq_ref[:, at].astype(F32)
        kept = []
        for sub in range(2):
            h = pair * 2 + sub
            every = jnp.concatenate([both, dboth, dboth], axis=0)[:, sub * HD : (sub + 1) * HD]
            block = kup[:, pl.ds(pl.multiple_of(h * DN, DN), DN)]
            absorbed = (dot(every[:, :DN].astype(BF16), block, 1, 1) * FACTOR).astype(BF16)
            rope = every[:, DN:] * FACTOR
            high = rope.astype(BF16).astype(F32)
            rope = jnp.concatenate([high, rope - high], axis=1).astype(BF16)
            here = pl.ds(pl.multiple_of(h * toks, toks), toks)
            queries[here, :DL] = absorbed[:toks]
            queries[here, DL:] = rope[:toks]
            kept.append((absorbed[toks:].astype(F32)[:rows], rope[toks:].astype(F32)[:rows]))
        here = pl.ds(pl.multiple_of(pre + pair * 2 * rows, 2 * rows), 2 * rows)
        queries[here, :DL] = jnp.concatenate([kept[0][0], kept[1][0]], axis=0).astype(BF16)
        queries[here, DL:] = jnp.concatenate([kept[0][1], kept[1][1]], axis=0).astype(BF16)

    lane = lax.broadcasted_iota(jnp.int32, (1, 128), 1)
    tok = lax.broadcasted_iota(jnp.int32, (toks, 1), 0)
    my_pos = jnp.where(tok < SPAN, place[2 * ctx], place[2 * ctx + 1]) * SPAN + (tok & (SPAN - 1))
    row = lax.broadcasted_iota(jnp.int32, (rows, 1), 0)
    limit = jnp.zeros((rows, 1), jnp.int32)
    for r in range(rows):
        limit = jnp.where(row == r, length[ctx * rows + r], limit)

    def scores(first, size, blocks, column):
        for j in range(size // 128):
            a, b = place[blocks[2 * j]], place[blocks[2 * j + 1]]
            pos = jnp.where(lane < SPAN, a, b) * SPAN + (lane & (SPAN - 1))
            cols = slice(j * 128, (j + 1) * 128)
            bias[:toks, cols] = jnp.where(pos <= my_pos, 0.0, MASKED)
            part = jnp.where(pos < limit, 0.0, MASKED)
            bias[toks:, cols] = jnp.concatenate([part] * (dec // rows), axis=0)
        from_keys = pl.ds(pl.multiple_of(first, 256), size)
        cols = pl.ds(pl.multiple_of(column, 256), size)
        half = pre // 2
        for begin, tall, extra in ((0, half, 0), (half, half, dec)):
            here = pl.ds(begin, tall + extra)
            add = [bias[:toks, :size]] * (tall // toks)
            if extra:
                add = add + [bias[toks:, :size]]
            s = dot(queries[here, :], keys[from_keys, :], 1, 1) + jnp.concatenate(add, axis=0)
            score[here, cols] = s
            best = top[here, :]
            for j in range(size // 128):
                best = jnp.maximum(best, s[:, j * 128 : (j + 1) * 128])
            top[here, :] = best

    def unit(dz, half, line):
        zz = at_z(dz)
        blocks = [2 * (j * NZ + zz) + half for j in range(NX)]
        scores(place_of(half, 0, zz), LINE, blocks, (line * 2 + half) * LINE)

    def weigh(here, best, lines):
        den = jnp.zeros((best.shape[0], 128), F32)
        num = None
        for i, dz in enumerate(lines):
            e = jnp.exp2(score[here, i * 2 * LINE : (i + 1) * 2 * LINE] - best)
            for j in range(2 * LINE // 128):
                den = den + e[:, j * 128 : (j + 1) * 128]
            values = keys[pl.ds(pl.multiple_of(place_of(0, 0, at_z(dz)), 2 * LINE), 2 * LINE), :DL]
            part = dot(e.astype(BF16), values, 1, 0)
            num = part if num is None else num + part
        return num, den

    near, rest = (0, 1, -1), (2, -2, 3, -3, 4)

    def early(here, size):
        best = jnp.max(top[here, :], axis=1, keepdims=True)
        acc[here, :], part_den[here, :] = weigh(here, best, near)
        base[here, :] = jnp.broadcast_to(best, (size, 128))

    def join(here, best):
        num, den = weigh(here, best, rest)
        factor = jnp.exp2(base[here, :] - best)
        den = jnp.sum(den + part_den[here, :] * factor, axis=1, keepdims=True)
        return num + acc[here, :] * jnp.concatenate([factor] * (DL // 128), axis=1), den

    pl.loop(0, 5)(absorb)

    @on(0)
    def _():
        landed(EVEN_Z, both(0))
        start(even_z(1))
        start(even_x(-1) + even_x(1))
        landed(EVEN_X, 3 * SPAN)

    @on(1)
    def _():
        for q, d in ((1, 3), (2, 1), (3, 2)):
            landed(ODD_X + d, SPAN)
            start(odd_z(0, q))

    twin(0).start()
    pl.loop(5, heads // 2)(absorb)
    top[...] = jnp.full_like(top, MASKED)

    def pass_on(t, q):
        @on(1)
        def _():
            landed(ODD_Z + t * 4 + q, both(t))
            if t < last:
                start(odd_z(t + 1, q))

    def gather_line(t):
        places = (t + 1, -t - 1) if t < last else (t + 1,)

        @on(0)
        def _():
            landed(EVEN_X + t + 1, 3 * SPAN * len(places))

        for dz in places:
            twin(dz).start()

    def step_even(t):
        @on(0)
        def _():
            landed(EVEN_Z + t, both(t))
            if t < last:
                start(even_z(t + 1) + even_x(-t - 1) + even_x(t + 1))
            else:
                start(even_x(t + 1))

    def pair_of_lines(t, q, line):
        @pl.when(q == 2)
        def _():
            twins_landed(t)

        flip = lax.rem(q, 2)
        unit(jnp.where(flip == 0, t, -t), jnp.where(q < 2, core, 1 - core), line + flip)

    @pl.loop(0, 2)
    def _(i):
        pass_on(0, 2 * i)

        @pl.when(i == 1)
        def _():
            twins_landed(0)

        unit(0, jnp.where(i == 0, core, 1 - core), 0)
        pass_on(0, 2 * i + 1)

    gather_line(0)
    step_even(1)

    @pl.loop(0, 4)
    def _(q):
        pass_on(1, q)
        pair_of_lines(1, q, 1)

    gather_line(1)
    step_even(2)

    @pl.loop(0, 4)
    def _(q):
        pass_on(2, q)
        early(pl.ds(pl.multiple_of(q * (pre // 4), 128), pre // 4), pre // 4)

    gather_line(2)
    step_even(3)
    early(pl.ds(pre, dec), dec)

    @pl.loop(0, 4)
    def _(q):
        pass_on(3, q)
        pair_of_lines(2, q, 0)

    gather_line(3)

    @pl.loop(0, 4)
    def _(q):
        pair_of_lines(3, q, 2)

    @pl.loop(0, 2)
    def _(i):
        @pl.when(i == 1)
        def _():
            twins_landed(NZ // 2)

        unit(NZ // 2, jnp.where(i == 0, core, 1 - core), 4)

    loads[2].wait()

    here = pl.ds(pre, dec)
    cache = dc_ref[...].astype(F32)
    own = jnp.concatenate([cache, cache[:, DL:]], axis=1)
    own = jnp.concatenate([own] * heads, axis=0)
    own_score = jnp.sum(queries[here, :].astype(F32) * own, axis=1, keepdims=True)
    best = jnp.maximum(jnp.max(top[here, :], axis=1, keepdims=True), own_score)
    num, den = join(here, best)
    own_weight = jnp.exp2(own_score - best)
    lat = (num + own_weight * own[:, :DL]) / (den + own_weight)
    high = lat.astype(BF16).astype(F32)
    low = lat - high
    outs = []
    for h in range(heads):
        part = slice(h * rows, (h + 1) * rows)
        pieces = jnp.concatenate([high[part], low[part]], axis=0).astype(BF16)
        doubled = dot(pieces, vup[:, h * DV : (h + 1) * DV], 1, 0)
        outs.append(doubled[:rows] + doubled[rows:])
    wide = heads // 2 * DV
    halves = [jnp.concatenate(outs[: heads // 2], axis=1), jnp.concatenate(outs[heads // 2 :], axis=1)]
    xrows[x] = jnp.concatenate(halves, axis=0).astype(BF16)

    def x_rows(d):
        return pltpu.make_async_remote_copy(
            src_ref=xrows.at[x], dst_ref=xrows.at[x], send_sem=dec_send.at[0],
            recv_sem=dec_recv.at[0], device_id=x_peer(d), device_id_type=MESH,
        )

    def z_rows(d):
        return pltpu.make_async_remote_copy(
            src_ref=zsend.at[at_z(d)], dst_ref=zrecv.at[d - 1], send_sem=dec_send.at[1],
            recv_sem=dec_recv.at[1], device_id=z_peer(d), device_id_type=MESH,
        )

    def whole(src, dst, send_sem, recv_sem):
        return pltpu.make_async_remote_copy(
            src_ref=src, dst_ref=dst, send_sem=send_sem, recv_sem=recv_sem,
            device_id=sibling, device_id_type=MESH,
        )

    all_x = whole(xrows.at[pl.ds(0, NX - 1)], xrows.at[pl.ds(0, NX - 1)], dec_send.at[0], dec_recv.at[0])
    all_z = whole(zsend.at[pl.ds(0, NZ - 1)], zrecv, dec_send.at[1], dec_recv.at[1])

    for d in range(1, NX):
        x_rows(d).start()

    share = out_ref.shape[0]
    width = heads * DV

    def deliver(first, size, d):
        other = lax.rem(member + d, 8)
        return pltpu.make_async_remote_copy(
            src_ref=staged.at[pl.ds(pl.multiple_of(other * share, share), share), pl.ds(first, size)],
            dst_ref=out_ref.at[:, pl.ds(pl.multiple_of(member * width + first, 128), size)],
            send_sem=out_send.at[0], recv_sem=out_recv.at[0],
            device_id=group_peer(d), device_id_type=MESH,
        )

    all_out = whole(
        staged.at[pl.ds(0, 7 * share), :], out_ref.at[:, pl.ds(0, 7 * width)],
        out_send.at[0], out_recv.at[0],
    )

    def sort_rows():
        all_x.wait_recv()
        tall = 2 * rows
        to = lax.broadcasted_iota(jnp.int32, (NZ * tall, NX * tall), 0)
        fro = lax.broadcasted_iota(jnp.int32, (NZ * tall, NX * tall), 1)
        target = (x * NZ + to // tall) * rows + (to & (rows - 1))
        slot = jnp.full((NZ * tall, NX * tall), -1, jnp.int32)
        for j in range(NX):
            for i in range(rows):
                hit = (fro // tall == j) & ((fro & (rows - 1)) == i)
                slot = jnp.where(hit, slots[(j * NZ + z) * rows + i], slot)
        pick = (slot == target) & ((to & rows) == (fro & rows))
        pick = jnp.where(pick, 1.0, 0.0).astype(BF16)
        moved = dot(pick, xrows[...].reshape(NX * tall, wide), 1, 0).astype(BF16)
        zsend[...] = moved.reshape(NZ, tall, wide)
        for d in range(1, NZ):
            z_rows(d).start()

    pairs = heads // 2
    cuts = (0, 3, 6, 7, 8)

    @pl.loop(0, pairs)
    def _(pair):
        here = pl.ds(pl.multiple_of(pair * 2 * toks, 2 * toks), 2 * toks)
        num, den = join(here, jnp.max(top[here, :], axis=1, keepdims=True))
        lat = (num / den).astype(BF16)
        for sub in range(2):
            cols = pl.ds(pl.multiple_of((pair * 2 + sub) * DV, DV), DV)
            part = dot(lat[sub * toks : (sub + 1) * toks], vup[:, cols], 1, 0)
            staged[:, cols] = part.astype(BF16)
        pl.when(pair == 2)(sort_rows)
        for begin, end in zip(cuts[:-1], cuts[1:]):

            @pl.when(pair == end - 1)
            def _(begin=begin, end=end):
                for d in range(1, 8):
                    deliver(begin * 2 * DV, (end - begin) * 2 * DV, d).start()

    ours = pl.ds(pl.multiple_of(member * width, width), width)
    out_ref[:, ours] = staged[pl.ds(pl.multiple_of(member * share, share), share), :]
    all_z.wait_recv()
    total = zsend[z].astype(F32)
    for d in range(1, NZ):
        total = total + zrecv[d - 1].astype(F32)
    dec_ref[...] = jnp.concatenate([total[:rows], total[rows:]], axis=1).astype(BF16)
    sent = 2 * NX * NZ * SPAN - SPAN
    whole(keys.at[pl.ds(0, sent), :], keys.at[pl.ds(0, sent), :], send.at[0], recv.at[0]).wait_send()
    all_x.wait_send()
    all_z.wait_send()
    all_out.wait_send()
    all_out.wait_recv()


def per_device(
    prefill_query, prompt_cache, key_up, value_up, block_place, decode_query, decode_cache,
    row_length, row_slot,
):
    toks, width = prefill_query.shape
    heads = width // HD
    rows = decode_query.shape[0]
    count = NX * NZ * toks
    smem = pl.BlockSpec(memory_space=pltpu.SMEM)
    vmem = pl.BlockSpec(memory_space=pltpu.VMEM)
    hbm = pl.BlockSpec(memory_space=pl.ANY)
    total = heads * (toks + rows)
    wide = heads // 2 * DV
    return pl.pallas_call(
        kernel,
        out_shape=(
            jax.ShapeDtypeStruct((toks // 8, 8 * heads * DV), BF16),
            jax.ShapeDtypeStruct((rows, heads * DV), BF16),
        ),
        in_specs=[smem, smem, smem, vmem, vmem, vmem, hbm, hbm, hbm],
        out_specs=(vmem, vmem),
        scratch_shapes=[
            pltpu.VMEM((toks, width), BF16),
            pltpu.VMEM((count, WIDE), BF16),
            pltpu.VMEM(key_up.shape, BF16),
            pltpu.VMEM(value_up.shape, BF16),
            pltpu.VMEM((total, WIDE), BF16),
            pltpu.VMEM((total, 5 * 2 * LINE), F32),
            pltpu.VMEM((total, 128), F32),
            pltpu.VMEM((total, DL), F32),
            pltpu.VMEM((total, 128), F32),
            pltpu.VMEM((total, 128), F32),
            pltpu.VMEM((toks + heads * rows, LINE), F32),
            pltpu.VMEM((toks, heads * DV), BF16),
            pltpu.VMEM((NX, 2 * rows, wide), BF16),
            pltpu.VMEM((NZ, 2 * rows, wide), BF16),
            pltpu.VMEM((NZ - 1, 2 * rows, wide), BF16),
            pltpu.SemaphoreType.DMA((3,)),
            pltpu.SemaphoreType.DMA((1,)),
            pltpu.SemaphoreType.DMA((34,)),
            pltpu.SemaphoreType.DMA((1,)),
            pltpu.SemaphoreType.DMA((1,)),
            pltpu.SemaphoreType.DMA((2,)),
            pltpu.SemaphoreType.DMA((2,)),
        ],
        compiler_params=pltpu.CompilerParams(
            vmem_limit_bytes=60 << 20, collective_id=0, has_side_effects=True
        ),
    )(
        block_place, row_length, row_slot, prompt_cache.T, decode_query, decode_cache,
        prefill_query, key_up, value_up,
    )


def solution(mesh):
    return jax.shard_map(
        per_device,
        mesh=mesh,
        in_specs=(
            P("ctx", ("tp", "grp")),
            P("ctx", None),
            P(None, ("tp", "grp")),
            P(None, ("tp", "grp")),
            P(),
            P("ctx", ("tp", "grp")),
            P("ctx", None),
            P(),
            P(),
        ),
        out_specs=(P(("ctx", "tp", "grp"), None), P("ctx", ("tp", "grp"))),
        check_vma=False,
    )
```

```python
import functools
import math

import jax
import jax.numpy as jnp
from jax import lax
from jax.experimental import pallas as pl
from jax.experimental.pallas import tpu as pltpu
from jax.sharding import PartitionSpec as P

DL = 512
DR = 64
DN = 128
DV = 128
HD = DN + DR
WIDE = DL + 2 * DR
SPAN = 64
FACTOR = HD**-0.5 * math.log2(math.e)
MASKED = -1e30
NX, NZ = 4, 8
LINE = NX * SPAN
MESH = pl.DeviceIdType.MESH
F32 = jnp.float32
BF16 = jnp.bfloat16


def dot(a, b, ca, cb):
    return lax.dot_general(a, b, (((ca,), (cb,)), ((), ())), preferred_element_type=F32)


def kernel(
    place, length, slots, cache_ref, dq_ref, dc_ref, q_hbm, kup_hbm, vup_hbm, out_ref, dec_ref,
    q_ref, keys, kup, vup, queries, score, top, acc, part_den, base, bias,
    staged, xrows, zsend, zrecv,
    load_sem, send, recv, out_send, out_recv, dec_send, dec_recv,
):
    toks = q_ref.shape[0]
    rows = dq_ref.shape[0]
    heads = q_ref.shape[1] // HD
    count = keys.shape[0]
    pre = heads * toks
    dec = heads * rows
    ctx = lax.axis_index("ctx")
    tp = lax.axis_index("tp")
    grp = lax.axis_index("grp")
    x, z = ctx // NZ, lax.rem(ctx, NZ)
    core = lax.rem(tp, 2)
    member = tp * 2 + grp

    def at_x(d):
        return lax.rem(x + d + NX, NX)

    def at_z(d):
        return lax.rem(z + d + NZ, NZ)

    def x_peer(d):
        return (at_x(d) * NZ + z, tp, grp)

    def z_peer(d):
        return (x * NZ + at_z(d), tp, grp)

    def group_peer(d):
        other = lax.rem(member + d, 8)
        return (ctx, other // 2, lax.rem(other, 2))

    sibling = (ctx, tp + 1 - 2 * core, grp)

    loads = [
        pltpu.make_async_copy(src, dst, load_sem.at[i])
        for i, (src, dst) in enumerate([(q_hbm, q_ref), (kup_hbm, kup), (vup_hbm, vup)])
    ]
    for load in loads:
        load.start()

    barrier = pltpu.get_barrier_semaphore()
    peers = [x_peer(d) for d in range(1, NX)] + [z_peer(d) for d in range(1, NZ)]
    peers += [group_peer(d) for d in range(1, 8)]
    for peer in peers:
        pl.semaphore_signal(barrier, inc=1, device_id=peer, device_id_type=MESH)

    def place_of(half, xx, zz):
        return (zz * 2 + half) * LINE + xx * SPAN

    turned = cache_ref[...].astype(F32).T
    mine = jnp.where(core == 0, turned[:SPAN], turned[SPAN:]).astype(BF16)
    here = pl.ds(pl.multiple_of(place_of(core, x, z), SPAN), SPAN)
    keys[here, : DL + DR] = mine
    keys[here, DL + DR :] = mine[:, DL:]
    pl.semaphore_wait(barrier, len(peers))

    def copy(first, size, sem, peer):
        part = keys.at[pl.ds(pl.multiple_of(first, SPAN // 2), size), :]
        return pltpu.make_async_remote_copy(
            src_ref=part, dst_ref=part, send_sem=send.at[0], recv_sem=recv.at[sem],
            device_id=peer, device_id_type=MESH,
        )

    def landed(sem, size):
        copy(0, size, sem, sibling).wait_recv()

    EVEN_Z, ODD_X, TWIN, EVEN_X, ODD_Z = 0, 4, 8, 13, 18
    ways = (1, -1)
    last = NZ // 2 - 1

    def along_z(half, xx, way, t, sem):
        first = place_of(half, xx, at_z(-way * t))
        if t < last:
            return copy(first, SPAN, sem, z_peer(way))
        return copy(first + (0 if way == 1 else SPAN // 2), SPAN // 2, sem, z_peer(way))

    def even_z(t):
        return [along_z(0, x, way, t, EVEN_Z + t) for way in ways]

    def odd_z(t, q):
        xx = at_x(jnp.where(q < 2, q, 5 - q))
        return [along_z(1, xx, way, t, ODD_Z + t * 4 + q) for way in ways]

    def both(t):
        return 2 * SPAN if t < last else SPAN

    def odd_x(d):
        return copy(place_of(1, x, z), SPAN, ODD_X + d, x_peer(d))

    def even_x(dz):
        first = place_of(0, x, at_z(dz))
        return [copy(first, SPAN, EVEN_X + abs(dz), x_peer(d)) for d in (1, 3, 2)]

    def twin(dz):
        return copy(place_of(core, 0, at_z(dz)), LINE, TWIN + abs(dz), sibling)

    def twins_landed(dz):
        landed(TWIN + dz, LINE if dz in (0, NZ // 2) else 2 * LINE)

    def start(copies):
        for one in copies:
            one.start()

    def on(which):
        return pl.when(core == which)

    @on(0)
    def _():
        start(even_z(0))

    @on(1)
    def _():
        for d in (3, 1, 2):
            odd_x(d).start()
        start(odd_z(0, 0))

    loads[0].wait()
    loads[1].wait()

    def absorb(pair):
        at = pl.ds(pl.multiple_of(pair * 2 * HD, 2 * HD), 2 * HD)
        both = q_ref[:, at].astype(F32)
        dboth = dq_ref[:, at].astype(F32)
        kept = []
        for sub in range(2):
            h = pair * 2 + sub
            every = jnp.concatenate([both, dboth, dboth], axis=0)[:, sub * HD : (sub + 1) * HD]
            block = kup[:, pl.ds(pl.multiple_of(h * DN, DN), DN)]
            absorbed = (dot(every[:, :DN].astype(BF16), block, 1, 1) * FACTOR).astype(BF16)
            rope = every[:, DN:] * FACTOR
            high = rope.astype(BF16).astype(F32)
            rope = jnp.concatenate([high, rope - high], axis=1).astype(BF16)
            here = pl.ds(pl.multiple_of(h * toks, toks), toks)
            queries[here, :DL] = absorbed[:toks]
            queries[here, DL:] = rope[:toks]
            kept.append((absorbed[toks:].astype(F32)[:rows], rope[toks:].astype(F32)[:rows]))
        here = pl.ds(pl.multiple_of(pre + pair * 2 * rows, 2 * rows), 2 * rows)
        queries[here, :DL] = jnp.concatenate([kept[0][0], kept[1][0]], axis=0).astype(BF16)
        queries[here, DL:] = jnp.concatenate([kept[0][1], kept[1][1]], axis=0).astype(BF16)

    lane = lax.broadcasted_iota(jnp.int32, (1, 128), 1)
    tok = lax.broadcasted_iota(jnp.int32, (toks, 1), 0)
    my_pos = jnp.where(tok < SPAN, place[2 * ctx], place[2 * ctx + 1]) * SPAN + (tok & (SPAN - 1))
    row = lax.broadcasted_iota(jnp.int32, (rows, 1), 0)
    limit = jnp.zeros((rows, 1), jnp.int32)
    for r in range(rows):
        limit = jnp.where(row == r, length[ctx * rows + r], limit)

    def scores(first, size, blocks, column):
        for j in range(size // 128):
            a, b = place[blocks[2 * j]], place[blocks[2 * j + 1]]
            pos = jnp.where(lane < SPAN, a, b) * SPAN + (lane & (SPAN - 1))
            cols = slice(j * 128, (j + 1) * 128)
            bias[:toks, cols] = jnp.where(pos <= my_pos, 0.0, MASKED)
            part = jnp.where(pos < limit, 0.0, MASKED)
            bias[toks:, cols] = jnp.concatenate([part] * (dec // rows), axis=0)
        from_keys = pl.ds(pl.multiple_of(first, 256), size)
        cols = pl.ds(pl.multiple_of(column, 256), size)
        half = pre // 2
        for begin, tall, extra in ((0, half, 0), (half, half, dec)):
            here = pl.ds(begin, tall + extra)
            add = [bias[:toks, :size]] * (tall // toks)
            if extra:
                add = add + [bias[toks:, :size]]
            s = dot(queries[here, :], keys[from_keys, :], 1, 1) + jnp.concatenate(add, axis=0)
            score[here, cols] = s
            best = top[here, :]
            for j in range(size // 128):
                best = jnp.maximum(best, s[:, j * 128 : (j + 1) * 128])
            top[here, :] = best

    def unit(dz, half, line):
        zz = at_z(dz)
        blocks = [2 * (j * NZ + zz) + half for j in range(NX)]
        scores(place_of(half, 0, zz), LINE, blocks, (line * 2 + half) * LINE)

    def full_line(dz, line):
        zz = at_z(dz)
        blocks = [2 * (j * NZ + zz) + half for half in (0, 1) for j in range(NX)]
        scores(place_of(0, 0, zz), 2 * LINE, blocks, line * 2 * LINE)

    def weigh(here, best, lines):
        den = jnp.zeros((best.shape[0], 128), F32)
        num = None
        for i, dz in enumerate(lines):
            e = jnp.exp2(score[here, i * 2 * LINE : (i + 1) * 2 * LINE] - best)
            for j in range(2 * LINE // 128):
                den = den + e[:, j * 128 : (j + 1) * 128]
            values = keys[pl.ds(pl.multiple_of(place_of(0, 0, at_z(dz)), 2 * LINE), 2 * LINE), :DL]
            part = dot(e.astype(BF16), values, 1, 0)
            num = part if num is None else num + part
        return num, den

    near, rest = (0, 1, -1), (2, -2, 3, -3, 4)

    def early(here, size):
        best = jnp.max(top[here, :], axis=1, keepdims=True)
        acc[here, :], part_den[here, :] = weigh(here, best, near)
        base[here, :] = jnp.broadcast_to(best, (size, 128))

    def join(here, best):
        num, den = weigh(here, best, rest)
        factor = jnp.exp2(base[here, :] - best)
        den = jnp.sum(den + part_den[here, :] * factor, axis=1, keepdims=True)
        return num + acc[here, :] * jnp.concatenate([factor] * (DL // 128), axis=1), den

    pl.loop(0, 1)(absorb)

    @on(0)
    def _():
        start(even_x(0))

    pl.loop(1, 6)(absorb)

    @on(0)
    def _():
        landed(EVEN_Z, both(0))
        start(even_z(1))
        start(even_x(-1) + even_x(1))
        landed(EVEN_X, 3 * SPAN)

    @on(1)
    def _():
        for q, d in ((1, 3), (2, 1), (3, 2)):
            landed(ODD_X + d, SPAN)
            start(odd_z(0, q))

    twin(0).start()
    pl.loop(6, heads // 2)(absorb)
    top[...] = jnp.full_like(top, MASKED)

    def pass_on(t, q):
        @on(1)
        def _():
            landed(ODD_Z + t * 4 + q, both(t))
            if t < last:
                start(odd_z(t + 1, q))

    def gather_line(t):
        places = (t + 1, -t - 1) if t < last else (t + 1,)

        @on(0)
        def _():
            landed(EVEN_X + t + 1, 3 * SPAN * len(places))

        for dz in places:
            twin(dz).start()

    def step_even(t):
        @on(0)
        def _():
            landed(EVEN_Z + t, both(t))
            if t < last:
                start(even_z(t + 1) + even_x(-t - 1) + even_x(t + 1))
            else:
                start(even_x(t + 1))

    def pair_of_lines(t, q, line):
        @pl.when(q == 2)
        def _():
            twins_landed(t)

        flip = lax.rem(q, 2)
        unit(jnp.where(flip == 0, t, -t), jnp.where(q < 2, core, 1 - core), line + flip)

    @pl.loop(0, 2)
    def _(i):
        pass_on(0, 2 * i)

        @pl.when(i == 1)
        def _():
            twins_landed(0)

        unit(0, jnp.where(i == 0, core, 1 - core), 0)
        pass_on(0, 2 * i + 1)

    gather_line(0)
    step_even(1)

    @pl.loop(0, 4)
    def _(q):
        pass_on(1, q)
        pair_of_lines(1, q, 1)

    gather_line(1)
    step_even(2)

    @pl.loop(0, 4)
    def _(q):
        pass_on(2, q)
        early(pl.ds(pl.multiple_of(q * (pre // 4), 128), pre // 4), pre // 4)

    gather_line(2)
    step_even(3)
    early(pl.ds(pre, dec), dec)

    twins_landed(2)

    @pl.loop(0, 2)
    def _(i):
        pass_on(3, 2 * i)
        pass_on(3, 2 * i + 1)
        full_line(2 - 4 * i, i)

    gather_line(3)
    twins_landed(3)

    @pl.loop(0, 3)
    def _(i):
        @pl.when(i == 2)
        def _():
            twins_landed(NZ // 2)

        full_line(jnp.where(i == 2, NZ // 2, 3 - 6 * i), 2 + i)

    loads[2].wait()

    here = pl.ds(pre, dec)
    cache = dc_ref[...].astype(F32)
    own = jnp.concatenate([cache, cache[:, DL:]], axis=1)
    own = jnp.concatenate([own] * heads, axis=0)
    own_score = jnp.sum(queries[here, :].astype(F32) * own, axis=1, keepdims=True)
    best = jnp.maximum(jnp.max(top[here, :], axis=1, keepdims=True), own_score)
    num, den = join(here, best)
    own_weight = jnp.exp2(own_score - best)
    lat = (num + own_weight * own[:, :DL]) / (den + own_weight)
    high = lat.astype(BF16).astype(F32)
    low = lat - high
    outs = []
    for h in range(heads):
        part = slice(h * rows, (h + 1) * rows)
        pieces = jnp.concatenate([high[part], low[part]], axis=0).astype(BF16)
        doubled = dot(pieces, vup[:, h * DV : (h + 1) * DV], 1, 0)
        outs.append(doubled[:rows] + doubled[rows:])
    wide = heads // 2 * DV
    halves = [jnp.concatenate(outs[: heads // 2], axis=1), jnp.concatenate(outs[heads // 2 :], axis=1)]
    xrows[x] = jnp.concatenate(halves, axis=0).astype(BF16)

    def x_rows(d):
        return pltpu.make_async_remote_copy(
            src_ref=xrows.at[x], dst_ref=xrows.at[x], send_sem=dec_send.at[0],
            recv_sem=dec_recv.at[0], device_id=x_peer(d), device_id_type=MESH,
        )

    def z_rows(d):
        return pltpu.make_async_remote_copy(
            src_ref=zsend.at[at_z(d)], dst_ref=zrecv.at[d - 1], send_sem=dec_send.at[1],
            recv_sem=dec_recv.at[1], device_id=z_peer(d), device_id_type=MESH,
        )

    def whole(src, dst, send_sem, recv_sem):
        return pltpu.make_async_remote_copy(
            src_ref=src, dst_ref=dst, send_sem=send_sem, recv_sem=recv_sem,
            device_id=sibling, device_id_type=MESH,
        )

    all_x = whole(xrows.at[pl.ds(0, NX - 1)], xrows.at[pl.ds(0, NX - 1)], dec_send.at[0], dec_recv.at[0])
    all_z = whole(zsend.at[pl.ds(0, NZ - 1)], zrecv, dec_send.at[1], dec_recv.at[1])

    for d in range(1, NX):
        x_rows(d).start()

    share = out_ref.shape[0]
    width = heads * DV

    def deliver(first, size, d):
        other = lax.rem(member + d, 8)
        return pltpu.make_async_remote_copy(
            src_ref=staged.at[pl.ds(pl.multiple_of(other * share, share), share), pl.ds(first, size)],
            dst_ref=out_ref.at[:, pl.ds(pl.multiple_of(member * width + first, 128), size)],
            send_sem=out_send.at[0], recv_sem=out_recv.at[0],
            device_id=group_peer(d), device_id_type=MESH,
        )

    all_out = whole(
        staged.at[pl.ds(0, 7 * share), :], out_ref.at[:, pl.ds(0, 7 * width)],
        out_send.at[0], out_recv.at[0],
    )

    def sort_rows():
        all_x.wait_recv()
        tall = 2 * rows
        to = lax.broadcasted_iota(jnp.int32, (NZ * tall, NX * tall), 0)
        fro = lax.broadcasted_iota(jnp.int32, (NZ * tall, NX * tall), 1)
        target = (x * NZ + to // tall) * rows + (to & (rows - 1))
        slot = jnp.full((NZ * tall, NX * tall), -1, jnp.int32)
        for j in range(NX):
            for i in range(rows):
                hit = (fro // tall == j) & ((fro & (rows - 1)) == i)
                slot = jnp.where(hit, slots[(j * NZ + z) * rows + i], slot)
        pick = (slot == target) & ((to & rows) == (fro & rows))
        pick = jnp.where(pick, 1.0, 0.0).astype(BF16)
        moved = dot(pick, xrows[...].reshape(NX * tall, wide), 1, 0).astype(BF16)
        zsend[...] = moved.reshape(NZ, tall, wide)
        for d in range(1, NZ):
            z_rows(d).start()

    pairs = heads // 2
    cuts = (0, 3, 6, 7, 8)

    @pl.loop(0, pairs)
    def _(pair):
        here = pl.ds(pl.multiple_of(pair * 2 * toks, 2 * toks), 2 * toks)
        num, den = join(here, jnp.max(top[here, :], axis=1, keepdims=True))
        lat = (num / den).astype(BF16)
        for sub in range(2):
            cols = pl.ds(pl.multiple_of((pair * 2 + sub) * DV, DV), DV)
            part = dot(lat[sub * toks : (sub + 1) * toks], vup[:, cols], 1, 0)
            staged[:, cols] = part.astype(BF16)
        pl.when(pair == 2)(sort_rows)
        for begin, end in zip(cuts[:-1], cuts[1:]):

            @pl.when(pair == end - 1)
            def _(begin=begin, end=end):
                for d in range(1, 8):
                    deliver(begin * 2 * DV, (end - begin) * 2 * DV, d).start()

    ours = pl.ds(pl.multiple_of(member * width, width), width)
    out_ref[:, ours] = staged[pl.ds(pl.multiple_of(member * share, share), share), :]
    all_z.wait_recv()
    total = zsend[z].astype(F32)
    for d in range(1, NZ):
        total = total + zrecv[d - 1].astype(F32)
    dec_ref[...] = jnp.concatenate([total[:rows], total[rows:]], axis=1).astype(BF16)
    sent = 2 * NX * NZ * SPAN - SPAN
    whole(keys.at[pl.ds(0, sent), :], keys.at[pl.ds(0, sent), :], send.at[0], recv.at[0]).wait_send()
    all_x.wait_send()
    all_z.wait_send()
    all_out.wait_send()
    all_out.wait_recv()


def hand_on(a, b, to_a, to_b, sems):
    copies = [pltpu.make_async_copy(a, to_a, sems.at[0]), pltpu.make_async_copy(b, to_b, sems.at[1])]
    for one in copies:
        one.start()
    for one in copies:
        one.wait()


def per_device(
    prefill_query, prompt_cache, key_up, value_up, block_place, decode_query, decode_cache,
    row_length, row_slot,
):
    toks, width = prefill_query.shape
    heads = width // HD
    rows = decode_query.shape[0]
    count = NX * NZ * toks
    smem = pl.BlockSpec(memory_space=pltpu.SMEM)
    vmem = pl.BlockSpec(memory_space=pltpu.VMEM)
    hbm = pl.BlockSpec(memory_space=pl.ANY)
    total = heads * (toks + rows)
    wide = heads // 2 * DV
    moved = pl.pallas_call(
        kernel,
        out_shape=(
            jax.ShapeDtypeStruct((toks // 8, 8 * heads * DV), BF16),
            jax.ShapeDtypeStruct((rows, heads * DV), BF16),
        ),
        in_specs=[smem, smem, smem, vmem, vmem, vmem, hbm, hbm, hbm],
        out_specs=(vmem, vmem),
        scratch_shapes=[
            pltpu.VMEM((toks, width), BF16),
            pltpu.VMEM((count, WIDE), BF16),
            pltpu.VMEM(key_up.shape, BF16),
            pltpu.VMEM(value_up.shape, BF16),
            pltpu.VMEM((total, WIDE), BF16),
            pltpu.VMEM((total, 5 * 2 * LINE), F32),
            pltpu.VMEM((total, 128), F32),
            pltpu.VMEM((total, DL), F32),
            pltpu.VMEM((total, 128), F32),
            pltpu.VMEM((total, 128), F32),
            pltpu.VMEM((toks + heads * rows, 2 * LINE), F32),
            pltpu.VMEM((toks, heads * DV), BF16),
            pltpu.VMEM((NX, 2 * rows, wide), BF16),
            pltpu.VMEM((NZ, 2 * rows, wide), BF16),
            pltpu.VMEM((NZ - 1, 2 * rows, wide), BF16),
            pltpu.SemaphoreType.DMA((3,)),
            pltpu.SemaphoreType.DMA((1,)),
            pltpu.SemaphoreType.DMA((34,)),
            pltpu.SemaphoreType.DMA((1,)),
            pltpu.SemaphoreType.DMA((1,)),
            pltpu.SemaphoreType.DMA((2,)),
            pltpu.SemaphoreType.DMA((2,)),
        ],
        compiler_params=pltpu.CompilerParams(
            vmem_limit_bytes=60 << 20, collective_id=0, has_side_effects=True
        ),
    )(
        block_place, row_length, row_slot, prompt_cache.T, decode_query, decode_cache,
        prefill_query, key_up, value_up,
    )
    return pl.pallas_call(
        hand_on,
        out_shape=tuple(jax.ShapeDtypeStruct(one.shape, one.dtype) for one in moved),
        in_specs=[hbm, hbm],
        out_specs=(hbm, hbm),
        scratch_shapes=[pltpu.SemaphoreType.DMA((2,))],
        compiler_params=pltpu.CompilerParams(vmem_limit_bytes=60 << 20),
    )(*moved)


def solution(mesh):
    return jax.shard_map(
        per_device,
        mesh=mesh,
        in_specs=(
            P("ctx", ("tp", "grp")),
            P("ctx", None),
            P(None, ("tp", "grp")),
            P(None, ("tp", "grp")),
            P(),
            P("ctx", ("tp", "grp")),
            P("ctx", None),
            P(),
            P(),
        ),
        out_specs=(P(("ctx", "tp", "grp"), None), P("ctx", ("tp", "grp"))),
        check_vma=False,
    )
```

```python
import functools
import math

import jax
import jax.numpy as jnp
from jax import lax
from jax.experimental import pallas as pl
from jax.experimental.pallas import tpu as pltpu
from jax.sharding import PartitionSpec as P

DL = 512
DR = 64
DN = 128
DV = 128
HD = DN + DR
WIDE = DL + 2 * DR
SPAN = 64
FACTOR = HD**-0.5 * math.log2(math.e)
MASKED = -1e30
NX, NZ = 4, 8
LINE = NX * SPAN
MESH = pl.DeviceIdType.MESH
F32 = jnp.float32
BF16 = jnp.bfloat16


def dot(a, b, ca, cb):
    return lax.dot_general(a, b, (((ca,), (cb,)), ((), ())), preferred_element_type=F32)


def kernel(
    place, length, slots, cache_ref, dq_ref, dc_ref, q_hbm, kup_hbm, vup_hbm, out_ref, dec_ref,
    q_ref, keys, kup, vup, queries, score, top, acc, part_den, base, bias,
    staged, xrows, zsend, zrecv,
    load_sem, send, recv, out_send, out_recv, dec_send, dec_recv,
):
    toks = q_ref.shape[0]
    rows = dq_ref.shape[0]
    heads = q_ref.shape[1] // HD
    count = keys.shape[0]
    pre = heads * toks
    dec = heads * rows
    ctx = lax.axis_index("ctx")
    tp = lax.axis_index("tp")
    grp = lax.axis_index("grp")
    x, z = ctx // NZ, lax.rem(ctx, NZ)
    core = lax.rem(tp, 2)
    member = tp * 2 + grp
    y = tp // 2 * 2 + grp

    def at_x(d):
        return lax.rem(x + d + NX, NX)

    def at_z(d):
        return lax.rem(z + d + NZ, NZ)

    def x_peer(d):
        return (at_x(d) * NZ + z, tp, grp)

    def z_peer(d):
        return (x * NZ + at_z(d), tp, grp)

    def group_peer(d):
        other = lax.rem(member + d, 8)
        return (ctx, other // 2, lax.rem(other, 2))

    def y_peer(d):
        other = lax.rem(y + d, 4)
        return (ctx, other // 2 * 2 + core, lax.rem(other, 2))

    sibling = (ctx, tp + 1 - 2 * core, grp)

    loads = [
        pltpu.make_async_copy(src, dst, load_sem.at[i])
        for i, (src, dst) in enumerate([(q_hbm, q_ref), (kup_hbm, kup), (vup_hbm, vup)])
    ]
    for load in loads:
        load.start()

    barrier = pltpu.get_barrier_semaphore()
    peers = [x_peer(d) for d in range(1, NX)] + [z_peer(d) for d in range(1, NZ)]
    peers += [group_peer(d) for d in range(1, 8)]
    for peer in peers:
        pl.semaphore_signal(barrier, inc=1, device_id=peer, device_id_type=MESH)

    def place_of(half, xx, zz):
        return (zz * 2 + half) * LINE + xx * SPAN

    turned = cache_ref[...].astype(F32).T
    mine = jnp.where(core == 0, turned[:SPAN], turned[SPAN:]).astype(BF16)

    @pl.when((core == 0) | (x == y))
    def _():
        here = pl.ds(pl.multiple_of(place_of(core, x, z), SPAN), SPAN)
        keys[here, : DL + DR] = mine
        keys[here, DL + DR :] = mine[:, DL:]

    pl.semaphore_wait(barrier, len(peers))

    def copy(first, size, sem, peer, sent=0):
        part = keys.at[pl.ds(pl.multiple_of(first, SPAN), size), :]
        return pltpu.make_async_remote_copy(
            src_ref=part, dst_ref=part, send_sem=send.at[sent], recv_sem=recv.at[sem],
            device_id=peer, device_id_type=MESH,
        )

    def landed(sem, size):
        copy(0, size, sem, sibling).wait_recv()

    def start(copies):
        for one in copies:
            one.start()

    def on(which):
        return pl.when(core == which)

    EVEN_Z, ODD_Z, TWIN, EVEN_X, ODD_Y, ODD_X = 0, 5, 10, 15, 20, 25
    far = NZ // 2

    def signs(k):
        return (k,) if k in (0, far) else (k, -k)

    def to_z(half, xx, sem):
        first = place_of(half, xx, z)
        return [copy(first, SPAN, sem + abs(d), z_peer(d)) for d in (1, -1, 2, -2, 3, -3, far)]

    def even_step(k):
        if k:
            landed(EVEN_Z + k, SPAN * len(signs(k)))
        for dz in signs(k):
            start([copy(place_of(0, x, at_z(dz)), SPAN, EVEN_X + k, x_peer(d)) for d in (1, 3, 2)])

    def odd_step(k):
        if k:
            landed(ODD_Z + k, SPAN * len(signs(k)))
        for dz in signs(k):
            start([copy(place_of(1, y, at_z(dz)), SPAN, ODD_Y + k, y_peer(d)) for d in (1, 3, 2)])

    def twin(dz):
        return copy(place_of(core, 0, at_z(dz)), LINE, TWIN + abs(dz), sibling)

    def even_line(k):
        landed(EVEN_X + k, 3 * SPAN * len(signs(k)))
        start([twin(dz) for dz in signs(k)])

    def odd_line(k):
        landed(ODD_Y + k, 3 * SPAN * len(signs(k)))
        start([twin(dz) for dz in signs(k)])

    def twins_landed(k):
        landed(TWIN + k, LINE * len(signs(k)))

    def odd_x():
        return [copy(place_of(1, x, z), SPAN, ODD_X, x_peer(d), 1) for d in (1, 3, 2)]

    @on(0)
    def _():
        start(to_z(0, x, EVEN_Z))
        even_step(0)

    @pl.when((core == 1) & (x == y))
    def _():
        start(odd_x())
        start(to_z(1, y, ODD_Z))
        odd_step(0)

    loads[0].wait()
    loads[1].wait()

    def absorb(pair):
        at = pl.ds(pl.multiple_of(pair * 2 * HD, 2 * HD), 2 * HD)
        both = q_ref[:, at].astype(F32)
        dboth = dq_ref[:, at].astype(F32)
        kept = []
        for sub in range(2):
            h = pair * 2 + sub
            every = jnp.concatenate([both, dboth, dboth], axis=0)[:, sub * HD : (sub + 1) * HD]
            block = kup[:, pl.ds(pl.multiple_of(h * DN, DN), DN)]
            absorbed = (dot(every[:, :DN].astype(BF16), block, 1, 1) * FACTOR).astype(BF16)
            rope = every[:, DN:] * FACTOR
            high = rope.astype(BF16).astype(F32)
            rope = jnp.concatenate([high, rope - high], axis=1).astype(BF16)
            here = pl.ds(pl.multiple_of(h * toks, toks), toks)
            queries[here, :DL] = absorbed[:toks]
            queries[here, DL:] = rope[:toks]
            kept.append((absorbed[toks:].astype(F32)[:rows], rope[toks:].astype(F32)[:rows]))
        here = pl.ds(pl.multiple_of(pre + pair * 2 * rows, 2 * rows), 2 * rows)
        queries[here, :DL] = jnp.concatenate([kept[0][0], kept[1][0]], axis=0).astype(BF16)
        queries[here, DL:] = jnp.concatenate([kept[0][1], kept[1][1]], axis=0).astype(BF16)

    lane = lax.broadcasted_iota(jnp.int32, (1, 128), 1)
    tok = lax.broadcasted_iota(jnp.int32, (toks, 1), 0)
    my_pos = jnp.where(tok < SPAN, place[2 * ctx], place[2 * ctx + 1]) * SPAN + (tok & (SPAN - 1))
    row = lax.broadcasted_iota(jnp.int32, (rows, 1), 0)
    limit = jnp.zeros((rows, 1), jnp.int32)
    for r in range(rows):
        limit = jnp.where(row == r, length[ctx * rows + r], limit)

    def scores(first, size, blocks, column):
        for j in range(size // 128):
            a, b = place[blocks[2 * j]], place[blocks[2 * j + 1]]
            pos = jnp.where(lane < SPAN, a, b) * SPAN + (lane & (SPAN - 1))
            cols = slice(j * 128, (j + 1) * 128)
            bias[:toks, cols] = jnp.where(pos <= my_pos, 0.0, MASKED)
            part = jnp.where(pos < limit, 0.0, MASKED)
            bias[toks:, cols] = jnp.concatenate([part] * (dec // rows), axis=0)
        from_keys = pl.ds(pl.multiple_of(first, 256), size)
        cols = pl.ds(pl.multiple_of(column, 256), size)
        half = pre // 2
        for begin, tall, extra in ((0, half, 0), (half, half, dec)):
            here = pl.ds(begin, tall + extra)
            add = [bias[:toks, :size]] * (tall // toks)
            if extra:
                add = add + [bias[toks:, :size]]
            s = dot(queries[here, :], keys[from_keys, :], 1, 1) + jnp.concatenate(add, axis=0)
            score[here, cols] = s
            best = top[here, :]
            for j in range(size // 128):
                best = jnp.maximum(best, s[:, j * 128 : (j + 1) * 128])
            top[here, :] = best

    def unit(dz, half, line):
        zz = at_z(dz)
        blocks = [2 * (j * NZ + zz) + half for j in range(NX)]
        scores(place_of(half, 0, zz), LINE, blocks, (line * 2 + half) * LINE)

    def full_line(dz, line):
        zz = at_z(dz)
        blocks = [2 * (j * NZ + zz) + half for half in (0, 1) for j in range(NX)]
        scores(place_of(0, 0, zz), 2 * LINE, blocks, line * 2 * LINE)

    def weigh(here, best, lines):
        den = jnp.zeros((best.shape[0], 128), F32)
        num = None
        for i, dz in enumerate(lines):
            e = jnp.exp2(score[here, i * 2 * LINE : (i + 1) * 2 * LINE] - best)
            for j in range(2 * LINE // 128):
                den = den + e[:, j * 128 : (j + 1) * 128]
            values = keys[pl.ds(pl.multiple_of(place_of(0, 0, at_z(dz)), 2 * LINE), 2 * LINE), :DL]
            part = dot(e.astype(BF16), values, 1, 0)
            num = part if num is None else num + part
        return num, den

    near, rest = (0, 1, -1), (2, -2, 3, -3, 4)

    def early(here, size):
        best = jnp.max(top[here, :], axis=1, keepdims=True)
        acc[here, :], part_den[here, :] = weigh(here, best, near)
        base[here, :] = jnp.broadcast_to(best, (size, 128))

    def join(here, best):
        num, den = weigh(here, best, rest)
        factor = jnp.exp2(base[here, :] - best)
        den = jnp.sum(den + part_den[here, :] * factor, axis=1, keepdims=True)
        return num + acc[here, :] * jnp.concatenate([factor] * (DL // 128), axis=1), den

    pl.loop(0, 4)(absorb)

    @pl.when((core == 1) & (x != y))
    def _():
        landed(ODD_X, SPAN)
        start(to_z(1, y, ODD_Z))
        odd_step(0)

    pl.loop(4, heads // 2)(absorb)
    top[...] = jnp.full_like(top, MASKED)

    @on(0)
    def _():
        even_step(1)
        even_line(0)

    @on(1)
    def _():
        twins_landed(0)

    @pl.loop(0, 3)
    def _(i):
        @pl.when((i == 1) & (core == 0))
        def _():
            even_step(2)
            even_line(1)

        @pl.when((i == 1) & (core == 1))
        def _():
            odd_line(0)
            odd_step(1)
            twins_landed(1)

        unit(jnp.where(i == 2, -1, i), 0, i)

    @pl.loop(0, 3)
    def _(i):
        @pl.when((i == 0) & (core == 0))
        def _():
            even_step(3)
            twins_landed(0)

        @pl.when((i == 0) & (core == 1))
        def _():
            odd_step(2)

        @pl.when((i == 1) & (core == 0))
        def _():
            even_line(2)
            even_step(4)
            twins_landed(1)

        @pl.when((i == 1) & (core == 1))
        def _():
            odd_line(1)
            odd_step(3)

        unit(jnp.where(i == 2, -1, i), 1, i)

    @pl.loop(0, 4)
    def _(q):
        @pl.when((q == 1) & (core == 0))
        def _():
            even_line(3)

        @pl.when((q == 1) & (core == 1))
        def _():
            odd_step(4)
            odd_line(2)

        @pl.when((q == 3) & (core == 0))
        def _():
            even_line(4)

        @pl.when((q == 3) & (core == 1))
        def _():
            odd_line(3)

        early(pl.ds(pl.multiple_of(q * (pre // 4), 128), pre // 4), pre // 4)

    early(pl.ds(pre, dec), dec)

    @on(1)
    def _():
        odd_line(4)

    twins_landed(2)

    @pl.loop(0, 2)
    def _(i):
        full_line(2 - 4 * i, i)

    twins_landed(3)

    @pl.loop(0, 3)
    def _(i):
        @pl.when(i == 2)
        def _():
            twins_landed(NZ // 2)

        full_line(jnp.where(i == 2, NZ // 2, 3 - 6 * i), 2 + i)

    loads[2].wait()

    here = pl.ds(pre, dec)
    cache = dc_ref[...].astype(F32)
    own = jnp.concatenate([cache, cache[:, DL:]], axis=1)
    own = jnp.concatenate([own] * heads, axis=0)
    own_score = jnp.sum(queries[here, :].astype(F32) * own, axis=1, keepdims=True)
    best = jnp.maximum(jnp.max(top[here, :], axis=1, keepdims=True), own_score)
    num, den = join(here, best)
    own_weight = jnp.exp2(own_score - best)
    lat = (num + own_weight * own[:, :DL]) / (den + own_weight)
    high = lat.astype(BF16).astype(F32)
    low = lat - high
    outs = []
    for h in range(heads):
        part = slice(h * rows, (h + 1) * rows)
        pieces = jnp.concatenate([high[part], low[part]], axis=0).astype(BF16)
        doubled = dot(pieces, vup[:, h * DV : (h + 1) * DV], 1, 0)
        outs.append(doubled[:rows] + doubled[rows:])
    wide = heads // 2 * DV
    halves = [jnp.concatenate(outs[: heads // 2], axis=1), jnp.concatenate(outs[heads // 2 :], axis=1)]
    xrows[x] = jnp.concatenate(halves, axis=0).astype(BF16)

    def x_rows(d):
        return pltpu.make_async_remote_copy(
            src_ref=xrows.at[x], dst_ref=xrows.at[x], send_sem=dec_send.at[0],
            recv_sem=dec_recv.at[0], device_id=x_peer(d), device_id_type=MESH,
        )

    def z_rows(d):
        return pltpu.make_async_remote_copy(
            src_ref=zsend.at[at_z(d)], dst_ref=zrecv.at[d - 1], send_sem=dec_send.at[1],
            recv_sem=dec_recv.at[1], device_id=z_peer(d), device_id_type=MESH,
        )

    def whole(src, dst, send_sem, recv_sem):
        return pltpu.make_async_remote_copy(
            src_ref=src, dst_ref=dst, send_sem=send_sem, recv_sem=recv_sem,
            device_id=sibling, device_id_type=MESH,
        )

    all_x = whole(xrows.at[pl.ds(0, NX - 1)], xrows.at[pl.ds(0, NX - 1)], dec_send.at[0], dec_recv.at[0])
    all_z = whole(zsend.at[pl.ds(0, NZ - 1)], zrecv, dec_send.at[1], dec_recv.at[1])

    for d in range(1, NX):
        x_rows(d).start()

    share = out_ref.shape[0]
    width = heads * DV

    def deliver(first, size, d):
        other = lax.rem(member + d, 8)
        return pltpu.make_async_remote_copy(
            src_ref=staged.at[pl.ds(pl.multiple_of(other * share, share), share), pl.ds(first, size)],
            dst_ref=out_ref.at[:, pl.ds(pl.multiple_of(member * width + first, 128), size)],
            send_sem=out_send.at[0], recv_sem=out_recv.at[0],
            device_id=group_peer(d), device_id_type=MESH,
        )

    all_out = whole(
        staged.at[pl.ds(0, 7 * share), :], out_ref.at[:, pl.ds(0, 7 * width)],
        out_send.at[0], out_recv.at[0],
    )

    def sort_rows():
        all_x.wait_recv()
        tall = 2 * rows
        to = lax.broadcasted_iota(jnp.int32, (NZ * tall, NX * tall), 0)
        fro = lax.broadcasted_iota(jnp.int32, (NZ * tall, NX * tall), 1)
        target = (x * NZ + to // tall) * rows + (to & (rows - 1))
        slot = jnp.full((NZ * tall, NX * tall), -1, jnp.int32)
        for j in range(NX):
            for i in range(rows):
                hit = (fro // tall == j) & ((fro & (rows - 1)) == i)
                slot = jnp.where(hit, slots[(j * NZ + z) * rows + i], slot)
        pick = (slot == target) & ((to & rows) == (fro & rows))
        pick = jnp.where(pick, 1.0, 0.0).astype(BF16)
        moved = dot(pick, xrows[...].reshape(NX * tall, wide), 1, 0).astype(BF16)
        zsend[...] = moved.reshape(NZ, tall, wide)
        for d in range(1, NZ):
            z_rows(d).start()

    pairs = heads // 2
    cuts = (0, 3, 6, 7, 8)

    @pl.loop(0, pairs)
    def _(pair):
        here = pl.ds(pl.multiple_of(pair * 2 * toks, 2 * toks), 2 * toks)
        num, den = join(here, jnp.max(top[here, :], axis=1, keepdims=True))
        lat = (num / den).astype(BF16)
        for sub in range(2):
            cols = pl.ds(pl.multiple_of((pair * 2 + sub) * DV, DV), DV)
            part = dot(lat[sub * toks : (sub + 1) * toks], vup[:, cols], 1, 0)
            staged[:, cols] = part.astype(BF16)
        pl.when(pair == 2)(sort_rows)
        for begin, end in zip(cuts[:-1], cuts[1:]):

            @pl.when(pair == end - 1)
            def _(begin=begin, end=end):
                for d in range(1, 8):
                    deliver(begin * 2 * DV, (end - begin) * 2 * DV, d).start()

    ours = pl.ds(pl.multiple_of(member * width, width), width)
    out_ref[:, ours] = staged[pl.ds(pl.multiple_of(member * share, share), share), :]
    all_z.wait_recv()
    total = zsend[z].astype(F32)
    for d in range(1, NZ):
        total = total + zrecv[d - 1].astype(F32)
    dec_ref[...] = jnp.concatenate([total[:rows], total[rows:]], axis=1).astype(BF16)
    sent = 2 * NX * NZ * SPAN - SPAN

    @pl.when((core == 1) & (x == y))
    def _():
        for one in odd_x():
            one.wait_send()

    whole(keys.at[pl.ds(0, sent), :], keys.at[pl.ds(0, sent), :], send.at[0], recv.at[0]).wait_send()
    all_x.wait_send()
    all_z.wait_send()
    all_out.wait_send()
    all_out.wait_recv()


def hand_on(a, b, to_a, to_b, sems):
    copies = [pltpu.make_async_copy(a, to_a, sems.at[0]), pltpu.make_async_copy(b, to_b, sems.at[1])]
    for one in copies:
        one.start()
    for one in copies:
        one.wait()


def per_device(
    prefill_query, prompt_cache, key_up, value_up, block_place, decode_query, decode_cache,
    row_length, row_slot,
):
    toks, width = prefill_query.shape
    heads = width // HD
    rows = decode_query.shape[0]
    count = NX * NZ * toks
    smem = pl.BlockSpec(memory_space=pltpu.SMEM)
    vmem = pl.BlockSpec(memory_space=pltpu.VMEM)
    hbm = pl.BlockSpec(memory_space=pl.ANY)
    total = heads * (toks + rows)
    wide = heads // 2 * DV
    moved = pl.pallas_call(
        kernel,
        out_shape=(
            jax.ShapeDtypeStruct((toks // 8, 8 * heads * DV), BF16),
            jax.ShapeDtypeStruct((rows, heads * DV), BF16),
        ),
        in_specs=[smem, smem, smem, vmem, vmem, vmem, hbm, hbm, hbm],
        out_specs=(vmem, vmem),
        scratch_shapes=[
            pltpu.VMEM((toks, width), BF16),
            pltpu.VMEM((count, WIDE), BF16),
            pltpu.VMEM(key_up.shape, BF16),
            pltpu.VMEM(value_up.shape, BF16),
            pltpu.VMEM((total, WIDE), BF16),
            pltpu.VMEM((total, 5 * 2 * LINE), F32),
            pltpu.VMEM((total, 128), F32),
            pltpu.VMEM((total, DL), F32),
            pltpu.VMEM((total, 128), F32),
            pltpu.VMEM((total, 128), F32),
            pltpu.VMEM((toks + heads * rows, 2 * LINE), F32),
            pltpu.VMEM((toks, heads * DV), BF16),
            pltpu.VMEM((NX, 2 * rows, wide), BF16),
            pltpu.VMEM((NZ, 2 * rows, wide), BF16),
            pltpu.VMEM((NZ - 1, 2 * rows, wide), BF16),
            pltpu.SemaphoreType.DMA((3,)),
            pltpu.SemaphoreType.DMA((2,)),
            pltpu.SemaphoreType.DMA((26,)),
            pltpu.SemaphoreType.DMA((1,)),
            pltpu.SemaphoreType.DMA((1,)),
            pltpu.SemaphoreType.DMA((2,)),
            pltpu.SemaphoreType.DMA((2,)),
        ],
        compiler_params=pltpu.CompilerParams(
            vmem_limit_bytes=60 << 20, collective_id=0, has_side_effects=True
        ),
    )(
        block_place, row_length, row_slot, prompt_cache.T, decode_query, decode_cache,
        prefill_query, key_up, value_up,
    )
    return pl.pallas_call(
        hand_on,
        out_shape=tuple(jax.ShapeDtypeStruct(one.shape, one.dtype) for one in moved),
        in_specs=[vmem, vmem],
        out_specs=(hbm, hbm),
        scratch_shapes=[pltpu.SemaphoreType.DMA((2,))],
    )(*moved)


def solution(mesh):
    return jax.shard_map(
        per_device,
        mesh=mesh,
        in_specs=(
            P("ctx", ("tp", "grp")),
            P("ctx", None),
            P(None, ("tp", "grp")),
            P(None, ("tp", "grp")),
            P(),
            P("ctx", ("tp", "grp")),
            P("ctx", None),
            P(),
            P(),
        ),
        out_specs=(P(("ctx", "tp", "grp"), None), P("ctx", ("tp", "grp"))),
        check_vma=False,
    )
```

```python
import functools
import math

import jax
import jax.numpy as jnp
from jax import lax
from jax.experimental import pallas as pl
from jax.experimental.pallas import tpu as pltpu
from jax.sharding import PartitionSpec as P

DL = 512
DR = 64
DN = 128
DV = 128
HD = DN + DR
WIDE = DL + 2 * DR
SPAN = 64
FACTOR = HD**-0.5 * math.log2(math.e)
MASKED = -1e30
NX, NZ = 4, 8
LINE = NX * SPAN
MESH = pl.DeviceIdType.MESH
F32 = jnp.float32
BF16 = jnp.bfloat16


def dot(a, b, ca, cb):
    return lax.dot_general(a, b, (((ca,), (cb,)), ((), ())), preferred_element_type=F32)


def kernel(
    place, length, slots, cache_ref, dq_ref, dc_ref, q_hbm, kup_hbm, vup_hbm, out_ref, dec_ref,
    q_ref, keys, kup, vup, queries, score, top, acc, part_den, base, bias,
    staged, xrows, zsend, zrecv,
    load_sem, send, recv, out_send, out_recv, dec_send, dec_recv,
):
    toks = q_ref.shape[0]
    rows = dq_ref.shape[0]
    heads = q_ref.shape[1] // HD
    count = keys.shape[0]
    pre = heads * toks
    dec = heads * rows
    ctx = lax.axis_index("ctx")
    tp = lax.axis_index("tp")
    grp = lax.axis_index("grp")
    x, z = ctx // NZ, lax.rem(ctx, NZ)
    core = lax.rem(tp, 2)
    member = tp * 2 + grp
    y = tp // 2 * 2 + grp

    def at_x(d):
        return lax.rem(x + d + NX, NX)

    def at_z(d):
        return lax.rem(z + d + NZ, NZ)

    def x_peer(d):
        return (at_x(d) * NZ + z, tp, grp)

    def z_peer(d):
        return (x * NZ + at_z(d), tp, grp)

    def group_peer(d):
        other = lax.rem(member + d, 8)
        return (ctx, other // 2, lax.rem(other, 2))

    def y_peer(d):
        other = lax.rem(y + d, 4)
        return (ctx, other // 2 * 2 + core, lax.rem(other, 2))

    sibling = (ctx, tp + 1 - 2 * core, grp)

    loads = [
        pltpu.make_async_copy(src, dst, load_sem.at[i])
        for i, (src, dst) in enumerate([(q_hbm, q_ref), (kup_hbm, kup), (vup_hbm, vup)])
    ]
    for load in loads:
        load.start()

    barrier = pltpu.get_barrier_semaphore()
    peers = [x_peer(d) for d in range(1, NX)] + [z_peer(d) for d in range(1, NZ)]
    peers += [group_peer(d) for d in range(1, 8)]
    for peer in peers:
        pl.semaphore_signal(barrier, inc=1, device_id=peer, device_id_type=MESH)

    def place_of(half, xx, zz):
        return (zz * 2 + half) * LINE + xx * SPAN

    turned = cache_ref[...].astype(F32).T
    mine = jnp.where(core == 0, turned[:SPAN], turned[SPAN:]).astype(BF16)

    here = pl.ds(pl.multiple_of(place_of(core, x, z), SPAN), SPAN)
    keys[here, : DL + DR] = mine
    keys[here, DL + DR :] = mine[:, DL:]
    pl.semaphore_wait(barrier, len(peers))

    def copy(first, size, sem, peer):
        part = keys.at[pl.ds(pl.multiple_of(first, SPAN), size), :]
        return pltpu.make_async_remote_copy(
            src_ref=part, dst_ref=part, send_sem=send.at[0], recv_sem=recv.at[sem],
            device_id=peer, device_id_type=MESH,
        )

    def landed(sem, size):
        copy(0, size, sem, sibling).wait_recv()

    def start(copies):
        for one in copies:
            one.start()

    def on(which):
        return pl.when(core == which)

    EVEN_Z, ODD_Z, TWIN, EVEN_X, ODD_Y, ODD_X = 0, 5, 10, 15, 20, 25
    far = NZ // 2

    def signs(k):
        return (k,) if k in (0, far) else (k, -k)

    def even_z(k):
        first = place_of(0, x, z)
        start([copy(first, SPAN, EVEN_Z + k, z_peer(dz)) for dz in signs(k)])

    def odd_z(k):
        first = place_of(1, y, z)
        start([copy(first, SPAN, ODD_Z + k, z_peer(dz)) for dz in signs(k)])

    def even_step(k):
        if k:
            landed(EVEN_Z + k, SPAN * len(signs(k)))
        for dz in signs(k):
            start([copy(place_of(0, x, at_z(dz)), SPAN, EVEN_X + k, x_peer(d)) for d in (1, 3, 2)])

    def odd_step(k):
        landed(ODD_Z + k, SPAN * len(signs(k)))
        for dz in signs(k):
            start([copy(place_of(1, y, at_z(dz)), SPAN, ODD_Y + k, y_peer(d)) for d in (1, 3, 2)])

    def twin(dz):
        return copy(place_of(core, 0, at_z(dz)), LINE, TWIN + abs(dz), sibling)

    def even_line(k):
        landed(EVEN_X + k, 3 * SPAN * len(signs(k)))
        start([twin(dz) for dz in signs(k)])

    def odd_line(k):
        landed(ODD_Y + k if k else ODD_X, 3 * SPAN * len(signs(k)))
        start([twin(dz) for dz in signs(k)])

    def twins_landed(k):
        landed(TWIN + k, LINE * len(signs(k)))

    @on(0)
    def _():
        even_z(1)

    @on(1)
    def _():
        start([copy(place_of(1, x, z), SPAN, ODD_X, x_peer(d)) for d in (1, 3, 2)])

    @pl.when((core == 1) & (x == y))
    def _():
        odd_z(1)

    loads[0].wait()
    loads[1].wait()

    def absorb(pair):
        at = pl.ds(pl.multiple_of(pair * 2 * HD, 2 * HD), 2 * HD)
        both = q_ref[:, at].astype(F32)
        dboth = dq_ref[:, at].astype(F32)
        kept = []
        for sub in range(2):
            h = pair * 2 + sub
            every = jnp.concatenate([both, dboth, dboth], axis=0)[:, sub * HD : (sub + 1) * HD]
            block = kup[:, pl.ds(pl.multiple_of(h * DN, DN), DN)]
            absorbed = (dot(every[:, :DN].astype(BF16), block, 1, 1) * FACTOR).astype(BF16)
            rope = every[:, DN:] * FACTOR
            high = rope.astype(BF16).astype(F32)
            rope = jnp.concatenate([high, rope - high], axis=1).astype(BF16)
            here = pl.ds(pl.multiple_of(h * toks, toks), toks)
            queries[here, :DL] = absorbed[:toks]
            queries[here, DL:] = rope[:toks]
            kept.append((absorbed[toks:].astype(F32)[:rows], rope[toks:].astype(F32)[:rows]))
        here = pl.ds(pl.multiple_of(pre + pair * 2 * rows, 2 * rows), 2 * rows)
        queries[here, :DL] = jnp.concatenate([kept[0][0], kept[1][0]], axis=0).astype(BF16)
        queries[here, DL:] = jnp.concatenate([kept[0][1], kept[1][1]], axis=0).astype(BF16)

    lane = lax.broadcasted_iota(jnp.int32, (1, 128), 1)
    tok = lax.broadcasted_iota(jnp.int32, (toks, 1), 0)
    my_pos = jnp.where(tok < SPAN, place[2 * ctx], place[2 * ctx + 1]) * SPAN + (tok & (SPAN - 1))
    row = lax.broadcasted_iota(jnp.int32, (rows, 1), 0)
    limit = jnp.zeros((rows, 1), jnp.int32)
    for r in range(rows):
        limit = jnp.where(row == r, length[ctx * rows + r], limit)

    def scores(first, size, blocks, column):
        for j in range(size // 128):
            a, b = place[blocks[2 * j]], place[blocks[2 * j + 1]]
            pos = jnp.where(lane < SPAN, a, b) * SPAN + (lane & (SPAN - 1))
            cols = slice(j * 128, (j + 1) * 128)
            bias[:toks, cols] = jnp.where(pos <= my_pos, 0.0, MASKED)
            part = jnp.where(pos < limit, 0.0, MASKED)
            bias[toks:, cols] = jnp.concatenate([part] * (dec // rows), axis=0)
        from_keys = pl.ds(pl.multiple_of(first, 256), size)
        cols = pl.ds(pl.multiple_of(column, 256), size)
        half = pre // 2
        for begin, tall, extra in ((0, half, 0), (half, half, dec)):
            here = pl.ds(begin, tall + extra)
            add = [bias[:toks, :size]] * (tall // toks)
            if extra:
                add = add + [bias[toks:, :size]]
            s = dot(queries[here, :], keys[from_keys, :], 1, 1) + jnp.concatenate(add, axis=0)
            score[here, cols] = s
            best = top[here, :]
            for j in range(size // 128):
                best = jnp.maximum(best, s[:, j * 128 : (j + 1) * 128])
            top[here, :] = best

    def unit(dz, half, line):
        zz = at_z(dz)
        blocks = [2 * (j * NZ + zz) + half for j in range(NX)]
        scores(place_of(half, 0, zz), LINE, blocks, (line * 2 + half) * LINE)

    def full_line(dz, line):
        zz = at_z(dz)
        blocks = [2 * (j * NZ + zz) + half for half in (0, 1) for j in range(NX)]
        scores(place_of(0, 0, zz), 2 * LINE, blocks, line * 2 * LINE)

    def weigh(here, best, lines):
        den = jnp.zeros((best.shape[0], 128), F32)
        num = None
        for i, dz in enumerate(lines):
            e = jnp.exp2(score[here, i * 2 * LINE : (i + 1) * 2 * LINE] - best)
            for j in range(2 * LINE // 128):
                den = den + e[:, j * 128 : (j + 1) * 128]
            values = keys[pl.ds(pl.multiple_of(place_of(0, 0, at_z(dz)), 2 * LINE), 2 * LINE), :DL]
            part = dot(e.astype(BF16), values, 1, 0)
            num = part if num is None else num + part
        return num, den

    near, rest = (0, 1, -1), (2, -2, 3, -3, 4)

    def early(here, size):
        best = jnp.max(top[here, :], axis=1, keepdims=True)
        acc[here, :], part_den[here, :] = weigh(here, best, near)
        base[here, :] = jnp.broadcast_to(best, (size, 128))

    def join(here, best):
        num, den = weigh(here, best, rest)
        factor = jnp.exp2(base[here, :] - best)
        den = jnp.sum(den + part_den[here, :] * factor, axis=1, keepdims=True)
        return num + acc[here, :] * jnp.concatenate([factor] * (DL // 128), axis=1), den

    pl.loop(0, 2)(absorb)

    @on(0)
    def _():
        even_step(0)
        even_z(2)

    pl.loop(2, 4)(absorb)

    @on(0)
    def _():
        even_z(3)

    pl.loop(4, 6)(absorb)

    @on(0)
    def _():
        even_step(1)
        even_z(4)

    @on(1)
    def _():
        odd_line(0)

    @pl.when((core == 1) & (x != y))
    def _():
        odd_z(1)

    @on(1)
    def _():
        odd_z(2)

    pl.loop(6, heads // 2)(absorb)
    top[...] = jnp.full_like(top, MASKED)

    @on(0)
    def _():
        even_line(0)

    @on(1)
    def _():
        odd_z(3)

    @pl.loop(0, 2)
    def _(i):
        @pl.when((i == 1) & (core == 0))
        def _():
            even_step(2)

        @pl.when((i == 1) & (core == 1))
        def _():
            odd_z(4)

        @pl.when(i == 1)
        def _():
            twins_landed(0)

        unit(0, jnp.where(i == 0, core, 1 - core), 0)

    @on(0)
    def _():
        even_step(3)
        even_line(1)
        even_step(4)

    @on(1)
    def _():
        odd_step(1)
        odd_step(2)
        twins_landed(1)

    @pl.loop(0, 4)
    def _(i):
        @pl.when((i == 2) & (core == 0))
        def _():
            even_line(2)
            twins_landed(1)

        @pl.when((i == 2) & (core == 1))
        def _():
            odd_line(1)
            odd_step(3)
            odd_step(4)

        flip = lax.rem(i, 2)
        unit(1 - 2 * flip, i // 2, 1 + flip)

    @pl.loop(0, 4)
    def _(q):
        @pl.when((q == 1) & (core == 0))
        def _():
            even_line(3)

        @pl.when((q == 1) & (core == 1))
        def _():
            odd_line(2)

        @pl.when((q == 3) & (core == 0))
        def _():
            even_line(4)

        @pl.when((q == 3) & (core == 1))
        def _():
            odd_line(3)

        early(pl.ds(pl.multiple_of(q * (pre // 4), 128), pre // 4), pre // 4)

    early(pl.ds(pre, dec), dec)

    @on(1)
    def _():
        odd_line(4)

    twins_landed(2)

    @pl.loop(0, 2)
    def _(i):
        full_line(2 - 4 * i, i)

    twins_landed(3)

    @pl.loop(0, 3)
    def _(i):
        @pl.when(i == 2)
        def _():
            twins_landed(NZ // 2)

        full_line(jnp.where(i == 2, NZ // 2, 3 - 6 * i), 2 + i)

    loads[2].wait()

    here = pl.ds(pre, dec)
    cache = dc_ref[...].astype(F32)
    own = jnp.concatenate([cache, cache[:, DL:]], axis=1)
    own = jnp.concatenate([own] * heads, axis=0)
    own_score = jnp.sum(queries[here, :].astype(F32) * own, axis=1, keepdims=True)
    best = jnp.maximum(jnp.max(top[here, :], axis=1, keepdims=True), own_score)
    num, den = join(here, best)
    own_weight = jnp.exp2(own_score - best)
    lat = (num + own_weight * own[:, :DL]) / (den + own_weight)
    high = lat.astype(BF16).astype(F32)
    low = lat - high
    outs = []
    for h in range(heads):
        part = slice(h * rows, (h + 1) * rows)
        pieces = jnp.concatenate([high[part], low[part]], axis=0).astype(BF16)
        doubled = dot(pieces, vup[:, h * DV : (h + 1) * DV], 1, 0)
        outs.append(doubled[:rows] + doubled[rows:])
    wide = heads // 2 * DV
    halves = [jnp.concatenate(outs[: heads // 2], axis=1), jnp.concatenate(outs[heads // 2 :], axis=1)]
    xrows[x] = jnp.concatenate(halves, axis=0).astype(BF16)

    def x_rows(d):
        return pltpu.make_async_remote_copy(
            src_ref=xrows.at[x], dst_ref=xrows.at[x], send_sem=dec_send.at[0],
            recv_sem=dec_recv.at[0], device_id=x_peer(d), device_id_type=MESH,
        )

    def z_rows(d):
        return pltpu.make_async_remote_copy(
            src_ref=zsend.at[at_z(d)], dst_ref=zrecv.at[d - 1], send_sem=dec_send.at[1],
            recv_sem=dec_recv.at[1], device_id=z_peer(d), device_id_type=MESH,
        )

    def whole(src, dst, send_sem, recv_sem):
        return pltpu.make_async_remote_copy(
            src_ref=src, dst_ref=dst, send_sem=send_sem, recv_sem=recv_sem,
            device_id=sibling, device_id_type=MESH,
        )

    all_x = whole(xrows.at[pl.ds(0, NX - 1)], xrows.at[pl.ds(0, NX - 1)], dec_send.at[0], dec_recv.at[0])
    all_z = whole(zsend.at[pl.ds(0, NZ - 1)], zrecv, dec_send.at[1], dec_recv.at[1])

    for d in range(1, NX):
        x_rows(d).start()

    share = out_ref.shape[0]
    width = heads * DV

    def deliver(first, size, d):
        other = lax.rem(member + d, 8)
        return pltpu.make_async_remote_copy(
            src_ref=staged.at[pl.ds(pl.multiple_of(other * share, share), share), pl.ds(first, size)],
            dst_ref=out_ref.at[:, pl.ds(pl.multiple_of(member * width + first, 128), size)],
            send_sem=out_send.at[0], recv_sem=out_recv.at[0],
            device_id=group_peer(d), device_id_type=MESH,
        )

    all_out = whole(
        staged.at[pl.ds(0, 7 * share), :], out_ref.at[:, pl.ds(0, 7 * width)],
        out_send.at[0], out_recv.at[0],
    )

    def sort_rows():
        all_x.wait_recv()
        tall = 2 * rows
        to = lax.broadcasted_iota(jnp.int32, (NZ * tall, NX * tall), 0)
        fro = lax.broadcasted_iota(jnp.int32, (NZ * tall, NX * tall), 1)
        target = (x * NZ + to // tall) * rows + (to & (rows - 1))
        slot = jnp.full((NZ * tall, NX * tall), -1, jnp.int32)
        for j in range(NX):
            for i in range(rows):
                hit = (fro // tall == j) & ((fro & (rows - 1)) == i)
                slot = jnp.where(hit, slots[(j * NZ + z) * rows + i], slot)
        pick = (slot == target) & ((to & rows) == (fro & rows))
        pick = jnp.where(pick, 1.0, 0.0).astype(BF16)
        moved = dot(pick, xrows[...].reshape(NX * tall, wide), 1, 0).astype(BF16)
        zsend[...] = moved.reshape(NZ, tall, wide)
        for d in range(1, NZ):
            z_rows(d).start()

    pairs = heads // 2
    cuts = (0, 3, 6, 7, 8)

    @pl.loop(0, pairs)
    def _(pair):
        here = pl.ds(pl.multiple_of(pair * 2 * toks, 2 * toks), 2 * toks)
        num, den = join(here, jnp.max(top[here, :], axis=1, keepdims=True))
        lat = (num / den).astype(BF16)
        for sub in range(2):
            cols = pl.ds(pl.multiple_of((pair * 2 + sub) * DV, DV), DV)
            part = dot(lat[sub * toks : (sub + 1) * toks], vup[:, cols], 1, 0)
            staged[:, cols] = part.astype(BF16)
        pl.when(pair == 2)(sort_rows)
        for begin, end in zip(cuts[:-1], cuts[1:]):

            @pl.when(pair == end - 1)
            def _(begin=begin, end=end):
                for d in range(1, 8):
                    deliver(begin * 2 * DV, (end - begin) * 2 * DV, d).start()

    ours = pl.ds(pl.multiple_of(member * width, width), width)
    out_ref[:, ours] = staged[pl.ds(pl.multiple_of(member * share, share), share), :]
    all_z.wait_recv()
    total = zsend[z].astype(F32)
    for d in range(1, NZ):
        total = total + zrecv[d - 1].astype(F32)
    dec_ref[...] = jnp.concatenate([total[:rows], total[rows:]], axis=1).astype(BF16)
    sent = 2 * NX * NZ * SPAN - SPAN

    whole(keys.at[pl.ds(0, sent), :], keys.at[pl.ds(0, sent), :], send.at[0], recv.at[0]).wait_send()
    all_x.wait_send()
    all_z.wait_send()
    all_out.wait_send()
    all_out.wait_recv()


def hand_on(a, b, to_a, to_b, sems):
    copies = [pltpu.make_async_copy(a, to_a, sems.at[0]), pltpu.make_async_copy(b, to_b, sems.at[1])]
    for one in copies:
        one.start()
    for one in copies:
        one.wait()


def per_device(
    prefill_query, prompt_cache, key_up, value_up, block_place, decode_query, decode_cache,
    row_length, row_slot,
):
    toks, width = prefill_query.shape
    heads = width // HD
    rows = decode_query.shape[0]
    count = NX * NZ * toks
    smem = pl.BlockSpec(memory_space=pltpu.SMEM)
    vmem = pl.BlockSpec(memory_space=pltpu.VMEM)
    hbm = pl.BlockSpec(memory_space=pl.ANY)
    total = heads * (toks + rows)
    wide = heads // 2 * DV
    moved = pl.pallas_call(
        kernel,
        out_shape=(
            jax.ShapeDtypeStruct((toks // 8, 8 * heads * DV), BF16),
            jax.ShapeDtypeStruct((rows, heads * DV), BF16),
        ),
        in_specs=[smem, smem, smem, vmem, vmem, vmem, hbm, hbm, hbm],
        out_specs=(vmem, vmem),
        scratch_shapes=[
            pltpu.VMEM((toks, width), BF16),
            pltpu.VMEM((count, WIDE), BF16),
            pltpu.VMEM(key_up.shape, BF16),
            pltpu.VMEM(value_up.shape, BF16),
            pltpu.VMEM((total, WIDE), BF16),
            pltpu.VMEM((total, 5 * 2 * LINE), F32),
            pltpu.VMEM((total, 128), F32),
            pltpu.VMEM((total, DL), F32),
            pltpu.VMEM((total, 128), F32),
            pltpu.VMEM((total, 128), F32),
            pltpu.VMEM((toks + heads * rows, 2 * LINE), F32),
            pltpu.VMEM((toks, heads * DV), BF16),
            pltpu.VMEM((NX, 2 * rows, wide), BF16),
            pltpu.VMEM((NZ, 2 * rows, wide), BF16),
            pltpu.VMEM((NZ - 1, 2 * rows, wide), BF16),
            pltpu.SemaphoreType.DMA((3,)),
            pltpu.SemaphoreType.DMA((1,)),
            pltpu.SemaphoreType.DMA((26,)),
            pltpu.SemaphoreType.DMA((1,)),
            pltpu.SemaphoreType.DMA((1,)),
            pltpu.SemaphoreType.DMA((2,)),
            pltpu.SemaphoreType.DMA((2,)),
        ],
        compiler_params=pltpu.CompilerParams(
            vmem_limit_bytes=60 << 20, collective_id=0, has_side_effects=True
        ),
    )(
        block_place, row_length, row_slot, prompt_cache.T, decode_query, decode_cache,
        prefill_query, key_up, value_up,
    )
    return pl.pallas_call(
        hand_on,
        out_shape=tuple(jax.ShapeDtypeStruct(one.shape, one.dtype) for one in moved),
        in_specs=[vmem, vmem],
        out_specs=(hbm, hbm),
        scratch_shapes=[pltpu.SemaphoreType.DMA((2,))],
    )(*moved)


def solution(mesh):
    return jax.shard_map(
        per_device,
        mesh=mesh,
        in_specs=(
            P("ctx", ("tp", "grp")),
            P("ctx", None),
            P(None, ("tp", "grp")),
            P(None, ("tp", "grp")),
            P(),
            P("ctx", ("tp", "grp")),
            P("ctx", None),
            P(),
            P(),
        ),
        out_specs=(P(("ctx", "tp", "grp"), None), P("ctx", ("tp", "grp"))),
        check_vma=False,
    )
```

```python
import functools
import math

import jax
import jax.numpy as jnp
from jax import lax
from jax.experimental import pallas as pl
from jax.experimental.pallas import tpu as pltpu
from jax.sharding import PartitionSpec as P

DL = 512
DR = 64
DN = 128
DV = 128
HD = DN + DR
WIDE = DL + 2 * DR
SPAN = 64
FACTOR = HD**-0.5 * math.log2(math.e)
MASKED = -1e30
NX, NZ = 4, 8
LINE = NX * SPAN
MESH = pl.DeviceIdType.MESH
F32 = jnp.float32
BF16 = jnp.bfloat16


def dot(a, b, ca, cb):
    return lax.dot_general(a, b, (((ca,), (cb,)), ((), ())), preferred_element_type=F32)


def kernel(
    place, length, slots, cache_ref, dq_ref, dc_ref, q_hbm, kup_hbm, vup_hbm, out_ref, dec_ref,
    q_ref, keys, kup, vup, queries, score, top, acc, part_den, base, bias,
    staged, xrows, zsend, zrecv,
    load_sem, send, recv, out_send, out_recv, dec_send, dec_recv,
):
    toks = q_ref.shape[0]
    rows = dq_ref.shape[0]
    heads = q_ref.shape[1] // HD
    count = keys.shape[0]
    pre = heads * toks
    dec = heads * rows
    ctx = lax.axis_index("ctx")
    tp = lax.axis_index("tp")
    grp = lax.axis_index("grp")
    x, z = ctx // NZ, lax.rem(ctx, NZ)
    core = lax.rem(tp, 2)
    member = tp * 2 + grp
    y = tp // 2 * 2 + grp

    def at_x(d):
        return lax.rem(x + d + NX, NX)

    def at_z(d):
        return lax.rem(z + d + NZ, NZ)

    def x_peer(d):
        return (at_x(d) * NZ + z, tp, grp)

    def z_peer(d):
        return (x * NZ + at_z(d), tp, grp)

    def group_peer(d):
        other = lax.rem(member + d, 8)
        return (ctx, other // 2, lax.rem(other, 2))

    def y_peer(d):
        other = lax.rem(y + d, 4)
        return (ctx, other // 2 * 2 + core, lax.rem(other, 2))

    sibling = (ctx, tp + 1 - 2 * core, grp)

    loads = [
        pltpu.make_async_copy(src, dst, load_sem.at[i])
        for i, (src, dst) in enumerate([(q_hbm, q_ref), (kup_hbm, kup), (vup_hbm, vup)])
    ]
    for load in loads:
        load.start()

    barrier = pltpu.get_barrier_semaphore()
    peers = [x_peer(d) for d in range(1, NX)] + [z_peer(d) for d in range(1, NZ)]
    peers += [group_peer(d) for d in range(1, 8)]
    for peer in peers:
        pl.semaphore_signal(barrier, inc=1, device_id=peer, device_id_type=MESH)

    def place_of(half, xx, zz):
        return (zz * 2 + half) * LINE + xx * SPAN

    turned = cache_ref[...].astype(F32).T
    mine = jnp.where(core == 0, turned[:SPAN], turned[SPAN:]).astype(BF16)

    here = pl.ds(pl.multiple_of(place_of(core, x, z), SPAN), SPAN)
    keys[here, : DL + DR] = mine
    keys[here, DL + DR :] = mine[:, DL:]
    pl.semaphore_wait(barrier, len(peers))

    def copy(first, size, sem, peer):
        part = keys.at[pl.ds(pl.multiple_of(first, SPAN), size), :]
        return pltpu.make_async_remote_copy(
            src_ref=part, dst_ref=part, send_sem=send.at[0], recv_sem=recv.at[sem],
            device_id=peer, device_id_type=MESH,
        )

    def landed(sem, size):
        copy(0, size, sem, sibling).wait_recv()

    def start(copies):
        for one in copies:
            one.start()

    def on(which):
        return pl.when(core == which)

    EVEN_Z, ODD_Z, TWIN, EVEN_X, ODD_Y, ODD_X = 0, 5, 10, 15, 20, 25
    far = NZ // 2

    def signs(k):
        return (k,) if k in (0, far) else (k, -k)

    def even_z(k):
        first = place_of(0, x, z)
        start([copy(first, SPAN, EVEN_Z + k, z_peer(dz)) for dz in signs(k)])

    def odd_z(k):
        first = place_of(1, y, z)
        start([copy(first, SPAN, ODD_Z + k, z_peer(dz)) for dz in signs(k)])

    def even_step(k):
        if k:
            landed(EVEN_Z + k, SPAN * len(signs(k)))
        for dz in signs(k):
            start([copy(place_of(0, x, at_z(dz)), SPAN, EVEN_X + k, x_peer(d)) for d in (1, 3, 2)])

    def odd_step(k):
        landed(ODD_Z + k, SPAN * len(signs(k)))
        for dz in signs(k):
            start([copy(place_of(1, y, at_z(dz)), SPAN, ODD_Y + k, y_peer(d)) for d in (1, 3, 2)])

    def twin(dz):
        return copy(place_of(core, 0, at_z(dz)), LINE, TWIN + abs(dz), sibling)

    def even_line(k):
        landed(EVEN_X + k, 3 * SPAN * len(signs(k)))
        start([twin(dz) for dz in signs(k)])

    def odd_line(k):
        landed(ODD_Y + k if k else ODD_X, 3 * SPAN * len(signs(k)))
        start([twin(dz) for dz in signs(k)])

    def twins_landed(k):
        landed(TWIN + k, LINE * len(signs(k)))

    @on(0)
    def _():
        even_z(1)

    @on(1)
    def _():
        start([copy(place_of(1, x, z), SPAN, ODD_X, x_peer(d)) for d in (1, 3, 2)])

    @pl.when((core == 1) & (x == y))
    def _():
        odd_z(1)

    loads[0].wait()
    loads[1].wait()

    def absorb(pair):
        at = pl.ds(pl.multiple_of(pair * 2 * HD, 2 * HD), 2 * HD)
        both = q_ref[:, at].astype(F32)
        dboth = dq_ref[:, at].astype(F32)
        kept = []
        for sub in range(2):
            h = pair * 2 + sub
            every = jnp.concatenate([both, dboth, dboth], axis=0)[:, sub * HD : (sub + 1) * HD]
            block = kup[:, pl.ds(pl.multiple_of(h * DN, DN), DN)]
            absorbed = (dot(every[:, :DN].astype(BF16), block, 1, 1) * FACTOR).astype(BF16)
            rope = every[:, DN:] * FACTOR
            high = rope.astype(BF16).astype(F32)
            rope = jnp.concatenate([high, rope - high], axis=1).astype(BF16)
            here = pl.ds(pl.multiple_of(h * toks, toks), toks)
            queries[here, :DL] = absorbed[:toks]
            queries[here, DL:] = rope[:toks]
            kept.append((absorbed[toks:].astype(F32)[:rows], rope[toks:].astype(F32)[:rows]))
        here = pl.ds(pl.multiple_of(pre + pair * 2 * rows, 2 * rows), 2 * rows)
        queries[here, :DL] = jnp.concatenate([kept[0][0], kept[1][0]], axis=0).astype(BF16)
        queries[here, DL:] = jnp.concatenate([kept[0][1], kept[1][1]], axis=0).astype(BF16)

    lane = lax.broadcasted_iota(jnp.int32, (1, 128), 1)
    tok = lax.broadcasted_iota(jnp.int32, (toks, 1), 0)
    my_pos = jnp.where(tok < SPAN, place[2 * ctx], place[2 * ctx + 1]) * SPAN + (tok & (SPAN - 1))
    row = lax.broadcasted_iota(jnp.int32, (rows, 1), 0)
    limit = jnp.zeros((rows, 1), jnp.int32)
    for r in range(rows):
        limit = jnp.where(row == r, length[ctx * rows + r], limit)

    def scores(first, size, blocks, column):
        for j in range(size // 128):
            a, b = place[blocks[2 * j]], place[blocks[2 * j + 1]]
            pos = jnp.where(lane < SPAN, a, b) * SPAN + (lane & (SPAN - 1))
            cols = slice(j * 128, (j + 1) * 128)
            bias[:toks, cols] = jnp.where(pos <= my_pos, 0.0, MASKED)
            part = jnp.where(pos < limit, 0.0, MASKED)
            bias[toks:, cols] = jnp.concatenate([part] * (dec // rows), axis=0)
        from_keys = pl.ds(pl.multiple_of(first, 256), size)
        cols = pl.ds(pl.multiple_of(column, 256), size)
        half = pre // 2
        for begin, tall, extra in ((0, half, 0), (half, half, dec)):
            here = pl.ds(begin, tall + extra)
            add = [bias[:toks, :size]] * (tall // toks)
            if extra:
                add = add + [bias[toks:, :size]]
            s = dot(queries[here, :], keys[from_keys, :], 1, 1) + jnp.concatenate(add, axis=0)
            score[here, cols] = s
            best = top[here, :]
            for j in range(size // 128):
                best = jnp.maximum(best, s[:, j * 128 : (j + 1) * 128])
            top[here, :] = best

    def unit(dz, half, line):
        zz = at_z(dz)
        blocks = [2 * (j * NZ + zz) + half for j in range(NX)]
        scores(place_of(half, 0, zz), LINE, blocks, (line * 2 + half) * LINE)

    def full_line(dz, line):
        zz = at_z(dz)
        blocks = [2 * (j * NZ + zz) + half for half in (0, 1) for j in range(NX)]
        scores(place_of(0, 0, zz), 2 * LINE, blocks, line * 2 * LINE)

    def weigh(here, best, lines):
        den = jnp.zeros((best.shape[0], 128), F32)
        num = None
        for i, dz in enumerate(lines):
            e = jnp.exp2(score[here, i * 2 * LINE : (i + 1) * 2 * LINE] - best)
            for j in range(2 * LINE // 128):
                den = den + e[:, j * 128 : (j + 1) * 128]
            values = keys[pl.ds(pl.multiple_of(place_of(0, 0, at_z(dz)), 2 * LINE), 2 * LINE), :DL]
            part = dot(e.astype(BF16), values, 1, 0)
            num = part if num is None else num + part
        return num, den

    near, rest = (0, 1, -1), (3, -3, 4, 2, -2)

    def early(here, size):
        best = jnp.max(top[here, :], axis=1, keepdims=True)
        acc[here, :], part_den[here, :] = weigh(here, best, near)
        base[here, :] = jnp.broadcast_to(best, (size, 128))

    def join(here, best):
        num, den = weigh(here, best, rest)
        factor = jnp.exp2(base[here, :] - best)
        den = jnp.sum(den + part_den[here, :] * factor, axis=1, keepdims=True)
        return num + acc[here, :] * jnp.concatenate([factor] * (DL // 128), axis=1), den

    pl.loop(0, 2)(absorb)

    @on(0)
    def _():
        even_step(0)
        even_z(2)

    pl.loop(2, 4)(absorb)

    @on(0)
    def _():
        even_z(3)

    pl.loop(4, 6)(absorb)

    @on(0)
    def _():
        even_step(1)
        even_z(4)

    @on(1)
    def _():
        odd_line(0)

    @pl.when((core == 1) & (x != y))
    def _():
        odd_z(1)

    @on(1)
    def _():
        odd_z(2)

    pl.loop(6, heads // 2)(absorb)
    top[...] = jnp.full_like(top, MASKED)

    @on(0)
    def _():
        even_line(0)

    @on(1)
    def _():
        odd_z(3)

    @pl.loop(0, 2)
    def _(i):
        @pl.when((i == 1) & (core == 0))
        def _():
            even_step(2)

        @pl.when((i == 1) & (core == 1))
        def _():
            odd_z(4)

        @pl.when(i == 1)
        def _():
            twins_landed(0)

        unit(0, jnp.where(i == 0, core, 1 - core), 0)

    @on(0)
    def _():
        even_step(3)
        even_line(1)
        even_step(4)

    @on(1)
    def _():
        odd_step(1)
        odd_step(2)
        twins_landed(1)

    @pl.loop(0, 6)
    def _(i):
        @pl.when((i == 2) & (core == 0))
        def _():
            even_line(2)

        @pl.when((i == 4) & (core == 0))
        def _():
            even_line(3)
            twins_landed(1)

        @pl.when((i == 2) & (core == 1))
        def _():
            odd_line(1)
            odd_step(3)
            odd_step(4)

        @pl.when((i == 4) & (core == 1))
        def _():
            twins_landed(2)

        flip = lax.rem(i, 2)
        second = i // 2 == 2 - (1 - core)
        half = jnp.where((i < 2) | second, 0, 1)
        dz = jnp.where(second, 2, 1)
        unit(jnp.where(flip == 0, dz, -dz), half, jnp.where(second, 3, 1) + flip)

    @pl.loop(0, 4)
    def _(q):
        @pl.when((q == 1) & (core == 1))
        def _():
            odd_line(2)

        @pl.when((q == 3) & (core == 0))
        def _():
            even_line(4)

        @pl.when((q == 3) & (core == 1))
        def _():
            odd_line(3)

        early(pl.ds(pl.multiple_of(q * (pre // 4), 128), pre // 4), pre // 4)

    early(pl.ds(pre, dec), dec)

    @on(1)
    def _():
        odd_line(4)

    @on(0)
    def _():
        twins_landed(2)

    @pl.loop(0, 2)
    def _(i):
        unit(2 - 4 * i, 1, 3 + i)

    twins_landed(3)

    @pl.loop(0, 3)
    def _(i):
        @pl.when(i == 2)
        def _():
            twins_landed(NZ // 2)

        full_line(jnp.where(i == 2, NZ // 2, 3 - 6 * i), i)

    loads[2].wait()

    here = pl.ds(pre, dec)
    cache = dc_ref[...].astype(F32)
    own = jnp.concatenate([cache, cache[:, DL:]], axis=1)
    own = jnp.concatenate([own] * heads, axis=0)
    own_score = jnp.sum(queries[here, :].astype(F32) * own, axis=1, keepdims=True)
    best = jnp.maximum(jnp.max(top[here, :], axis=1, keepdims=True), own_score)
    num, den = join(here, best)
    own_weight = jnp.exp2(own_score - best)
    lat = (num + own_weight * own[:, :DL]) / (den + own_weight)
    high = lat.astype(BF16).astype(F32)
    low = lat - high
    outs = []
    for h in range(heads):
        part = slice(h * rows, (h + 1) * rows)
        pieces = jnp.concatenate([high[part], low[part]], axis=0).astype(BF16)
        doubled = dot(pieces, vup[:, h * DV : (h + 1) * DV], 1, 0)
        outs.append(doubled[:rows] + doubled[rows:])
    wide = heads // 2 * DV
    halves = [jnp.concatenate(outs[: heads // 2], axis=1), jnp.concatenate(outs[heads // 2 :], axis=1)]
    xrows[x] = jnp.concatenate(halves, axis=0).astype(BF16)

    def x_rows(d):
        return pltpu.make_async_remote_copy(
            src_ref=xrows.at[x], dst_ref=xrows.at[x], send_sem=dec_send.at[0],
            recv_sem=dec_recv.at[0], device_id=x_peer(d), device_id_type=MESH,
        )

    def z_rows(d):
        return pltpu.make_async_remote_copy(
            src_ref=zsend.at[at_z(d)], dst_ref=zrecv.at[d - 1], send_sem=dec_send.at[1],
            recv_sem=dec_recv.at[1], device_id=z_peer(d), device_id_type=MESH,
        )

    def whole(src, dst, send_sem, recv_sem):
        return pltpu.make_async_remote_copy(
            src_ref=src, dst_ref=dst, send_sem=send_sem, recv_sem=recv_sem,
            device_id=sibling, device_id_type=MESH,
        )

    all_x = whole(xrows.at[pl.ds(0, NX - 1)], xrows.at[pl.ds(0, NX - 1)], dec_send.at[0], dec_recv.at[0])
    all_z = whole(zsend.at[pl.ds(0, NZ - 1)], zrecv, dec_send.at[1], dec_recv.at[1])

    for d in range(1, NX):
        x_rows(d).start()

    share = out_ref.shape[0]
    width = heads * DV

    def deliver(first, size, d):
        other = lax.rem(member + d, 8)
        return pltpu.make_async_remote_copy(
            src_ref=staged.at[pl.ds(pl.multiple_of(other * share, share), share), pl.ds(first, size)],
            dst_ref=out_ref.at[:, pl.ds(pl.multiple_of(member * width + first, 128), size)],
            send_sem=out_send.at[0], recv_sem=out_recv.at[0],
            device_id=group_peer(d), device_id_type=MESH,
        )

    all_out = whole(
        staged.at[pl.ds(0, 7 * share), :], out_ref.at[:, pl.ds(0, 7 * width)],
        out_send.at[0], out_recv.at[0],
    )

    def sort_rows():
        all_x.wait_recv()
        tall = 2 * rows
        to = lax.broadcasted_iota(jnp.int32, (NZ * tall, NX * tall), 0)
        fro = lax.broadcasted_iota(jnp.int32, (NZ * tall, NX * tall), 1)
        target = (x * NZ + to // tall) * rows + (to & (rows - 1))
        slot = jnp.full((NZ * tall, NX * tall), -1, jnp.int32)
        for j in range(NX):
            for i in range(rows):
                hit = (fro // tall == j) & ((fro & (rows - 1)) == i)
                slot = jnp.where(hit, slots[(j * NZ + z) * rows + i], slot)
        pick = (slot == target) & ((to & rows) == (fro & rows))
        pick = jnp.where(pick, 1.0, 0.0).astype(BF16)
        moved = dot(pick, xrows[...].reshape(NX * tall, wide), 1, 0).astype(BF16)
        zsend[...] = moved.reshape(NZ, tall, wide)
        for d in range(1, NZ):
            z_rows(d).start()

    pairs = heads // 2
    cuts = (0, 3, 6, 7, 8)

    @pl.loop(0, pairs)
    def _(pair):
        here = pl.ds(pl.multiple_of(pair * 2 * toks, 2 * toks), 2 * toks)
        num, den = join(here, jnp.max(top[here, :], axis=1, keepdims=True))
        lat = (num * (1.0 / den)).astype(BF16)
        for sub in range(2):
            cols = pl.ds(pl.multiple_of((pair * 2 + sub) * DV, DV), DV)
            part = dot(lat[sub * toks : (sub + 1) * toks], vup[:, cols], 1, 0)
            staged[:, cols] = part.astype(BF16)
        pl.when(pair == 2)(sort_rows)
        for begin, end in zip(cuts[:-1], cuts[1:]):

            @pl.when(pair == end - 1)
            def _(begin=begin, end=end):
                for d in range(1, 8):
                    deliver(begin * 2 * DV, (end - begin) * 2 * DV, d).start()

    ours = pl.ds(pl.multiple_of(member * width, width), width)
    out_ref[:, ours] = staged[pl.ds(pl.multiple_of(member * share, share), share), :]
    all_z.wait_recv()
    total = zsend[z].astype(F32)
    for d in range(1, NZ):
        total = total + zrecv[d - 1].astype(F32)
    dec_ref[...] = jnp.concatenate([total[:rows], total[rows:]], axis=1).astype(BF16)
    sent = 2 * NX * NZ * SPAN - SPAN

    whole(keys.at[pl.ds(0, sent), :], keys.at[pl.ds(0, sent), :], send.at[0], recv.at[0]).wait_send()
    all_x.wait_send()
    all_z.wait_send()
    all_out.wait_send()
    all_out.wait_recv()


def hand_on(a, b, to_a, to_b, sems):
    copies = [pltpu.make_async_copy(a, to_a, sems.at[0]), pltpu.make_async_copy(b, to_b, sems.at[1])]
    for one in copies:
        one.start()
    for one in copies:
        one.wait()


def per_device(
    prefill_query, prompt_cache, key_up, value_up, block_place, decode_query, decode_cache,
    row_length, row_slot,
):
    toks, width = prefill_query.shape
    heads = width // HD
    rows = decode_query.shape[0]
    count = NX * NZ * toks
    smem = pl.BlockSpec(memory_space=pltpu.SMEM)
    vmem = pl.BlockSpec(memory_space=pltpu.VMEM)
    hbm = pl.BlockSpec(memory_space=pl.ANY)
    total = heads * (toks + rows)
    wide = heads // 2 * DV
    moved = pl.pallas_call(
        kernel,
        out_shape=(
            jax.ShapeDtypeStruct((toks // 8, 8 * heads * DV), BF16),
            jax.ShapeDtypeStruct((rows, heads * DV), BF16),
        ),
        in_specs=[smem, smem, smem, vmem, vmem, vmem, hbm, hbm, hbm],
        out_specs=(vmem, vmem),
        scratch_shapes=[
            pltpu.VMEM((toks, width), BF16),
            pltpu.VMEM((count, WIDE), BF16),
            pltpu.VMEM(key_up.shape, BF16),
            pltpu.VMEM(value_up.shape, BF16),
            pltpu.VMEM((total, WIDE), BF16),
            pltpu.VMEM((total, 5 * 2 * LINE), F32),
            pltpu.VMEM((total, 128), F32),
            pltpu.VMEM((total, DL), F32),
            pltpu.VMEM((total, 128), F32),
            pltpu.VMEM((total, 128), F32),
            pltpu.VMEM((toks + heads * rows, 2 * LINE), F32),
            pltpu.VMEM((toks, heads * DV), BF16),
            pltpu.VMEM((NX, 2 * rows, wide), BF16),
            pltpu.VMEM((NZ, 2 * rows, wide), BF16),
            pltpu.VMEM((NZ - 1, 2 * rows, wide), BF16),
            pltpu.SemaphoreType.DMA((3,)),
            pltpu.SemaphoreType.DMA((1,)),
            pltpu.SemaphoreType.DMA((26,)),
            pltpu.SemaphoreType.DMA((1,)),
            pltpu.SemaphoreType.DMA((1,)),
            pltpu.SemaphoreType.DMA((2,)),
            pltpu.SemaphoreType.DMA((2,)),
        ],
        compiler_params=pltpu.CompilerParams(
            vmem_limit_bytes=60 << 20, collective_id=0, has_side_effects=True
        ),
    )(
        block_place, row_length, row_slot, prompt_cache.T, decode_query, decode_cache,
        prefill_query, key_up, value_up,
    )
    return pl.pallas_call(
        hand_on,
        out_shape=tuple(jax.ShapeDtypeStruct(one.shape, one.dtype) for one in moved),
        in_specs=[vmem, vmem],
        out_specs=(hbm, hbm),
        scratch_shapes=[pltpu.SemaphoreType.DMA((2,))],
    )(*moved)


def solution(mesh):
    return jax.shard_map(
        per_device,
        mesh=mesh,
        in_specs=(
            P("ctx", ("tp", "grp")),
            P("ctx", None),
            P(None, ("tp", "grp")),
            P(None, ("tp", "grp")),
            P(),
            P("ctx", ("tp", "grp")),
            P("ctx", None),
            P(),
            P(),
        ),
        out_specs=(P(("ctx", "tp", "grp"), None), P("ctx", ("tp", "grp"))),
        check_vma=False,
    )
```

```python
import functools
import math

import jax
import jax.numpy as jnp
from jax import lax
from jax.experimental import pallas as pl
from jax.experimental.pallas import tpu as pltpu
from jax.sharding import PartitionSpec as P

DL = 512
DR = 64
DN = 128
DV = 128
HD = DN + DR
WIDE = DL + 2 * DR
SPAN = 64
FACTOR = HD**-0.5 * math.log2(math.e)
MASKED = -1e30
NX, NZ = 4, 8
LINE = NX * SPAN
MESH = pl.DeviceIdType.MESH
F32 = jnp.float32
BF16 = jnp.bfloat16


def dot(a, b, ca, cb):
    return lax.dot_general(a, b, (((ca,), (cb,)), ((), ())), preferred_element_type=F32)


def kernel(
    place, length, slots, cache_ref, dq_ref, dc_ref, q_hbm, kup_hbm, vup_hbm, out_ref, dec_ref,
    q_ref, keys, kup, vup, queries, score, top, acc, part_den, base, bias,
    staged, xrows, zsend, zrecv,
    load_sem, send, recv, out_send, out_recv, dec_send, dec_recv,
):
    toks = q_ref.shape[0]
    rows = dq_ref.shape[0]
    heads = q_ref.shape[1] // HD
    count = keys.shape[0]
    pre = heads * toks
    dec = heads * rows
    ctx = lax.axis_index("ctx")
    tp = lax.axis_index("tp")
    grp = lax.axis_index("grp")
    x, z = ctx // NZ, lax.rem(ctx, NZ)
    core = lax.rem(tp, 2)
    member = tp * 2 + grp
    y = tp // 2 * 2 + grp

    def at_x(d):
        return lax.rem(x + d + NX, NX)

    def at_z(d):
        return lax.rem(z + d + NZ, NZ)

    def x_peer(d):
        return (at_x(d) * NZ + z, tp, grp)

    def z_peer(d):
        return (x * NZ + at_z(d), tp, grp)

    def group_peer(d):
        other = lax.rem(member + d, 8)
        return (ctx, other // 2, lax.rem(other, 2))

    def y_peer(d):
        other = lax.rem(y + d, 4)
        return (ctx, other // 2 * 2 + core, lax.rem(other, 2))

    sibling = (ctx, tp + 1 - 2 * core, grp)

    loads = [
        pltpu.make_async_copy(src, dst, load_sem.at[i])
        for i, (src, dst) in enumerate([(q_hbm, q_ref), (kup_hbm, kup), (vup_hbm, vup)])
    ]
    for load in loads:
        load.start()

    barrier = pltpu.get_barrier_semaphore()
    peers = [x_peer(d) for d in range(1, NX)] + [z_peer(d) for d in range(1, NZ)]
    peers += [group_peer(d) for d in range(1, 8)]
    for peer in peers:
        pl.semaphore_signal(barrier, inc=1, device_id=peer, device_id_type=MESH)

    def place_of(half, xx, zz):
        return (zz * 2 + half) * LINE + xx * SPAN

    turned = cache_ref[...].astype(F32).T
    mine = jnp.where(core == 0, turned[:SPAN], turned[SPAN:]).astype(BF16)

    here = pl.ds(pl.multiple_of(place_of(core, x, z), SPAN), SPAN)
    keys[here, : DL + DR] = mine
    keys[here, DL + DR :] = mine[:, DL:]
    pl.semaphore_wait(barrier, len(peers))

    def copy(first, size, sem, peer):
        part = keys.at[pl.ds(pl.multiple_of(first, SPAN), size), :]
        return pltpu.make_async_remote_copy(
            src_ref=part, dst_ref=part, send_sem=send.at[0], recv_sem=recv.at[sem],
            device_id=peer, device_id_type=MESH,
        )

    def landed(sem, size):
        copy(0, size, sem, sibling).wait_recv()

    def start(copies):
        for one in copies:
            one.start()

    def on(which):
        return pl.when(core == which)

    EVEN_Z, ODD_Z, TWIN, EVEN_X, ODD_Y, ODD_X = 0, 8, 16, 24, 32, 40
    far = NZ // 2

    def signs(k):
        return (k,) if k in (0, far) else (k, -k)

    def even_z(k):
        first = place_of(0, x, z)
        start([copy(first, SPAN, EVEN_Z + (-d) % NZ, z_peer(d)) for d in signs(k)])

    def odd_z(k):
        first = place_of(1, y, z)
        start([copy(first, SPAN, ODD_Z + (-d) % NZ, z_peer(d)) for d in signs(k)])

    def even_step(k):
        for dz in signs(k):
            if k:
                landed(EVEN_Z + dz % NZ, SPAN)
            first = place_of(0, x, at_z(dz))
            start([copy(first, SPAN, EVEN_X + dz % NZ, x_peer(d)) for d in (1, 3, 2)])

    def odd_step(k):
        for dz in signs(k):
            landed(ODD_Z + dz % NZ, SPAN)
            first = place_of(1, y, at_z(dz))
            start([copy(first, SPAN, ODD_Y + dz % NZ, y_peer(d)) for d in (1, 3, 2)])

    def twin(dz):
        return copy(place_of(core, 0, at_z(dz)), LINE, TWIN + dz % NZ, sibling)

    def even_line(dz):
        landed(EVEN_X + dz % NZ, 3 * SPAN)
        twin(dz).start()

    def odd_line(dz):
        landed(ODD_Y + dz % NZ if dz else ODD_X, 3 * SPAN)
        twin(dz).start()

    def twin_landed(dz):
        landed(TWIN + dz % NZ, LINE)

    @on(0)
    def _():
        even_z(1)

    @on(1)
    def _():
        start([copy(place_of(1, x, z), SPAN, ODD_X, x_peer(d)) for d in (1, 3, 2)])

    @pl.when((core == 1) & (x == y))
    def _():
        odd_z(1)

    loads[0].wait()
    loads[1].wait()

    def absorb(pair):
        at = pl.ds(pl.multiple_of(pair * 2 * HD, 2 * HD), 2 * HD)
        both = q_ref[:, at].astype(F32)
        dboth = dq_ref[:, at].astype(F32)
        kept = []
        for sub in range(2):
            h = pair * 2 + sub
            every = jnp.concatenate([both, dboth, dboth], axis=0)[:, sub * HD : (sub + 1) * HD]
            block = kup[:, pl.ds(pl.multiple_of(h * DN, DN), DN)]
            absorbed = (dot(every[:, :DN].astype(BF16), block, 1, 1) * FACTOR).astype(BF16)
            rope = every[:, DN:] * FACTOR
            high = rope.astype(BF16).astype(F32)
            rope = jnp.concatenate([high, rope - high], axis=1).astype(BF16)
            here = pl.ds(pl.multiple_of(h * toks, toks), toks)
            queries[here, :DL] = absorbed[:toks]
            queries[here, DL:] = rope[:toks]
            kept.append((absorbed[toks:].astype(F32)[:rows], rope[toks:].astype(F32)[:rows]))
        here = pl.ds(pl.multiple_of(pre + pair * 2 * rows, 2 * rows), 2 * rows)
        queries[here, :DL] = jnp.concatenate([kept[0][0], kept[1][0]], axis=0).astype(BF16)
        queries[here, DL:] = jnp.concatenate([kept[0][1], kept[1][1]], axis=0).astype(BF16)

    lane = lax.broadcasted_iota(jnp.int32, (1, 128), 1)
    tok = lax.broadcasted_iota(jnp.int32, (toks, 1), 0)
    my_pos = jnp.where(tok < SPAN, place[2 * ctx], place[2 * ctx + 1]) * SPAN + (tok & (SPAN - 1))
    row = lax.broadcasted_iota(jnp.int32, (rows, 1), 0)
    limit = jnp.zeros((rows, 1), jnp.int32)
    for r in range(rows):
        limit = jnp.where(row == r, length[ctx * rows + r], limit)

    def scores(first, size, blocks, column):
        for j in range(size // 128):
            a, b = place[blocks[2 * j]], place[blocks[2 * j + 1]]
            pos = jnp.where(lane < SPAN, a, b) * SPAN + (lane & (SPAN - 1))
            cols = slice(j * 128, (j + 1) * 128)
            bias[:toks, cols] = jnp.where(pos <= my_pos, 0.0, MASKED)
            part = jnp.where(pos < limit, 0.0, MASKED)
            bias[toks:, cols] = jnp.concatenate([part] * (dec // rows), axis=0)
        from_keys = pl.ds(pl.multiple_of(first, 256), size)
        cols = pl.ds(pl.multiple_of(column, 256), size)
        half = pre // 2
        for begin, tall, extra in ((0, half, 0), (half, half, dec)):
            here = pl.ds(begin, tall + extra)
            add = [bias[:toks, :size]] * (tall // toks)
            if extra:
                add = add + [bias[toks:, :size]]
            s = dot(queries[here, :], keys[from_keys, :], 1, 1) + jnp.concatenate(add, axis=0)
            score[here, cols] = s
            best = top[here, :]
            for j in range(size // 128):
                best = jnp.maximum(best, s[:, j * 128 : (j + 1) * 128])
            top[here, :] = best

    def unit(dz, half, line):
        zz = at_z(dz)
        blocks = [2 * (j * NZ + zz) + half for j in range(NX)]
        scores(place_of(half, 0, zz), LINE, blocks, (line * 2 + half) * LINE)

    def full_line(dz, line):
        zz = at_z(dz)
        blocks = [2 * (j * NZ + zz) + half for half in (0, 1) for j in range(NX)]
        scores(place_of(0, 0, zz), 2 * LINE, blocks, line * 2 * LINE)

    def weigh(here, best, lines):
        den = jnp.zeros((best.shape[0], 128), F32)
        num = None
        for i, dz in enumerate(lines):
            e = jnp.exp2(score[here, i * 2 * LINE : (i + 1) * 2 * LINE] - best)
            for j in range(2 * LINE // 128):
                den = den + e[:, j * 128 : (j + 1) * 128]
            values = keys[pl.ds(pl.multiple_of(place_of(0, 0, at_z(dz)), 2 * LINE), 2 * LINE), :DL]
            part = dot(e.astype(BF16), values, 1, 0)
            num = part if num is None else num + part
        return num, den

    near, rest = (0, 1, -1), (3, -3, 4, 2, -2)

    def early(here, size):
        best = jnp.max(top[here, :], axis=1, keepdims=True)
        acc[here, :], part_den[here, :] = weigh(here, best, near)
        base[here, :] = jnp.broadcast_to(best, (size, 128))

    def join(here, best):
        num, den = weigh(here, best, rest)
        factor = jnp.exp2(base[here, :] - best)
        den = jnp.sum(den + part_den[here, :] * factor, axis=1, keepdims=True)
        return num + acc[here, :] * jnp.concatenate([factor] * (DL // 128), axis=1), den

    pl.loop(0, 2)(absorb)

    @on(0)
    def _():
        even_step(0)
        even_z(2)

    pl.loop(2, 4)(absorb)

    @on(0)
    def _():
        even_z(3)

    pl.loop(4, 6)(absorb)

    @on(0)
    def _():
        even_step(1)
        even_z(4)

    @on(1)
    def _():
        odd_line(0)

    @pl.when((core == 1) & (x != y))
    def _():
        odd_z(1)

    @on(1)
    def _():
        odd_z(2)

    pl.loop(6, heads // 2)(absorb)
    top[...] = jnp.full_like(top, MASKED)

    @on(0)
    def _():
        even_line(0)

    @on(1)
    def _():
        odd_z(3)

    @pl.loop(0, 2)
    def _(i):
        @pl.when((i == 1) & (core == 0))
        def _():
            even_step(2)

        @pl.when((i == 1) & (core == 1))
        def _():
            odd_z(4)

        @pl.when(i == 1)
        def _():
            twin_landed(0)

        unit(0, jnp.where(i == 0, core, 1 - core), 0)

    @on(0)
    def _():
        even_step(3)
        even_line(1)
        even_step(4)

    @on(1)
    def _():
        odd_step(1)
        odd_step(2)
        twin_landed(1)

    @pl.loop(0, 6)
    def _(i):
        def at(turn, which):
            return pl.when((i == turn) & (core == which))

        @at(1, 0)
        def _():
            even_line(-1)

        @at(1, 1)
        def _():
            twin_landed(-1)

        @at(2, 0)
        def _():
            even_line(2)

        @at(2, 1)
        def _():
            odd_line(1)
            odd_step(3)

        @at(3, 0)
        def _():
            even_line(-2)

        @at(3, 1)
        def _():
            odd_line(-1)
            odd_step(4)

        @at(4, 0)
        def _():
            twin_landed(1)

        @at(4, 1)
        def _():
            twin_landed(2)

        @at(5, 0)
        def _():
            twin_landed(-1)

        @at(5, 1)
        def _():
            twin_landed(-2)

        flip = lax.rem(i, 2)
        second = i // 2 == 2 - (1 - core)
        half = jnp.where((i < 2) | second, 0, 1)
        dz = jnp.where(second, 2, 1)
        unit(jnp.where(flip == 0, dz, -dz), half, jnp.where(second, 3, 1) + flip)

    @pl.loop(0, 4)
    def _(q):
        @pl.when((q == 1) & (core == 0))
        def _():
            even_line(3)
            even_line(-3)

        @pl.when((q == 1) & (core == 1))
        def _():
            odd_line(2)
            odd_line(-2)

        @pl.when((q == 3) & (core == 0))
        def _():
            even_line(far)

        @pl.when((q == 3) & (core == 1))
        def _():
            odd_line(3)
            odd_line(-3)

        early(pl.ds(pl.multiple_of(q * (pre // 4), 128), pre // 4), pre // 4)

    early(pl.ds(pre, dec), dec)

    @on(1)
    def _():
        odd_line(far)

    @on(0)
    def _():
        twin_landed(2)
        twin_landed(-2)

    @pl.loop(0, 2)
    def _(i):
        unit(2 - 4 * i, 1, 3 + i)

    twin_landed(3)
    twin_landed(-3)

    @pl.loop(0, 3)
    def _(i):
        @pl.when(i == 2)
        def _():
            twin_landed(far)

        full_line(jnp.where(i == 2, NZ // 2, 3 - 6 * i), i)

    loads[2].wait()

    here = pl.ds(pre, dec)
    cache = dc_ref[...].astype(F32)
    own = jnp.concatenate([cache, cache[:, DL:]], axis=1)
    own = jnp.concatenate([own] * heads, axis=0)
    own_score = jnp.sum(queries[here, :].astype(F32) * own, axis=1, keepdims=True)
    best = jnp.maximum(jnp.max(top[here, :], axis=1, keepdims=True), own_score)
    num, den = join(here, best)
    own_weight = jnp.exp2(own_score - best)
    lat = (num + own_weight * own[:, :DL]) / (den + own_weight)
    high = lat.astype(BF16).astype(F32)
    low = lat - high
    outs = []
    for h in range(heads):
        part = slice(h * rows, (h + 1) * rows)
        pieces = jnp.concatenate([high[part], low[part]], axis=0).astype(BF16)
        doubled = dot(pieces, vup[:, h * DV : (h + 1) * DV], 1, 0)
        outs.append(doubled[:rows] + doubled[rows:])
    wide = heads // 2 * DV
    halves = [jnp.concatenate(outs[: heads // 2], axis=1), jnp.concatenate(outs[heads // 2 :], axis=1)]
    xrows[x] = jnp.concatenate(halves, axis=0).astype(BF16)

    def x_rows(d):
        return pltpu.make_async_remote_copy(
            src_ref=xrows.at[x], dst_ref=xrows.at[x], send_sem=dec_send.at[0],
            recv_sem=dec_recv.at[0], device_id=x_peer(d), device_id_type=MESH,
        )

    def z_rows(d):
        return pltpu.make_async_remote_copy(
            src_ref=zsend.at[at_z(d)], dst_ref=zrecv.at[d - 1], send_sem=dec_send.at[1],
            recv_sem=dec_recv.at[1], device_id=z_peer(d), device_id_type=MESH,
        )

    def whole(src, dst, send_sem, recv_sem):
        return pltpu.make_async_remote_copy(
            src_ref=src, dst_ref=dst, send_sem=send_sem, recv_sem=recv_sem,
            device_id=sibling, device_id_type=MESH,
        )

    all_x = whole(xrows.at[pl.ds(0, NX - 1)], xrows.at[pl.ds(0, NX - 1)], dec_send.at[0], dec_recv.at[0])
    all_z = whole(zsend.at[pl.ds(0, NZ - 1)], zrecv, dec_send.at[1], dec_recv.at[1])

    for d in range(1, NX):
        x_rows(d).start()

    share = out_ref.shape[0]
    width = heads * DV

    def deliver(first, size, d):
        other = lax.rem(member + d, 8)
        return pltpu.make_async_remote_copy(
            src_ref=staged.at[pl.ds(pl.multiple_of(other * share, share), share), pl.ds(first, size)],
            dst_ref=out_ref.at[:, pl.ds(pl.multiple_of(member * width + first, 128), size)],
            send_sem=out_send.at[0], recv_sem=out_recv.at[0],
            device_id=group_peer(d), device_id_type=MESH,
        )

    all_out = whole(
        staged.at[pl.ds(0, 7 * share), :], out_ref.at[:, pl.ds(0, 7 * width)],
        out_send.at[0], out_recv.at[0],
    )

    def sort_rows():
        all_x.wait_recv()
        tall = 2 * rows
        to = lax.broadcasted_iota(jnp.int32, (NZ * tall, NX * tall), 0)
        fro = lax.broadcasted_iota(jnp.int32, (NZ * tall, NX * tall), 1)
        target = (x * NZ + to // tall) * rows + (to & (rows - 1))
        slot = jnp.full((NZ * tall, NX * tall), -1, jnp.int32)
        for j in range(NX):
            for i in range(rows):
                hit = (fro // tall == j) & ((fro & (rows - 1)) == i)
                slot = jnp.where(hit, slots[(j * NZ + z) * rows + i], slot)
        pick = (slot == target) & ((to & rows) == (fro & rows))
        pick = jnp.where(pick, 1.0, 0.0).astype(BF16)
        moved = dot(pick, xrows[...].reshape(NX * tall, wide), 1, 0).astype(BF16)
        zsend[...] = moved.reshape(NZ, tall, wide)
        for d in range(1, NZ):
            z_rows(d).start()

    pairs = heads // 2
    cuts = (0, 3, 6, 7, 8)

    @pl.loop(0, pairs)
    def _(pair):
        here = pl.ds(pl.multiple_of(pair * 2 * toks, 2 * toks), 2 * toks)
        num, den = join(here, jnp.max(top[here, :], axis=1, keepdims=True))
        lat = (num * (1.0 / den)).astype(BF16)
        for sub in range(2):
            cols = pl.ds(pl.multiple_of((pair * 2 + sub) * DV, DV), DV)
            part = dot(lat[sub * toks : (sub + 1) * toks], vup[:, cols], 1, 0)
            staged[:, cols] = part.astype(BF16)
        pl.when(pair == 2)(sort_rows)
        for begin, end in zip(cuts[:-1], cuts[1:]):

            @pl.when(pair == end - 1)
            def _(begin=begin, end=end):
                for d in range(1, 8):
                    deliver(begin * 2 * DV, (end - begin) * 2 * DV, d).start()

    ours = pl.ds(pl.multiple_of(member * width, width), width)
    out_ref[:, ours] = staged[pl.ds(pl.multiple_of(member * share, share), share), :]
    all_z.wait_recv()
    total = zsend[z].astype(F32)
    for d in range(1, NZ):
        total = total + zrecv[d - 1].astype(F32)
    dec_ref[...] = jnp.concatenate([total[:rows], total[rows:]], axis=1).astype(BF16)
    sent = 2 * NX * NZ * SPAN - SPAN

    whole(keys.at[pl.ds(0, sent), :], keys.at[pl.ds(0, sent), :], send.at[0], recv.at[0]).wait_send()
    all_x.wait_send()
    all_z.wait_send()
    all_out.wait_send()
    all_out.wait_recv()


def hand_on(a, b, to_a, to_b, sems):
    copies = [pltpu.make_async_copy(a, to_a, sems.at[0]), pltpu.make_async_copy(b, to_b, sems.at[1])]
    for one in copies:
        one.start()
    for one in copies:
        one.wait()


def per_device(
    prefill_query, prompt_cache, key_up, value_up, block_place, decode_query, decode_cache,
    row_length, row_slot,
):
    toks, width = prefill_query.shape
    heads = width // HD
    rows = decode_query.shape[0]
    count = NX * NZ * toks
    smem = pl.BlockSpec(memory_space=pltpu.SMEM)
    vmem = pl.BlockSpec(memory_space=pltpu.VMEM)
    hbm = pl.BlockSpec(memory_space=pl.ANY)
    total = heads * (toks + rows)
    wide = heads // 2 * DV
    moved = pl.pallas_call(
        kernel,
        out_shape=(
            jax.ShapeDtypeStruct((toks // 8, 8 * heads * DV), BF16),
            jax.ShapeDtypeStruct((rows, heads * DV), BF16),
        ),
        in_specs=[smem, smem, smem, vmem, vmem, vmem, hbm, hbm, hbm],
        out_specs=(vmem, vmem),
        scratch_shapes=[
            pltpu.VMEM((toks, width), BF16),
            pltpu.VMEM((count, WIDE), BF16),
            pltpu.VMEM(key_up.shape, BF16),
            pltpu.VMEM(value_up.shape, BF16),
            pltpu.VMEM((total, WIDE), BF16),
            pltpu.VMEM((total, 5 * 2 * LINE), F32),
            pltpu.VMEM((total, 128), F32),
            pltpu.VMEM((total, DL), F32),
            pltpu.VMEM((total, 128), F32),
            pltpu.VMEM((total, 128), F32),
            pltpu.VMEM((toks + heads * rows, 2 * LINE), F32),
            pltpu.VMEM((toks, heads * DV), BF16),
            pltpu.VMEM((NX, 2 * rows, wide), BF16),
            pltpu.VMEM((NZ, 2 * rows, wide), BF16),
            pltpu.VMEM((NZ - 1, 2 * rows, wide), BF16),
            pltpu.SemaphoreType.DMA((3,)),
            pltpu.SemaphoreType.DMA((1,)),
            pltpu.SemaphoreType.DMA((41,)),
            pltpu.SemaphoreType.DMA((1,)),
            pltpu.SemaphoreType.DMA((1,)),
            pltpu.SemaphoreType.DMA((2,)),
            pltpu.SemaphoreType.DMA((2,)),
        ],
        compiler_params=pltpu.CompilerParams(
            vmem_limit_bytes=60 << 20, collective_id=0, has_side_effects=True
        ),
    )(
        block_place, row_length, row_slot, prompt_cache.T, decode_query, decode_cache,
        prefill_query, key_up, value_up,
    )
    return pl.pallas_call(
        hand_on,
        out_shape=tuple(jax.ShapeDtypeStruct(one.shape, one.dtype) for one in moved),
        in_specs=[vmem, vmem],
        out_specs=(hbm, hbm),
        scratch_shapes=[pltpu.SemaphoreType.DMA((2,))],
    )(*moved)


def solution(mesh):
    return jax.shard_map(
        per_device,
        mesh=mesh,
        in_specs=(
            P("ctx", ("tp", "grp")),
            P("ctx", None),
            P(None, ("tp", "grp")),
            P(None, ("tp", "grp")),
            P(),
            P("ctx", ("tp", "grp")),
            P("ctx", None),
            P(),
            P(),
        ),
        out_specs=(P(("ctx", "tp", "grp"), None), P("ctx", ("tp", "grp"))),
        check_vma=False,
    )
```

```python
import functools
import math

import jax
import jax.numpy as jnp
from jax import lax
from jax.experimental import pallas as pl
from jax.experimental.pallas import tpu as pltpu
from jax.sharding import PartitionSpec as P

DL = 512
DR = 64
DN = 128
DV = 128
HD = DN + DR
WIDE = DL + 2 * DR
SPAN = 64
FACTOR = HD**-0.5 * math.log2(math.e)
MASKED = -1e30
NX, NZ = 4, 8
LINE = NX * SPAN
MESH = pl.DeviceIdType.MESH
F32 = jnp.float32
BF16 = jnp.bfloat16


def dot(a, b, ca, cb):
    return lax.dot_general(a, b, (((ca,), (cb,)), ((), ())), preferred_element_type=F32)


def kernel(
    place, length, slots, cache_ref, dq_ref, dc_ref, q_hbm, kup_hbm, vup_hbm, out_ref, dec_ref,
    q_ref, keys, kup, vup, queries, score, top, acc, part_den, base, bias,
    staged, xrows, zsend, zrecv,
    load_sem, send, recv, out_send, out_recv, dec_send, dec_recv,
):
    toks = q_ref.shape[0]
    rows = dq_ref.shape[0]
    heads = q_ref.shape[1] // HD
    count = keys.shape[0]
    pre = heads * toks
    dec = heads * rows
    ctx = lax.axis_index("ctx")
    tp = lax.axis_index("tp")
    grp = lax.axis_index("grp")
    x, z = ctx // NZ, lax.rem(ctx, NZ)
    core = lax.rem(tp, 2)
    member = tp * 2 + grp
    y = tp // 2 * 2 + grp

    def at_x(d):
        return lax.rem(x + d + NX, NX)

    def at_z(d):
        return lax.rem(z + d + NZ, NZ)

    def x_peer(d):
        return (at_x(d) * NZ + z, tp, grp)

    def z_peer(d):
        return (x * NZ + at_z(d), tp, grp)

    def group_peer(d):
        other = lax.rem(member + d, 8)
        return (ctx, other // 2, lax.rem(other, 2))

    def y_peer(d):
        other = lax.rem(y + d, 4)
        return (ctx, other // 2 * 2 + core, lax.rem(other, 2))

    sibling = (ctx, tp + 1 - 2 * core, grp)

    loads = [
        pltpu.make_async_copy(src, dst, load_sem.at[i])
        for i, (src, dst) in enumerate([(q_hbm, q_ref), (kup_hbm, kup), (vup_hbm, vup)])
    ]
    for load in loads:
        load.start()

    barrier = pltpu.get_barrier_semaphore()
    peers = [x_peer(d) for d in range(1, NX)] + [z_peer(d) for d in range(1, NZ)]
    peers += [group_peer(d) for d in range(1, 8)]
    for peer in peers:
        pl.semaphore_signal(barrier, inc=1, device_id=peer, device_id_type=MESH)

    def place_of(half, xx, zz):
        return (zz * 2 + half) * LINE + xx * SPAN

    turned = cache_ref[...].astype(F32).T
    mine = jnp.where(core == 0, turned[:SPAN], turned[SPAN:]).astype(BF16)

    here = pl.ds(pl.multiple_of(place_of(core, x, z), SPAN), SPAN)
    keys[here, : DL + DR] = mine
    keys[here, DL + DR :] = mine[:, DL:]
    pl.semaphore_wait(barrier, len(peers))

    def copy(first, size, sem, peer):
        part = keys.at[pl.ds(pl.multiple_of(first, SPAN), size), :]
        return pltpu.make_async_remote_copy(
            src_ref=part, dst_ref=part, send_sem=send.at[0], recv_sem=recv.at[sem],
            device_id=peer, device_id_type=MESH,
        )

    def landed(sem, size):
        copy(0, size, sem, sibling).wait_recv()

    def start(copies):
        for one in copies:
            one.start()

    def on(which):
        return pl.when(core == which)

    EVEN_Z, ODD_Z, TWIN, EVEN_X, ODD_Y, ODD_X = 0, 8, 16, 24, 32, 40
    far = NZ // 2

    def signs(k):
        return (k,) if k in (0, far) else (k, -k)

    def even_z(k):
        first = place_of(0, x, z)
        start([copy(first, SPAN, EVEN_Z + (-d) % NZ, z_peer(d)) for d in signs(k)])

    def odd_z(k):
        first = place_of(1, y, z)
        start([copy(first, SPAN, ODD_Z + (-d) % NZ, z_peer(d)) for d in signs(k)])

    def even_step(k):
        for dz in signs(k):
            if k:
                landed(EVEN_Z + dz % NZ, SPAN)
            first = place_of(0, x, at_z(dz))
            start([copy(first, SPAN, EVEN_X + dz % NZ, x_peer(d)) for d in (1, 3, 2)])

    def odd_step(k):
        for dz in signs(k):
            landed(ODD_Z + dz % NZ, SPAN)
            first = place_of(1, y, at_z(dz))
            start([copy(first, SPAN, ODD_Y + dz % NZ, y_peer(d)) for d in (1, 3, 2)])

    def twin(dz):
        return copy(place_of(core, 0, at_z(dz)), LINE, TWIN + dz % NZ, sibling)

    def even_line(dz):
        landed(EVEN_X + dz % NZ, 3 * SPAN)
        twin(dz).start()

    def odd_line(dz):
        landed(ODD_Y + dz % NZ if dz else ODD_X, 3 * SPAN)
        twin(dz).start()

    def twin_landed(dz):
        landed(TWIN + dz % NZ, LINE)

    @on(0)
    def _():
        even_z(1)

    @on(1)
    def _():
        start([copy(place_of(1, x, z), SPAN, ODD_X, x_peer(d)) for d in (1, 3, 2)])

    @pl.when((core == 1) & (x == y))
    def _():
        odd_z(1)

    loads[0].wait()
    loads[1].wait()

    def absorb(pair):
        at = pl.ds(pl.multiple_of(pair * 2 * HD, 2 * HD), 2 * HD)
        both = q_ref[:, at].astype(F32)
        dboth = dq_ref[:, at].astype(F32)
        kept = []
        for sub in range(2):
            h = pair * 2 + sub
            every = jnp.concatenate([both, dboth, dboth], axis=0)[:, sub * HD : (sub + 1) * HD]
            block = kup[:, pl.ds(pl.multiple_of(h * DN, DN), DN)]
            absorbed = (dot(every[:, :DN].astype(BF16), block, 1, 1) * FACTOR).astype(BF16)
            rope = every[:, DN:] * FACTOR
            high = rope.astype(BF16).astype(F32)
            rope = jnp.concatenate([high, rope - high], axis=1).astype(BF16)
            here = pl.ds(pl.multiple_of(h * toks, toks), toks)
            queries[here, :DL] = absorbed[:toks]
            queries[here, DL:] = rope[:toks]
            kept.append((absorbed[toks:].astype(F32)[:rows], rope[toks:].astype(F32)[:rows]))
        here = pl.ds(pl.multiple_of(pre + pair * 2 * rows, 2 * rows), 2 * rows)
        queries[here, :DL] = jnp.concatenate([kept[0][0], kept[1][0]], axis=0).astype(BF16)
        queries[here, DL:] = jnp.concatenate([kept[0][1], kept[1][1]], axis=0).astype(BF16)

    lane = lax.broadcasted_iota(jnp.int32, (1, 128), 1)
    tok = lax.broadcasted_iota(jnp.int32, (toks, 1), 0)
    my_pos = jnp.where(tok < SPAN, place[2 * ctx], place[2 * ctx + 1]) * SPAN + (tok & (SPAN - 1))
    row = lax.broadcasted_iota(jnp.int32, (rows, 1), 0)
    limit = jnp.zeros((rows, 1), jnp.int32)
    for r in range(rows):
        limit = jnp.where(row == r, length[ctx * rows + r], limit)

    def scores(first, size, blocks, column):
        for j in range(size // 128):
            a, b = place[blocks[2 * j]], place[blocks[2 * j + 1]]
            pos = jnp.where(lane < SPAN, a, b) * SPAN + (lane & (SPAN - 1))
            cols = slice(j * 128, (j + 1) * 128)
            bias[:toks, cols] = jnp.where(pos <= my_pos, 0.0, MASKED)
            part = jnp.where(pos < limit, 0.0, MASKED)
            bias[toks:, cols] = jnp.concatenate([part] * (dec // rows), axis=0)
        from_keys = pl.ds(pl.multiple_of(first, 256), size)
        cols = pl.ds(pl.multiple_of(column, 256), size)
        half = pre // 2
        for begin, tall, extra in ((0, half, 0), (half, half, dec)):
            here = pl.ds(begin, tall + extra)
            add = [bias[:toks, :size]] * (tall // toks)
            if extra:
                add = add + [bias[toks:, :size]]
            s = dot(queries[here, :], keys[from_keys, :], 1, 1) + jnp.concatenate(add, axis=0)
            score[here, cols] = s
            best = top[here, :]
            for j in range(size // 128):
                best = jnp.maximum(best, s[:, j * 128 : (j + 1) * 128])
            top[here, :] = best

    def unit(dz, half, line):
        zz = at_z(dz)
        blocks = [2 * (j * NZ + zz) + half for j in range(NX)]
        scores(place_of(half, 0, zz), LINE, blocks, (line * 2 + half) * LINE)

    def full_line(dz, line):
        zz = at_z(dz)
        blocks = [2 * (j * NZ + zz) + half for half in (0, 1) for j in range(NX)]
        scores(place_of(0, 0, zz), 2 * LINE, blocks, line * 2 * LINE)

    def weigh(here, best, lines):
        den = jnp.zeros((best.shape[0], 128), F32)
        num = None
        for i, dz in enumerate(lines):
            e = jnp.exp2(score[here, i * 2 * LINE : (i + 1) * 2 * LINE] - best)
            for j in range(2 * LINE // 128):
                den = den + e[:, j * 128 : (j + 1) * 128]
            values = keys[pl.ds(pl.multiple_of(place_of(0, 0, at_z(dz)), 2 * LINE), 2 * LINE), :DL]
            part = dot(e.astype(BF16), values, 1, 0)
            num = part if num is None else num + part
        return num, den

    near, rest = (0, 1, -1), (3, -3, 4, 2, -2)

    def early(here, size):
        best = jnp.max(top[here, :], axis=1, keepdims=True)
        acc[here, :], part_den[here, :] = weigh(here, best, near)
        base[here, :] = jnp.broadcast_to(best, (size, 128))

    def join(here, best):
        num, den = weigh(here, best, rest)
        factor = jnp.exp2(base[here, :] - best)
        den = jnp.sum(den + part_den[here, :] * factor, axis=1, keepdims=True)
        return num + acc[here, :] * jnp.concatenate([factor] * (DL // 128), axis=1), den

    pl.loop(0, 2)(absorb)

    @on(0)
    def _():
        even_step(0)
        even_z(2)

    pl.loop(2, 4)(absorb)

    @on(0)
    def _():
        even_z(3)

    pl.loop(4, 6)(absorb)

    @on(0)
    def _():
        even_step(1)
        even_z(4)

    @on(1)
    def _():
        odd_line(0)

    @pl.when((core == 1) & (x != y))
    def _():
        odd_z(1)

    @on(1)
    def _():
        odd_z(2)

    pl.loop(6, heads // 2)(absorb)
    top[...] = jnp.full_like(top, MASKED)

    @on(0)
    def _():
        even_line(0)

    @on(1)
    def _():
        odd_z(3)

    @pl.loop(0, 2)
    def _(i):
        @pl.when((i == 1) & (core == 0))
        def _():
            even_step(2)

        @pl.when((i == 1) & (core == 1))
        def _():
            odd_z(4)

        @pl.when(i == 1)
        def _():
            twin_landed(0)

        unit(0, jnp.where(i == 0, core, 1 - core), 0)

    @on(0)
    def _():
        even_step(3)
        even_line(1)
        even_step(4)

    @on(1)
    def _():
        odd_step(1)
        odd_step(2)
        twin_landed(1)

    @pl.loop(0, 6)
    def _(i):
        def at(turn, which):
            return pl.when((i == turn) & (core == which))

        @at(1, 0)
        def _():
            even_line(-1)

        @at(1, 1)
        def _():
            twin_landed(-1)

        @at(2, 0)
        def _():
            even_line(2)

        @at(2, 1)
        def _():
            odd_line(1)
            odd_step(3)

        @at(3, 0)
        def _():
            even_line(-2)

        @at(3, 1)
        def _():
            odd_line(-1)
            odd_step(4)

        @at(4, 0)
        def _():
            twin_landed(1)

        @at(4, 1)
        def _():
            twin_landed(2)

        @at(5, 0)
        def _():
            twin_landed(-1)

        @at(5, 1)
        def _():
            twin_landed(-2)

        flip = lax.rem(i, 2)
        second = i // 2 == 2 - (1 - core)
        half = jnp.where((i < 2) | second, 0, 1)
        dz = jnp.where(second, 2, 1)
        unit(jnp.where(flip == 0, dz, -dz), half, jnp.where(second, 3, 1) + flip)

    @pl.loop(0, 4)
    def _(q):
        @pl.when((q == 1) & (core == 0))
        def _():
            even_line(3)
            even_line(-3)

        @pl.when((q == 1) & (core == 1))
        def _():
            odd_line(2)
            odd_line(-2)

        @pl.when((q == 3) & (core == 0))
        def _():
            even_line(far)

        @pl.when((q == 3) & (core == 1))
        def _():
            odd_line(3)
            odd_line(-3)

        early(pl.ds(pl.multiple_of(q * (pre // 4), 128), pre // 4), pre // 4)

    early(pl.ds(pre, dec), dec)

    @on(1)
    def _():
        odd_line(far)

    @on(0)
    def _():
        twin_landed(2)
        twin_landed(-2)

    @pl.loop(0, 2)
    def _(i):
        unit(2 - 4 * i, 1, 3 + i)

    twin_landed(3)
    twin_landed(-3)

    @pl.loop(0, 3)
    def _(i):
        @pl.when(i == 2)
        def _():
            twin_landed(far)

        full_line(jnp.where(i == 2, NZ // 2, 3 - 6 * i), i)

    loads[2].wait()

    here = pl.ds(pre, dec)
    cache = dc_ref[...].astype(F32)
    own = jnp.concatenate([cache, cache[:, DL:]], axis=1)
    own = jnp.concatenate([own] * heads, axis=0)
    own_score = jnp.sum(queries[here, :].astype(F32) * own, axis=1, keepdims=True)
    best = jnp.maximum(jnp.max(top[here, :], axis=1, keepdims=True), own_score)
    num, den = join(here, best)
    own_weight = jnp.exp2(own_score - best)
    lat = (num + own_weight * own[:, :DL]) / (den + own_weight)
    high = lat.astype(BF16).astype(F32)
    low = lat - high
    outs = []
    for h in range(heads):
        part = slice(h * rows, (h + 1) * rows)
        pieces = jnp.concatenate([high[part], low[part]], axis=0).astype(BF16)
        doubled = dot(pieces, vup[:, h * DV : (h + 1) * DV], 1, 0)
        outs.append(doubled[:rows] + doubled[rows:])
    wide = heads // 2 * DV
    halves = [jnp.concatenate(outs[: heads // 2], axis=1), jnp.concatenate(outs[heads // 2 :], axis=1)]
    xrows[x] = jnp.concatenate(halves, axis=0).astype(BF16)

    def x_rows(d):
        return pltpu.make_async_remote_copy(
            src_ref=xrows.at[x], dst_ref=xrows.at[x], send_sem=dec_send.at[0],
            recv_sem=dec_recv.at[0], device_id=x_peer(d), device_id_type=MESH,
        )

    def z_rows(d):
        return pltpu.make_async_remote_copy(
            src_ref=zsend.at[at_z(d)], dst_ref=zrecv.at[d - 1], send_sem=dec_send.at[1],
            recv_sem=dec_recv.at[1], device_id=z_peer(d), device_id_type=MESH,
        )

    def whole(src, dst, send_sem, recv_sem):
        return pltpu.make_async_remote_copy(
            src_ref=src, dst_ref=dst, send_sem=send_sem, recv_sem=recv_sem,
            device_id=sibling, device_id_type=MESH,
        )

    all_x = whole(xrows.at[pl.ds(0, NX - 1)], xrows.at[pl.ds(0, NX - 1)], dec_send.at[0], dec_recv.at[0])
    all_z = whole(zsend.at[pl.ds(0, NZ - 1)], zrecv, dec_send.at[1], dec_recv.at[1])

    for d in range(1, NX):
        x_rows(d).start()

    share = out_ref.shape[0]
    width = heads * DV

    def deliver(first, size, d):
        other = lax.rem(member + d, 8)
        return pltpu.make_async_remote_copy(
            src_ref=staged.at[pl.ds(pl.multiple_of(other * share, share), share), pl.ds(first, size)],
            dst_ref=out_ref.at[:, pl.ds(pl.multiple_of(member * width + first, 128), size)],
            send_sem=out_send.at[0], recv_sem=out_recv.at[0],
            device_id=group_peer(d), device_id_type=MESH,
        )

    all_out = whole(
        staged.at[pl.ds(0, 7 * share), :], out_ref.at[:, pl.ds(0, 7 * width)],
        out_send.at[0], out_recv.at[0],
    )

    def sort_rows():
        all_x.wait_recv()
        tall = 2 * rows
        to = lax.broadcasted_iota(jnp.int32, (NZ * tall, NX * tall), 0)
        fro = lax.broadcasted_iota(jnp.int32, (NZ * tall, NX * tall), 1)
        target = (x * NZ + to // tall) * rows + (to & (rows - 1))
        slot = jnp.full((NZ * tall, NX * tall), -1, jnp.int32)
        for j in range(NX):
            for i in range(rows):
                hit = (fro // tall == j) & ((fro & (rows - 1)) == i)
                slot = jnp.where(hit, slots[(j * NZ + z) * rows + i], slot)
        pick = (slot == target) & ((to & rows) == (fro & rows))
        pick = jnp.where(pick, 1.0, 0.0).astype(BF16)
        moved = dot(pick, xrows[...].reshape(NX * tall, wide), 1, 0).astype(BF16)
        zsend[...] = moved.reshape(NZ, tall, wide)
        for d in range(1, NZ):
            z_rows(d).start()

    pairs = heads // 2
    cuts = (0, 3, 6, 7, 8)

    @pl.loop(0, pairs)
    def _(pair):
        here = pl.ds(pl.multiple_of(pair * 2 * toks, 2 * toks), 2 * toks)
        num, den = join(here, jnp.max(top[here, :], axis=1, keepdims=True))
        lat = (num * (1.0 / den)).astype(BF16)
        for sub in range(2):
            cols = pl.ds(pl.multiple_of((pair * 2 + sub) * DV, DV), DV)
            part = dot(lat[sub * toks : (sub + 1) * toks], vup[:, cols], 1, 0)
            staged[:, cols] = part.astype(BF16)
        pl.when(pair == 3)(sort_rows)
        for begin, end in zip(cuts[:-1], cuts[1:]):

            @pl.when(pair == end - 1)
            def _(begin=begin, end=end):
                for d in (4, 2, 6, 3, 5, 1, 7):
                    deliver(begin * 2 * DV, (end - begin) * 2 * DV, d).start()

    ours = pl.ds(pl.multiple_of(member * width, width), width)
    out_ref[:, ours] = staged[pl.ds(pl.multiple_of(member * share, share), share), :]
    all_z.wait_recv()
    total = zsend[z].astype(F32)
    for d in range(1, NZ):
        total = total + zrecv[d - 1].astype(F32)
    dec_ref[...] = jnp.concatenate([total[:rows], total[rows:]], axis=1).astype(BF16)
    sent = 2 * NX * NZ * SPAN - SPAN

    whole(keys.at[pl.ds(0, sent), :], keys.at[pl.ds(0, sent), :], send.at[0], recv.at[0]).wait_send()
    all_x.wait_send()
    all_z.wait_send()
    all_out.wait_send()
    all_out.wait_recv()


def hand_on(a, b, to_a, to_b, sems):
    copies = [pltpu.make_async_copy(a, to_a, sems.at[0]), pltpu.make_async_copy(b, to_b, sems.at[1])]
    for one in copies:
        one.start()
    for one in copies:
        one.wait()


def per_device(
    prefill_query, prompt_cache, key_up, value_up, block_place, decode_query, decode_cache,
    row_length, row_slot,
):
    toks, width = prefill_query.shape
    heads = width // HD
    rows = decode_query.shape[0]
    count = NX * NZ * toks
    smem = pl.BlockSpec(memory_space=pltpu.SMEM)
    vmem = pl.BlockSpec(memory_space=pltpu.VMEM)
    hbm = pl.BlockSpec(memory_space=pl.ANY)
    total = heads * (toks + rows)
    wide = heads // 2 * DV
    moved = pl.pallas_call(
        kernel,
        out_shape=(
            jax.ShapeDtypeStruct((toks // 8, 8 * heads * DV), BF16),
            jax.ShapeDtypeStruct((rows, heads * DV), BF16),
        ),
        in_specs=[smem, smem, smem, vmem, vmem, vmem, hbm, hbm, hbm],
        out_specs=(vmem, vmem),
        scratch_shapes=[
            pltpu.VMEM((toks, width), BF16),
            pltpu.VMEM((count, WIDE), BF16),
            pltpu.VMEM(key_up.shape, BF16),
            pltpu.VMEM(value_up.shape, BF16),
            pltpu.VMEM((total, WIDE), BF16),
            pltpu.VMEM((total, 5 * 2 * LINE), F32),
            pltpu.VMEM((total, 128), F32),
            pltpu.VMEM((total, DL), F32),
            pltpu.VMEM((total, 128), F32),
            pltpu.VMEM((total, 128), F32),
            pltpu.VMEM((toks + heads * rows, 2 * LINE), F32),
            pltpu.VMEM((toks, heads * DV), BF16),
            pltpu.VMEM((NX, 2 * rows, wide), BF16),
            pltpu.VMEM((NZ, 2 * rows, wide), BF16),
            pltpu.VMEM((NZ - 1, 2 * rows, wide), BF16),
            pltpu.SemaphoreType.DMA((3,)),
            pltpu.SemaphoreType.DMA((1,)),
            pltpu.SemaphoreType.DMA((41,)),
            pltpu.SemaphoreType.DMA((1,)),
            pltpu.SemaphoreType.DMA((1,)),
            pltpu.SemaphoreType.DMA((2,)),
            pltpu.SemaphoreType.DMA((2,)),
        ],
        compiler_params=pltpu.CompilerParams(
            vmem_limit_bytes=60 << 20, collective_id=0, has_side_effects=True
        ),
    )(
        block_place, row_length, row_slot, prompt_cache.T, decode_query, decode_cache,
        prefill_query, key_up, value_up,
    )
    return pl.pallas_call(
        hand_on,
        out_shape=tuple(jax.ShapeDtypeStruct(one.shape, one.dtype) for one in moved),
        in_specs=[vmem, vmem],
        out_specs=(hbm, hbm),
        scratch_shapes=[pltpu.SemaphoreType.DMA((2,))],
    )(*moved)


def solution(mesh):
    return jax.shard_map(
        per_device,
        mesh=mesh,
        in_specs=(
            P("ctx", ("tp", "grp")),
            P("ctx", None),
            P(None, ("tp", "grp")),
            P(None, ("tp", "grp")),
            P(),
            P("ctx", ("tp", "grp")),
            P("ctx", None),
            P(),
            P(),
        ),
        out_specs=(P(("ctx", "tp", "grp"), None), P("ctx", ("tp", "grp"))),
        check_vma=False,
    )
```

```python
import functools
import math

import jax
import jax.numpy as jnp
from jax import lax
from jax.experimental import pallas as pl
from jax.experimental.pallas import tpu as pltpu
from jax.sharding import PartitionSpec as P

DL = 512
DR = 64
DN = 128
DV = 128
HD = DN + DR
WIDE = DL + 2 * DR
SPAN = 64
FACTOR = HD**-0.5 * math.log2(math.e)
MASKED = -1e30
NX, NZ = 4, 8
LINE = NX * SPAN
MESH = pl.DeviceIdType.MESH
F32 = jnp.float32
BF16 = jnp.bfloat16


def dot(a, b, ca, cb):
    return lax.dot_general(a, b, (((ca,), (cb,)), ((), ())), preferred_element_type=F32)


def kernel(
    place, length, slots, cache_ref, dq_ref, dc_ref, q_hbm, kup_hbm, vup_hbm, out_ref, dec_ref,
    q_ref, keys, kup, vup, queries, score, top, acc, part_den, base, bias,
    staged, xrows, zsend, zrecv,
    load_sem, send, recv, out_send, out_recv, dec_send, dec_recv,
):
    toks = q_ref.shape[0]
    rows = dq_ref.shape[0]
    heads = q_ref.shape[1] // HD
    count = keys.shape[0]
    pre = heads * toks
    dec = heads * rows
    ctx = lax.axis_index("ctx")
    tp = lax.axis_index("tp")
    grp = lax.axis_index("grp")
    x, z = ctx // NZ, lax.rem(ctx, NZ)
    core = lax.rem(tp, 2)
    member = tp * 2 + grp
    y = tp // 2 * 2 + grp

    def at_x(d):
        return lax.rem(x + d + NX, NX)

    def at_z(d):
        return lax.rem(z + d + NZ, NZ)

    def x_peer(d):
        return (at_x(d) * NZ + z, tp, grp)

    def z_peer(d):
        return (x * NZ + at_z(d), tp, grp)

    def group_peer(d):
        other = lax.rem(member + d, 8)
        return (ctx, other // 2, lax.rem(other, 2))

    def y_peer(d):
        other = lax.rem(y + d, 4)
        return (ctx, other // 2 * 2 + core, lax.rem(other, 2))

    sibling = (ctx, tp + 1 - 2 * core, grp)

    loads = [
        pltpu.make_async_copy(src, dst, load_sem.at[i])
        for i, (src, dst) in enumerate([(q_hbm, q_ref), (kup_hbm, kup), (vup_hbm, vup)])
    ]
    for load in loads:
        load.start()

    barrier = pltpu.get_barrier_semaphore()
    peers = [x_peer(d) for d in range(1, NX)] + [z_peer(d) for d in range(1, NZ)]
    peers += [group_peer(d) for d in range(1, 8)]
    for peer in peers:
        pl.semaphore_signal(barrier, inc=1, device_id=peer, device_id_type=MESH)

    def place_of(half, xx, zz):
        return (zz * 2 + half) * LINE + xx * SPAN

    turned = cache_ref[...].astype(F32).T
    mine = jnp.where(core == 0, turned[:SPAN], turned[SPAN:]).astype(BF16)

    here = pl.ds(pl.multiple_of(place_of(core, x, z), SPAN), SPAN)
    keys[here, : DL + DR] = mine
    keys[here, DL + DR :] = mine[:, DL:]
    pl.semaphore_wait(barrier, len(peers))

    def copy(first, size, sem, peer):
        part = keys.at[pl.ds(pl.multiple_of(first, SPAN), size), :]
        return pltpu.make_async_remote_copy(
            src_ref=part, dst_ref=part, send_sem=send.at[0], recv_sem=recv.at[sem],
            device_id=peer, device_id_type=MESH,
        )

    def landed(sem, size):
        copy(0, size, sem, sibling).wait_recv()

    def start(copies):
        for one in copies:
            one.start()

    def on(which):
        return pl.when(core == which)

    EVEN_Z, ODD_Z, TWIN, EVEN_X, ODD_Y, ODD_X = 0, 8, 16, 24, 32, 40
    far = NZ // 2

    def signs(k):
        return (k,) if k in (0, far) else (k, -k)

    def even_z(k):
        first = place_of(0, x, z)
        start([copy(first, SPAN, EVEN_Z + (-d) % NZ, z_peer(d)) for d in signs(k)])

    def odd_z(k):
        first = place_of(1, y, z)
        start([copy(first, SPAN, ODD_Z + (-d) % NZ, z_peer(d)) for d in signs(k)])

    def even_step(k):
        for dz in signs(k):
            if k:
                landed(EVEN_Z + dz % NZ, SPAN)
            first = place_of(0, x, at_z(dz))
            start([copy(first, SPAN, EVEN_X + dz % NZ, x_peer(d)) for d in (1, 3, 2)])

    def odd_step(k):
        for dz in signs(k):
            landed(ODD_Z + dz % NZ, SPAN)
            first = place_of(1, y, at_z(dz))
            start([copy(first, SPAN, ODD_Y + dz % NZ, y_peer(d)) for d in (1, 3, 2)])

    def twin(dz):
        return copy(place_of(core, 0, at_z(dz)), LINE, TWIN + dz % NZ, sibling)

    def even_line(dz):
        landed(EVEN_X + dz % NZ, 3 * SPAN)
        twin(dz).start()

    def odd_line(dz):
        landed(ODD_Y + dz % NZ if dz else ODD_X, 3 * SPAN)
        twin(dz).start()

    def twin_landed(dz):
        landed(TWIN + dz % NZ, LINE)

    @on(0)
    def _():
        even_z(1)
        even_step(0)

    @on(1)
    def _():
        start([copy(place_of(1, x, z), SPAN, ODD_X, x_peer(d)) for d in (1, 3, 2)])

    @pl.when((core == 1) & (x == y))
    def _():
        odd_z(1)

    loads[0].wait()
    loads[1].wait()

    def absorb(pair):
        at = pl.ds(pl.multiple_of(pair * 2 * HD, 2 * HD), 2 * HD)
        both = q_ref[:, at].astype(F32)
        dboth = dq_ref[:, at].astype(F32)
        kept = []
        for sub in range(2):
            h = pair * 2 + sub
            every = jnp.concatenate([both, dboth, dboth], axis=0)[:, sub * HD : (sub + 1) * HD]
            block = kup[:, pl.ds(pl.multiple_of(h * DN, DN), DN)]
            absorbed = (dot(every[:, :DN].astype(BF16), block, 1, 1) * FACTOR).astype(BF16)
            rope = every[:, DN:] * FACTOR
            high = rope.astype(BF16).astype(F32)
            rope = jnp.concatenate([high, rope - high], axis=1).astype(BF16)
            here = pl.ds(pl.multiple_of(h * toks, toks), toks)
            queries[here, :DL] = absorbed[:toks]
            queries[here, DL:] = rope[:toks]
            kept.append((absorbed[toks:].astype(F32)[:rows], rope[toks:].astype(F32)[:rows]))
        here = pl.ds(pl.multiple_of(pre + pair * 2 * rows, 2 * rows), 2 * rows)
        queries[here, :DL] = jnp.concatenate([kept[0][0], kept[1][0]], axis=0).astype(BF16)
        queries[here, DL:] = jnp.concatenate([kept[0][1], kept[1][1]], axis=0).astype(BF16)

    lane = lax.broadcasted_iota(jnp.int32, (1, 128), 1)
    tok = lax.broadcasted_iota(jnp.int32, (toks, 1), 0)
    my_pos = jnp.where(tok < SPAN, place[2 * ctx], place[2 * ctx + 1]) * SPAN + (tok & (SPAN - 1))
    row = lax.broadcasted_iota(jnp.int32, (rows, 1), 0)
    limit = jnp.zeros((rows, 1), jnp.int32)
    for r in range(rows):
        limit = jnp.where(row == r, length[ctx * rows + r], limit)

    def scores(first, size, blocks, column):
        for j in range(size // 128):
            a, b = place[blocks[2 * j]], place[blocks[2 * j + 1]]
            pos = jnp.where(lane < SPAN, a, b) * SPAN + (lane & (SPAN - 1))
            cols = slice(j * 128, (j + 1) * 128)
            bias[:toks, cols] = jnp.where(pos <= my_pos, 0.0, MASKED)
            part = jnp.where(pos < limit, 0.0, MASKED)
            bias[toks:, cols] = jnp.concatenate([part] * (dec // rows), axis=0)
        from_keys = pl.ds(pl.multiple_of(first, 256), size)
        cols = pl.ds(pl.multiple_of(column, 256), size)
        half = pre // 2
        for begin, tall, extra in ((0, half, 0), (half, half, dec)):
            here = pl.ds(begin, tall + extra)
            add = [bias[:toks, :size]] * (tall // toks)
            if extra:
                add = add + [bias[toks:, :size]]
            s = dot(queries[here, :], keys[from_keys, :], 1, 1) + jnp.concatenate(add, axis=0)
            score[here, cols] = s
            best = top[here, :]
            for j in range(size // 128):
                best = jnp.maximum(best, s[:, j * 128 : (j + 1) * 128])
            top[here, :] = best

    def unit(dz, half, line):
        zz = at_z(dz)
        blocks = [2 * (j * NZ + zz) + half for j in range(NX)]
        scores(place_of(half, 0, zz), LINE, blocks, (line * 2 + half) * LINE)

    def full_line(dz, line):
        zz = at_z(dz)
        blocks = [2 * (j * NZ + zz) + half for half in (0, 1) for j in range(NX)]
        scores(place_of(0, 0, zz), 2 * LINE, blocks, line * 2 * LINE)

    def weigh(here, best, lines):
        den = jnp.zeros((best.shape[0], 128), F32)
        num = None
        for i, dz in enumerate(lines):
            e = jnp.exp2(score[here, i * 2 * LINE : (i + 1) * 2 * LINE] - best)
            for j in range(2 * LINE // 128):
                den = den + e[:, j * 128 : (j + 1) * 128]
            values = keys[pl.ds(pl.multiple_of(place_of(0, 0, at_z(dz)), 2 * LINE), 2 * LINE), :DL]
            part = dot(e.astype(BF16), values, 1, 0)
            num = part if num is None else num + part
        return num, den

    near, rest = (0, 1, -1), (3, -3, 4, 2, -2)

    def early(here, size):
        best = jnp.max(top[here, :], axis=1, keepdims=True)
        acc[here, :], part_den[here, :] = weigh(here, best, near)
        base[here, :] = jnp.broadcast_to(best, (size, 128))

    def join(here, best):
        num, den = weigh(here, best, rest)
        factor = jnp.exp2(base[here, :] - best)
        den = jnp.sum(den + part_den[here, :] * factor, axis=1, keepdims=True)
        return num + acc[here, :] * jnp.concatenate([factor] * (DL // 128), axis=1), den

    pl.loop(0, 2)(absorb)

    @on(0)
    def _():
        even_z(2)

    pl.loop(2, 4)(absorb)

    @on(0)
    def _():
        even_z(3)

    pl.loop(4, 6)(absorb)

    @on(0)
    def _():
        even_step(1)
        even_z(4)

    @on(1)
    def _():
        odd_line(0)

    @pl.when((core == 1) & (x != y))
    def _():
        odd_z(1)

    @on(1)
    def _():
        odd_z(2)

    pl.loop(6, heads // 2)(absorb)
    top[...] = jnp.full_like(top, MASKED)

    @on(0)
    def _():
        even_line(0)

    @on(1)
    def _():
        odd_z(3)

    @pl.loop(0, 2)
    def _(i):
        @pl.when((i == 1) & (core == 0))
        def _():
            even_step(2)

        @pl.when((i == 1) & (core == 1))
        def _():
            odd_z(4)

        @pl.when(i == 1)
        def _():
            twin_landed(0)

        unit(0, jnp.where(i == 0, core, 1 - core), 0)

    @on(0)
    def _():
        even_step(3)
        even_line(1)
        even_step(4)

    @on(1)
    def _():
        odd_step(1)
        odd_step(2)
        twin_landed(1)

    @pl.loop(0, 6)
    def _(i):
        def at(turn, which):
            return pl.when((i == turn) & (core == which))

        @at(1, 0)
        def _():
            even_line(-1)

        @at(1, 1)
        def _():
            twin_landed(-1)

        @at(2, 0)
        def _():
            even_line(2)

        @at(2, 1)
        def _():
            odd_line(1)
            odd_step(3)

        @at(3, 0)
        def _():
            even_line(-2)

        @at(3, 1)
        def _():
            odd_line(-1)
            odd_step(4)

        @at(4, 0)
        def _():
            twin_landed(1)

        @at(4, 1)
        def _():
            twin_landed(2)

        @at(5, 0)
        def _():
            twin_landed(-1)

        @at(5, 1)
        def _():
            twin_landed(-2)

        flip = lax.rem(i, 2)
        second = i // 2 == 2 - (1 - core)
        half = jnp.where((i < 2) | second, 0, 1)
        dz = jnp.where(second, 2, 1)
        unit(jnp.where(flip == 0, dz, -dz), half, jnp.where(second, 3, 1) + flip)

    @pl.loop(0, 4)
    def _(q):
        @pl.when((q == 1) & (core == 0))
        def _():
            even_line(3)
            even_line(-3)

        @pl.when((q == 1) & (core == 1))
        def _():
            odd_line(2)
            odd_line(-2)

        @pl.when((q == 3) & (core == 0))
        def _():
            even_line(far)

        @pl.when((q == 3) & (core == 1))
        def _():
            odd_line(3)
            odd_line(-3)

        early(pl.ds(pl.multiple_of(q * (pre // 4), 128), pre // 4), pre // 4)

    early(pl.ds(pre, dec), dec)

    @on(1)
    def _():
        odd_line(far)

    @on(0)
    def _():
        twin_landed(2)
        twin_landed(-2)

    @pl.loop(0, 2)
    def _(i):
        unit(2 - 4 * i, 1, 3 + i)

    twin_landed(3)
    twin_landed(-3)

    @pl.loop(0, 3)
    def _(i):
        @pl.when(i == 2)
        def _():
            twin_landed(far)

        full_line(jnp.where(i == 2, NZ // 2, 3 - 6 * i), i)

    loads[2].wait()

    here = pl.ds(pre, dec)
    cache = dc_ref[...].astype(F32)
    own = jnp.concatenate([cache, cache[:, DL:]], axis=1)
    own = jnp.concatenate([own] * heads, axis=0)
    own_score = jnp.sum(queries[here, :].astype(F32) * own, axis=1, keepdims=True)
    best = jnp.maximum(jnp.max(top[here, :], axis=1, keepdims=True), own_score)
    num, den = join(here, best)
    own_weight = jnp.exp2(own_score - best)
    lat = (num + own_weight * own[:, :DL]) / (den + own_weight)
    high = lat.astype(BF16).astype(F32)
    low = lat - high
    outs = []
    for h in range(heads):
        part = slice(h * rows, (h + 1) * rows)
        pieces = jnp.concatenate([high[part], low[part]], axis=0).astype(BF16)
        doubled = dot(pieces, vup[:, h * DV : (h + 1) * DV], 1, 0)
        outs.append(doubled[:rows] + doubled[rows:])
    wide = heads // 2 * DV
    halves = [jnp.concatenate(outs[: heads // 2], axis=1), jnp.concatenate(outs[heads // 2 :], axis=1)]
    xrows[x] = jnp.concatenate(halves, axis=0).astype(BF16)

    def x_rows(d):
        return pltpu.make_async_remote_copy(
            src_ref=xrows.at[x], dst_ref=xrows.at[x], send_sem=dec_send.at[0],
            recv_sem=dec_recv.at[0], device_id=x_peer(d), device_id_type=MESH,
        )

    def z_rows(d):
        return pltpu.make_async_remote_copy(
            src_ref=zsend.at[at_z(d)], dst_ref=zrecv.at[d - 1], send_sem=dec_send.at[1],
            recv_sem=dec_recv.at[1], device_id=z_peer(d), device_id_type=MESH,
        )

    def whole(src, dst, send_sem, recv_sem):
        return pltpu.make_async_remote_copy(
            src_ref=src, dst_ref=dst, send_sem=send_sem, recv_sem=recv_sem,
            device_id=sibling, device_id_type=MESH,
        )

    all_x = whole(xrows.at[pl.ds(0, NX - 1)], xrows.at[pl.ds(0, NX - 1)], dec_send.at[0], dec_recv.at[0])
    all_z = whole(zsend.at[pl.ds(0, NZ - 1)], zrecv, dec_send.at[1], dec_recv.at[1])

    for d in range(1, NX):
        x_rows(d).start()

    share = out_ref.shape[0]
    width = heads * DV

    def deliver(first, size, d):
        other = lax.rem(member + d, 8)
        return pltpu.make_async_remote_copy(
            src_ref=staged.at[pl.ds(pl.multiple_of(other * share, share), share), pl.ds(first, size)],
            dst_ref=out_ref.at[:, pl.ds(pl.multiple_of(member * width + first, 128), size)],
            send_sem=out_send.at[0], recv_sem=out_recv.at[0],
            device_id=group_peer(d), device_id_type=MESH,
        )

    all_out = whole(
        staged.at[pl.ds(0, 7 * share), :], out_ref.at[:, pl.ds(0, 7 * width)],
        out_send.at[0], out_recv.at[0],
    )

    def sort_rows():
        all_x.wait_recv()
        tall = 2 * rows
        to = lax.broadcasted_iota(jnp.int32, (NZ * tall, NX * tall), 0)
        fro = lax.broadcasted_iota(jnp.int32, (NZ * tall, NX * tall), 1)
        target = (x * NZ + to // tall) * rows + (to & (rows - 1))
        slot = jnp.full((NZ * tall, NX * tall), -1, jnp.int32)
        for j in range(NX):
            for i in range(rows):
                hit = (fro // tall == j) & ((fro & (rows - 1)) == i)
                slot = jnp.where(hit, slots[(j * NZ + z) * rows + i], slot)
        pick = (slot == target) & ((to & rows) == (fro & rows))
        pick = jnp.where(pick, 1.0, 0.0).astype(BF16)
        moved = dot(pick, xrows[...].reshape(NX * tall, wide), 1, 0).astype(BF16)
        zsend[...] = moved.reshape(NZ, tall, wide)
        for d in range(1, NZ):
            z_rows(d).start()

    pairs = heads // 2
    cuts = (0, 3, 6, 7, 8)

    @pl.loop(0, pairs)
    def _(pair):
        here = pl.ds(pl.multiple_of(pair * 2 * toks, 2 * toks), 2 * toks)
        num, den = join(here, jnp.max(top[here, :], axis=1, keepdims=True))
        lat = (num * (1.0 / den)).astype(BF16)
        for sub in range(2):
            cols = pl.ds(pl.multiple_of((pair * 2 + sub) * DV, DV), DV)
            part = dot(lat[sub * toks : (sub + 1) * toks], vup[:, cols], 1, 0)
            staged[:, cols] = part.astype(BF16)
        pl.when(pair == 3)(sort_rows)
        for begin, end in zip(cuts[:-1], cuts[1:]):

            @pl.when(pair == end - 1)
            def _(begin=begin, end=end):
                for d in (4, 2, 6, 3, 5, 1, 7):
                    deliver(begin * 2 * DV, (end - begin) * 2 * DV, d).start()

    ours = pl.ds(pl.multiple_of(member * width, width), width)
    out_ref[:, ours] = staged[pl.ds(pl.multiple_of(member * share, share), share), :]
    all_z.wait_recv()
    total = zsend[z].astype(F32)
    for d in range(1, NZ):
        total = total + zrecv[d - 1].astype(F32)
    dec_ref[...] = jnp.concatenate([total[:rows], total[rows:]], axis=1).astype(BF16)
    sent = 2 * NX * NZ * SPAN - SPAN

    whole(keys.at[pl.ds(0, sent), :], keys.at[pl.ds(0, sent), :], send.at[0], recv.at[0]).wait_send()
    all_x.wait_send()
    all_z.wait_send()
    all_out.wait_send()
    all_out.wait_recv()


def hand_on(a, b, to_a, to_b, sems):
    copies = [pltpu.make_async_copy(a, to_a, sems.at[0]), pltpu.make_async_copy(b, to_b, sems.at[1])]
    for one in copies:
        one.start()
    for one in copies:
        one.wait()


def per_device(
    prefill_query, prompt_cache, key_up, value_up, block_place, decode_query, decode_cache,
    row_length, row_slot,
):
    toks, width = prefill_query.shape
    heads = width // HD
    rows = decode_query.shape[0]
    count = NX * NZ * toks
    smem = pl.BlockSpec(memory_space=pltpu.SMEM)
    vmem = pl.BlockSpec(memory_space=pltpu.VMEM)
    hbm = pl.BlockSpec(memory_space=pl.ANY)
    total = heads * (toks + rows)
    wide = heads // 2 * DV
    moved = pl.pallas_call(
        kernel,
        out_shape=(
            jax.ShapeDtypeStruct((toks // 8, 8 * heads * DV), BF16),
            jax.ShapeDtypeStruct((rows, heads * DV), BF16),
        ),
        in_specs=[smem, smem, smem, vmem, vmem, vmem, hbm, hbm, hbm],
        out_specs=(vmem, vmem),
        scratch_shapes=[
            pltpu.VMEM((toks, width), BF16),
            pltpu.VMEM((count, WIDE), BF16),
            pltpu.VMEM(key_up.shape, BF16),
            pltpu.VMEM(value_up.shape, BF16),
            pltpu.VMEM((total, WIDE), BF16),
            pltpu.VMEM((total, 5 * 2 * LINE), F32),
            pltpu.VMEM((total, 128), F32),
            pltpu.VMEM((total, DL), F32),
            pltpu.VMEM((total, 128), F32),
            pltpu.VMEM((total, 128), F32),
            pltpu.VMEM((toks + heads * rows, 2 * LINE), F32),
            pltpu.VMEM((toks, heads * DV), BF16),
            pltpu.VMEM((NX, 2 * rows, wide), BF16),
            pltpu.VMEM((NZ, 2 * rows, wide), BF16),
            pltpu.VMEM((NZ - 1, 2 * rows, wide), BF16),
            pltpu.SemaphoreType.DMA((3,)),
            pltpu.SemaphoreType.DMA((1,)),
            pltpu.SemaphoreType.DMA((41,)),
            pltpu.SemaphoreType.DMA((1,)),
            pltpu.SemaphoreType.DMA((1,)),
            pltpu.SemaphoreType.DMA((2,)),
            pltpu.SemaphoreType.DMA((2,)),
        ],
        compiler_params=pltpu.CompilerParams(
            vmem_limit_bytes=60 << 20, collective_id=0, has_side_effects=True
        ),
    )(
        block_place, row_length, row_slot, prompt_cache.T, decode_query, decode_cache,
        prefill_query, key_up, value_up,
    )
    return pl.pallas_call(
        hand_on,
        out_shape=tuple(jax.ShapeDtypeStruct(one.shape, one.dtype) for one in moved),
        in_specs=[vmem, vmem],
        out_specs=(hbm, hbm),
        scratch_shapes=[pltpu.SemaphoreType.DMA((2,))],
    )(*moved)


def solution(mesh):
    return jax.shard_map(
        per_device,
        mesh=mesh,
        in_specs=(
            P("ctx", ("tp", "grp")),
            P("ctx", None),
            P(None, ("tp", "grp")),
            P(None, ("tp", "grp")),
            P(),
            P("ctx", ("tp", "grp")),
            P("ctx", None),
            P(),
            P(),
        ),
        out_specs=(P(("ctx", "tp", "grp"), None), P("ctx", ("tp", "grp"))),
        check_vma=False,
    )
```
